32 devices in a mesh: grp: 2 (over y), ep: 4 (over z), tp: 4 (over x, core).
Axes of the slice: x: 2, y: 2, z: 4, core: 2. Of those that a mesh axis runs over, the one named last changes fastest.
Arguments:
- tokens: bfloat16 [1536, 5120], P(('grp', 'ep'), 'tp'), parts along dimension 0, may hold values from -6 to 6
- expert_ids: int32 [1536, 6], P(('grp', 'ep')), parts along dimension 0, may hold values from 0 to 31, all different within a row; in each aligned block of 192 rows (0 to 191, 192 to 383, ...) at most 48 rows name the same one
- gate_weights: bfloat16 [1536, 6], P(('grp', 'ep')), parts along dimension 0, may hold values from 0.049804688 to 1
- gu_weight: bfloat16 [32, 1024, 2, 5120], P('ep', None, None, 'tp'), may hold values from -0.078125 to 0.078125
- down_weight: bfloat16 [32, 1024, 5120], P('ep', None, 'tp'), may hold values from -0.1875 to 0.1875
Outputs:
- mixed: bfloat16 [1536, 5120], P(('grp', 'ep'), 'tp'), parts along dimension 0
The draws below stay inside these ranges and needn't reach their ends.
There are 2 independent parts, one for each index of `grp`. The reference program is written for one: setup_inputs(seed, part) draws one part's arguments, and reference() takes and returns one part's arrays. A program takes and returns all parts, laid end to end along the dimension named above; an argument that names none is the same for every part. Nothing has to cross between parts.
Inputs may be any that keep to these rules, and one draw needn't show every extreme that they name: `expert_ids`: each token names 6 different experts. Among the 192 tokens of one block no expert is named more than 48 times, and in every draw some expert is named exactly 48 times in some block.
All inputs are finite; a program needn't handle non-finite values.
Results may differ from the reference program's by a relative error of at most 0.019.
Values may be sent and summed in bfloat16 or wider, within the bound.
No kernel may reach another device: no remote copies, remote signals or barrier semaphores. Data moves between devices by JAX's collectives and lax.ppermute only.
A program may use at most 192 MiB of HBM per device.

```python
import math
import jax
import jax.numpy as jnp
import numpy as np
from jax import lax

D = 5120
FF = 1024
EXPERTS = 32
TOPK = 6
TOK_DEV = 192
CAP = 48
TOKENS = 768
N_TP = 4


def steps_of(key, extent, pieces, low, largest):
    factor_of = 1.0
    for dim, blocks in pieces:
        steps = jax.random.uniform(jax.random.fold_in(jax.random.fold_in(key, 6), dim), (blocks,), jnp.float32, low / len(pieces), largest / len(pieces))
        factor_of = factor_of * jnp.repeat(jnp.exp(steps), extent[dim] // blocks).reshape((-1,) + (1,) * (len(extent) - 1 - dim))
    return factor_of


def shared_out(own_key, own, number, rows, count, top, reach, lean):
    ranking = jax.random.permutation(own_key, count)
    packed, ordinary = shares(count, rows * top, reach, lean, True), shares(count, rows * top, reach, lean, False)
    places = jnp.arange(count)

    def named(lengths, turn):
        used = int((lengths > 0).sum())
        fixed = max(1, used // 4)
        shifted = fixed + (places - fixed + turn * (used - fixed)) % max(1, count - fixed)
        return jnp.zeros((count,), jnp.int32).at[ranking[jnp.where(places < fixed, places, shifted)]].set(jnp.asarray(lengths, jnp.int32))

    lengths = jnp.where(number % 4 == 0, named(packed, number // 4), named(ordinary, number - number // 4 - 1))
    mixed = jax.random.permutation(jax.random.fold_in(own, 3), count)
    source_of, taker = mixed[0:count // 2 * 2:2], mixed[1:count // 2 * 2:2]
    room = jnp.minimum(lengths[source_of] - 1, reach - lengths[taker]) // 2
    room = jnp.where((source_of == ranking[0]) | (taker == ranking[0]) | (lengths[taker] == 0), 0, jnp.maximum(room, 0))
    shifted = jax.random.randint(jax.random.fold_in(own, 4), (count // 2,), 0, 1 << 20) % (room + 1)
    lengths = lengths.at[source_of].add(-shifted).at[taker].add(shifted)
    items = jnp.searchsorted(jnp.cumsum(lengths), jnp.arange(rows * top), side="right").astype(jnp.int32)
    table = items.reshape(top, rows).T
    table = table[jax.random.permutation(jax.random.fold_in(own, 1), rows)]
    turn = jax.random.randint(jax.random.fold_in(own, 2), (rows, 1), 0, top)
    return jnp.take_along_axis(table, (jnp.arange(top)[None, :] + turn) % top, axis=1)


def shares(count, total, most, skew, full):
    loads = [(1 << 20) // math.isqrt(grade ** skew) + 1 for grade in range(1, count + 1)]
    largest = most if full else min(most, max(-(-total // count), total * loads[0] // sum(loads)))
    least = 1 if total - largest >= count - 1 else 0
    counts, surplus = [largest] + [least] * (count - 1), total - largest - least * (count - 1)
    while surplus > 0:
        candidates = [i for i in range(1, count) if counts[i] < largest] or [i for i in range(1, count) if counts[i] < most]
        pool, left = sum([loads[i] for i in candidates]), surplus
        for i in candidates:
            addition = min(most - counts[i], max(1, left * loads[i] // pool), surplus)
            counts[i] = counts[i] + addition
            surplus = surplus - addition
    return np.array(counts)


def scatter_about(key, extent, spread, reach, cuts=(), kind=jnp.bfloat16):
    array = jax.random.normal(key, extent, jnp.float32) * spread
    if len(cuts) > 0:
        array = steps_of(key, extent, cuts, -0.22, 0.18) * array
    return jnp.clip(array, min=-reach, max=reach).astype(kind)


def setup_inputs(seed: int = 0, part: int = 0) -> dict:
    seeds = jax.random.split(jax.random.key(seed), 6)
    part_splits = jax.random.split(jax.random.fold_in(seeds[5], part), 6)
    tokens = scatter_about(part_splits[0], (TOKENS, D), 1.0, 6.0, ((0, 4), (1, 4)))
    expert_ids_keys = jax.random.split(jax.random.fold_in(part_splits[1], 1), TOKENS // TOK_DEV)
    expert_ids_turns = jax.random.permutation(jax.random.fold_in(part_splits[1], 3), TOKENS // TOK_DEV)
    expert_ids = jax.vmap(lambda own, number: shared_out(jax.random.fold_in(part_splits[1], 2), own, number, TOK_DEV, EXPERTS, TOPK, CAP, 2))(expert_ids_keys, expert_ids_turns).reshape((TOKENS, TOPK))
    gate_weights = jnp.clip(jnp.exp(math.log(1.0) - 2.9996462 * jax.random.uniform(part_splits[2], (TOKENS, TOPK), jnp.float32) ** steps_of(part_splits[2], (TOKENS, TOPK), ((0, 4),), -0.2, 0.2)), 0.049804688, 1.0).astype(jnp.bfloat16)
    gu_weight = scatter_about(seeds[3], (EXPERTS, FF, 2, D), D ** -0.5, 0.078125, ((0, 4), (3, 4)))
    down_weight = scatter_about(seeds[4], (EXPERTS, FF, D), FF ** -0.5, 0.1875, ((0, 4), (2, 4)))
    return dict(tokens=tokens, expert_ids=expert_ids, gate_weights=gate_weights, gu_weight=gu_weight, down_weight=down_weight)


def reference(tokens, expert_ids, gate_weights, gu_weight, down_weight):
    n_source = TOKENS // TOK_DEV
    pair_ids = expert_ids.reshape(n_source, TOK_DEV * TOPK)
    onehot = (pair_ids[:, :, None] == jnp.arange(EXPERTS, dtype=jnp.int32)[None, None, :]).astype(jnp.int32)
    earlier = jnp.cumsum(onehot, axis=1) - onehot
    position = jnp.sum(earlier * onehot, axis=2).astype(jnp.int32)
    source = jnp.broadcast_to(jnp.arange(n_source, dtype=jnp.int32)[:, None], position.shape)
    token_index = (jnp.arange(TOK_DEV * TOPK, dtype=jnp.int32) // TOPK)[None, :] + source * TOK_DEV
    buffers = jnp.zeros((EXPERTS, n_source, CAP, D), jnp.bfloat16)
    buffers = buffers.at[pair_ids, source, position].set(tokens[token_index])
    buffers = buffers.reshape(EXPERTS, n_source * CAP, D)

    def one_expert(operands):
        rows, gate_up_w, down_w = operands
        rows_blocks = rows.reshape(n_source * CAP, N_TP, D // N_TP).astype(jnp.float32)
        weight_blocks = gate_up_w.reshape(FF, 2, N_TP, D // N_TP).astype(jnp.float32)
        partial_sums = jnp.einsum("sbd,fgbd->bfgs", rows_blocks, weight_blocks)
        partial_sums = lax.optimization_barrier(partial_sums.astype(jnp.bfloat16)).astype(jnp.float32)
        gate_up = jnp.sum(partial_sums, axis=0)
        hidden = (jax.nn.silu(gate_up[:, 0]) * gate_up[:, 1]).astype(jnp.bfloat16)
        return jnp.dot(hidden.T, down_w, preferred_element_type=jnp.float32).astype(jnp.bfloat16)

    expert_out = lax.map(one_expert, (buffers, gu_weight, down_weight))
    expert_out = expert_out.reshape(EXPERTS, n_source, CAP, D)
    picked = expert_out[pair_ids, source, position].astype(jnp.float32)
    weights = gate_weights.reshape(n_source, TOK_DEV * TOPK).astype(jnp.float32)
    weighted = (picked * weights[:, :, None]).reshape(n_source, TOK_DEV, TOPK, D)
    mixed = jnp.sum(weighted, axis=2).reshape(TOKENS, D)
    return mixed.astype(jnp.bfloat16)
```

```python
import functools

import jax
import jax.numpy as jnp
from jax import lax
from jax.experimental import pallas as pl
from jax.experimental.pallas import tpu as pltpu
from jax.sharding import PartitionSpec as P

EXPERTS = 32
TOPK = 6
CAP = 48
LANES = 128
BF16, F32 = jnp.bfloat16, jnp.float32
NT = (((1,), (1,)), ((), ()))
TN = (((0,), (0,)), ((), ()))
NN = (((1,), (0,)), ((), ()))

PAIR = [(0, 1), (1, 0), (2, 3), (3, 2)]
MIDDLE = [(1, 2), (2, 1)]
OUTWARD = [(1, 0), (2, 3)]
INWARD = [(0, 1), (3, 2)]
ACROSS_X = [(0, 2), (1, 3), (2, 0), (3, 1)]
ACROSS_CORE = [(0, 1), (1, 0), (2, 3), (3, 2)]


def params(mib):
    return pltpu.CompilerParams(vmem_limit_bytes=mib << 20)


def route_kernel(ids_ref, gates_ref, out_ref):
    count = ids_ref.shape[1]
    expert = lax.broadcasted_iota(jnp.int32, (EXPERTS, count), 0)
    weight = jnp.zeros((EXPERTS, count), F32)
    chosen = jnp.zeros((EXPERTS, count), F32)
    for k in range(TOPK):
        hit = ids_ref[k : k + 1, :] == expert
        chosen = jnp.where(hit, 1.0, chosen)
        weight = jnp.where(hit, gates_ref[k : k + 1, :], weight)
    first = lax.broadcasted_iota(jnp.int32, (count, count), 0)
    second = lax.broadcasted_iota(jnp.int32, (count, count), 1)
    before = jnp.where(first < second, 1.0, 0.0).astype(BF16)
    position = lax.dot_general(chosen.astype(BF16), before, NN, preferred_element_type=F32)
    out_ref[:EXPERTS, :] = jnp.where(chosen > 0.0, position, -1.0)
    out_ref[EXPERTS:, :] = weight


def route(expert_ids, gate_weights):
    return pl.pallas_call(
        route_kernel,
        out_shape=jax.ShapeDtypeStruct((2 * EXPERTS, expert_ids.shape[0]), F32),
        name="route",
    )(expert_ids.T, gate_weights.T.astype(F32))


def windows(group, rows):
    found, base = [], 0
    for e in range(group):
        first = e * rows // LANES
        last = -(-(e + 1) * rows // LANES)
        found.append((first, last - first, e * rows - first * LANES, base))
        base += (last - first) * LANES
    return found, base


def gate_up_kernel(group, n_blocks, n_parts, chunk, where_ref, *refs):
    token_refs, refs = refs[: sum(n_parts)], refs[sum(n_parts) :]
    route_refs, refs = refs[:n_blocks], refs[n_blocks:]
    w_hbm, send_ref, keep_ref, rows_ref, w_buf, sems = refs
    rows = n_blocks * CAP
    found, _ = windows(group, rows)
    quarter = w_hbm.shape[1] // 4
    count = route_refs[0].shape[1]
    expert0 = where_ref[0]
    x, core = where_ref[1], where_ref[2]
    order = [(1 - x, 1 - core), (x, 1 - core), (1 - x, core), (x, core)]

    def fetch(j, e):
        f0 = pl.multiple_of((order[j][0] * 2 + order[j][1]) * quarter, quarter)
        slot = (j % 2) * group + e
        return pltpu.make_async_copy(
            w_hbm.at[chunk * group + e, pl.ds(f0, quarter)], w_buf.at[slot], sems.at[slot]
        )

    for j in range(2):
        for e in range(group):
            fetch(j, e).start()

    rows_ref[...] = jnp.zeros_like(rows_ref)
    slot_of = lax.broadcasted_iota(jnp.int32, (CAP, count), 0).astype(F32)
    part = 0
    for i in range(n_blocks):
        table = [
            jnp.where(route_refs[i][pl.ds(expert0 + e, 1), :] == slot_of, 1.0, 0.0)
            for e in range(group)
        ]
        table = jnp.concatenate(table, axis=0).astype(BF16)
        tokens = token_refs[part][...]
        for extra in range(1, n_parts[i]):
            tokens = tokens + token_refs[part + extra][...]
        part += n_parts[i]
        placed = lax.dot_general(table, tokens, NN, preferred_element_type=F32).astype(BF16)
        for e in range(group):
            _, _, offset, base = found[e]
            start = base + offset + i * CAP
            rows_ref[start : start + CAP, :] = placed[e * CAP : (e + 1) * CAP]

    for j in range(4):
        tiles = [None] * (group * rows // LANES)
        for e in range(group):
            first, width, _, base = found[e]
            fetch(j, e).wait()
            w = w_buf[(j % 2) * group + e].reshape(2 * quarter, w_buf.shape[3])
            r = rows_ref[base : base + width * LANES, :]
            part_sum = lax.dot_general(w, r, NT, preferred_element_type=F32)
            for n in range(width):
                piece = part_sum[:, n * LANES : (n + 1) * LANES]
                held = tiles[first + n]
                tiles[first + n] = piece if held is None else held + piece
            if j < 2:
                fetch(j + 2, e).start()
        target = send_ref if j < 2 else keep_ref
        for n, tile in enumerate(tiles):
            target[j % 2, :, n * LANES : (n + 1) * LANES] = tile.astype(BF16)


def gate_up(where, blocks, routes, gu_weight, chunk, group):
    n_parts = tuple(len(b) for b in blocks)
    tokens = [t for b in blocks for t in b]
    rows = len(blocks) * CAP
    _, total = windows(group, rows)
    quarter = gu_weight.shape[1] // 4
    width = gu_weight.shape[3]
    half = jax.ShapeDtypeStruct((2, 2 * quarter, group * rows), BF16)
    whole = pl.BlockSpec(memory_space=pltpu.VMEM)
    return pl.pallas_call(
        functools.partial(gate_up_kernel, group, len(blocks), n_parts, chunk),
        out_shape=(half, half),
        in_specs=[pl.BlockSpec(memory_space=pltpu.SMEM)]
        + [whole] * (len(tokens) + len(routes))
        + [pl.BlockSpec(memory_space=pl.ANY)],
        out_specs=(whole, whole),
        scratch_shapes=[
            pltpu.VMEM((total, width), BF16),
            pltpu.VMEM((2 * group, quarter, 2, width), BF16),
            pltpu.SemaphoreType.DMA((2 * group,)),
        ],
        compiler_params=params(40),
        cost_estimate=pl.CostEstimate(
            flops=2 * group * 8 * quarter * width * 256,
            bytes_accessed=group * 16 * quarter * width,
            transcendentals=0,
        ),
        name="gate_up",
    )(where, *tokens, *routes, gu_weight)


def hidden_kernel(keep_ref, near_ref, far_ref, out_ref, sums):
    units = out_ref.shape[1]
    for n in range(sums.shape[0]):
        lanes = slice(n * LANES, (n + 1) * LANES)
        total = keep_ref[0, :, lanes].astype(F32) + near_ref[0, :, lanes].astype(F32)
        sums[n] = total + far_ref[:, lanes].astype(F32)
        gate = sums[n, pl.ds(0, units, stride=2), :]
        up = sums[n, pl.ds(1, units, stride=2), :]
        out_ref[lanes, :] = (gate / (1.0 + jnp.exp(-gate)) * up).T.astype(BF16)


def hidden_quarter(keep, near, far):
    _, doubled, columns = keep.shape
    mine = pl.BlockSpec((1, doubled, columns), lambda i: (1, 0, 0))
    return pl.pallas_call(
        hidden_kernel,
        grid=(1,),
        out_shape=jax.ShapeDtypeStruct((columns, doubled // 2), BF16),
        in_specs=[mine, mine, pl.BlockSpec((doubled, columns), lambda i: (0, 0))],
        out_specs=pl.BlockSpec((columns, doubled // 2), lambda i: (0, 0)),
        scratch_shapes=[pltpu.VMEM((columns // LANES, doubled, LANES), F32)],
        compiler_params=params(24),
        name="hidden",
    )(keep, near, far)


def add_kernel(keep_ref, near_ref, out_ref):
    out_ref[...] = (keep_ref[0].astype(F32) + near_ref[0].astype(F32)).astype(BF16)


def chip_sum(keep, near):
    _, doubled, columns = keep.shape
    other = pl.BlockSpec((1, doubled, columns), lambda i: (0, 0, 0))
    return pl.pallas_call(
        add_kernel,
        grid=(1,),
        out_shape=jax.ShapeDtypeStruct((doubled, columns), BF16),
        in_specs=[other, other],
        out_specs=pl.BlockSpec((doubled, columns), lambda i: (0, 0)),
        compiler_params=params(24),
        name="chip_sum",
    )(keep, near)


def down_kernel(group, n_blocks, chunk, has_carry, where_ref, *refs):
    hidden_refs, refs = refs[:4], refs[4:]
    route_refs, refs = refs[:n_blocks], refs[n_blocks:]
    w_hbm, refs = refs[0], refs[1:]
    carry_ref, refs = (refs[0], refs[1:]) if has_carry else (None, refs)
    out_refs, refs = refs[:n_blocks], refs[n_blocks:]
    held, w_buf, sems = refs
    rows = n_blocks * CAP
    quarter = w_hbm.shape[1] // 4
    count = route_refs[0].shape[1]
    expert0 = where_ref[0]
    x, core = where_ref[1], where_ref[2]
    order = [(x, core), (1 - x, core), (x, 1 - core), (1 - x, 1 - core)]

    def fetch(e, j):
        f0 = pl.multiple_of((order[j][0] * 2 + order[j][1]) * quarter, quarter)
        return pltpu.make_async_copy(
            w_hbm.at[chunk * group + e, pl.ds(f0, quarter)],
            w_buf.at[e, pl.ds(j * quarter, quarter)],
            sems.at[e, j],
        )

    for e in range(group):
        for j in range(4):
            fetch(e, j).start()
    for e in range(group):
        units = jnp.concatenate([h[e * rows : (e + 1) * rows, :] for h in hidden_refs], axis=1)
        for j in range(4):
            fetch(e, j).wait()
        out = lax.dot_general(units, w_buf[e], NN, preferred_element_type=F32).astype(BF16)
        for i in range(n_blocks):
            held[i, e * CAP : (e + 1) * CAP, :] = out[i * CAP : (i + 1) * CAP]
    slot_of = lax.broadcasted_iota(jnp.int32, (CAP, count), 0).astype(F32)
    for i in range(n_blocks):
        table = [
            jnp.where(
                route_refs[i][pl.ds(expert0 + e, 1), :] == slot_of,
                route_refs[i][pl.ds(EXPERTS + expert0 + e, 1), :],
                0.0,
            )
            for e in range(group)
        ]
        table = jnp.concatenate(table, axis=0).astype(BF16)
        total = lax.dot_general(table, held[i], TN, preferred_element_type=F32)
        if has_carry:
            total = total + carry_ref[i]
            out_refs[i][...] = total.astype(BF16)
        else:
            out_refs[0][i] = total


def down(where, hidden, routes, down_weight, chunk, group, carry):
    rows, units = hidden[0].shape
    n_blocks = len(routes)
    count = routes[0].shape[1]
    width = down_weight.shape[2]
    whole = pl.BlockSpec(memory_space=pltpu.VMEM)
    if carry is None:
        kernel = functools.partial(down_first_kernel, group, n_blocks, chunk)
        out_shape = (jax.ShapeDtypeStruct((n_blocks, count, width), F32),)
        carried = []
    else:
        kernel = functools.partial(down_kernel, group, n_blocks, chunk, True)
        out_shape = tuple(jax.ShapeDtypeStruct((count, width), BF16) for _ in routes)
        carried = [carry]
    return pl.pallas_call(
        kernel,
        out_shape=out_shape,
        in_specs=[pl.BlockSpec(memory_space=pltpu.SMEM)]
        + [whole] * (4 + n_blocks)
        + [pl.BlockSpec(memory_space=pl.ANY)]
        + [whole] * len(carried),
        out_specs=tuple(whole for _ in out_shape),
        scratch_shapes=[
            pltpu.VMEM((n_blocks, group * CAP, width), BF16),
            pltpu.VMEM((group, 4 * units, width), BF16),
            pltpu.SemaphoreType.DMA((group, 4)),
        ],
        compiler_params=params(40),
        cost_estimate=pl.CostEstimate(
            flops=2 * group * 4 * units * width * 256,
            bytes_accessed=group * 8 * units * width,
            transcendentals=0,
        ),
        name="down",
    )(where, *hidden, *routes, down_weight, *carried)


def down_first_kernel(group, n_blocks, chunk, where_ref, *refs):
    ins, out_ref, scratch = refs[: 5 + n_blocks], refs[5 + n_blocks], refs[6 + n_blocks :]
    outs = (out_ref,) * n_blocks
    down_kernel(group, n_blocks, chunk, False, where_ref, *ins, *outs, *scratch)


def one_pass(z, x, core, blocks, routes, gu_weight, down_weight, group):
    local = gu_weight.shape[0]
    carry = None
    stages = []
    for chunk in range(local // group):
        where = jnp.stack([z * local + chunk * group, x, core]).astype(jnp.int32)
        send, keep = gate_up(where, blocks, routes, gu_weight, chunk, group)
        near = lax.ppermute(send, "tp", ACROSS_CORE)
        far = lax.ppermute(chip_sum(keep, near), "tp", ACROSS_X)
        own = hidden_quarter(keep, near, far)
        own_x = lax.ppermute(own, "tp", ACROSS_X)
        own_core = lax.ppermute(own, "tp", ACROSS_CORE)
        both = lax.ppermute(own_x, "tp", ACROSS_CORE)
        stages.append((where, (own, own_x, own_core, both)))
    for chunk, (where, hidden) in enumerate(stages):
        carry = down(where, hidden, routes, down_weight, chunk, group, carry)
        if chunk == 0:
            carry = carry[0]
    return carry


def local_square(tokens, expert_ids, gate_weights, gu_weight, down_weight):
    z, t = lax.axis_index("ep"), lax.axis_index("tp")
    x, core = t // 2, t % 2
    group = 4

    def hop(array, pairs):
        return lax.ppermute(array, "ep", pairs)

    table = route(expert_ids, gate_weights)
    neighbour = hop(tokens, PAIR)
    table_1 = hop(table, PAIR)
    middle_1 = hop(tokens, MIDDLE)
    table_2 = hop(table, [(i, i ^ 2) for i in range(4)])
    table_3 = hop(table, [(i, i ^ 3) for i in range(4)])
    inner = (z == 1) | (z == 2)
    table_in = jnp.where(inner, table_3, table_2)
    table_out = jnp.where(inner, table_2, table_3)
    middle_2 = hop(neighbour, MIDDLE)
    end_1 = hop(middle_1, OUTWARD)
    end_2 = hop(middle_2, OUTWARD)

    own, other = one_pass(
        z, x, core, [(tokens,), (neighbour,)], [table, table_1], gu_weight, down_weight, group
    )
    far_in, far_out = one_pass(
        z, x, core, [(middle_1, end_1), (middle_2, end_2)], [table_in, table_out],
        gu_weight, down_weight, group,
    )

    def plus(a, b):
        return (a.astype(F32) + b.astype(F32)).astype(BF16)

    out_inner = hop(far_out, INWARD)
    in_inner = hop(far_in, INWARD)
    out_mid = hop(plus(far_out, out_inner), MIDDLE)
    in_mid = hop(plus(far_in, in_inner), MIDDLE)
    last = hop(plus(other, out_mid), PAIR)
    return (own.astype(F32) + in_mid.astype(F32) + last.astype(F32)).astype(BF16)


def local_general(tokens, expert_ids, gate_weights, gu_weight, down_weight):
    tok_rows, local_width = tokens.shape
    table = route(expert_ids, gate_weights)
    slots = jnp.arange(CAP, dtype=jnp.int32).astype(F32)
    matches = table[:EXPERTS, None, :] == slots[None, :, None]
    dispatch_table = matches.astype(BF16).reshape(EXPERTS * CAP, tok_rows)
    outgoing = jnp.dot(dispatch_table, tokens, preferred_element_type=F32)
    outgoing = outgoing.astype(BF16).reshape(EXPERTS, CAP, local_width)
    received = lax.all_to_all(outgoing, "ep", split_axis=0, concat_axis=1, tiled=True)
    terms = jnp.einsum("efgd,esd->fegs", gu_weight, received, preferred_element_type=F32)
    totals = lax.psum(terms.astype(BF16), "tp").astype(F32)
    hidden = (jax.nn.silu(totals[:, :, 0]) * totals[:, :, 1]).astype(BF16)
    expert_out = jnp.einsum("fes,efd->esd", hidden, down_weight, preferred_element_type=F32)
    returned = lax.all_to_all(
        expert_out.astype(BF16), "ep", split_axis=1, concat_axis=0, tiled=True
    )
    combine_table = jnp.where(matches, table[EXPERTS:, None, :], 0.0).astype(BF16)
    mixed = lax.dot_general(
        combine_table.reshape(EXPERTS * CAP, tok_rows),
        returned.reshape(EXPERTS * CAP, local_width),
        TN,
        preferred_element_type=F32,
    )
    return mixed.astype(BF16)


def solution(mesh):
    placed = (
        P(("grp", "ep"), "tp"),
        P(("grp", "ep"), None),
        P(("grp", "ep"), None),
        P("ep", None, None, "tp"),
        P("ep", None, "tp"),
    )
    square = mesh.shape["ep"] == 4 and mesh.shape["tp"] == 4
    return jax.shard_map(
        local_square if square else local_general,
        mesh=mesh,
        in_specs=placed,
        out_specs=P(("grp", "ep"), "tp"),
        check_vma=False,
    )
```

```python
import functools

import jax
import jax.numpy as jnp
from jax import lax
from jax.experimental import pallas as pl
from jax.experimental.pallas import tpu as pltpu
from jax.sharding import PartitionSpec as P

EXPERTS = 32
TOPK = 6
CAP = 48
LANES = 128
BF16, F32 = jnp.bfloat16, jnp.float32
NT = (((1,), (1,)), ((), ()))
TN = (((0,), (0,)), ((), ()))
NN = (((1,), (0,)), ((), ()))

PAIR = [(0, 1), (1, 0), (2, 3), (3, 2)]
MIDDLE = [(1, 2), (2, 1)]
OUTWARD = [(1, 0), (2, 3)]
INWARD = [(0, 1), (3, 2)]
ACROSS_X = [(0, 2), (1, 3), (2, 0), (3, 1)]
ACROSS_CORE = [(0, 1), (1, 0), (2, 3), (3, 2)]


QUICK = pl.CostEstimate(flops=1024, bytes_accessed=1024, transcendentals=0)


def params(mib):
    return pltpu.CompilerParams(vmem_limit_bytes=mib << 20)


def route_kernel(ids_ref, gates_ref, out_ref):
    count = ids_ref.shape[1]
    expert = lax.broadcasted_iota(jnp.int32, (EXPERTS, count), 0)
    weight = jnp.zeros((EXPERTS, count), F32)
    chosen = jnp.zeros((EXPERTS, count), F32)
    for k in range(TOPK):
        hit = ids_ref[k : k + 1, :] == expert
        chosen = jnp.where(hit, 1.0, chosen)
        weight = jnp.where(hit, gates_ref[k : k + 1, :], weight)
    first = lax.broadcasted_iota(jnp.int32, (count, count), 0)
    second = lax.broadcasted_iota(jnp.int32, (count, count), 1)
    before = jnp.where(first < second, 1.0, 0.0).astype(BF16)
    position = lax.dot_general(chosen.astype(BF16), before, NN, preferred_element_type=F32)
    out_ref[:EXPERTS, :] = jnp.where(chosen > 0.0, position, -1.0)
    out_ref[EXPERTS:, :] = weight


def route(expert_ids, gate_weights):
    return pl.pallas_call(
        route_kernel,
        out_shape=jax.ShapeDtypeStruct((2 * EXPERTS, expert_ids.shape[0]), F32),
        name="route",
    )(expert_ids.T, gate_weights.T.astype(F32))


def windows(group, rows):
    found, base = [], 0
    for e in range(group):
        first = e * rows // LANES
        last = -(-(e + 1) * rows // LANES)
        found.append((first, last - first, e * rows - first * LANES, base))
        base += (last - first) * LANES
    return found, base


def gate_up_kernel(group, n_blocks, n_parts, chunk, where_ref, *refs):
    token_refs, refs = refs[: sum(n_parts)], refs[sum(n_parts) :]
    route_refs, refs = refs[:n_blocks], refs[n_blocks:]
    w_hbm, _, send_ref, keep_ref, rows_ref, w_buf, sems = refs
    rows = n_blocks * CAP
    found, _ = windows(group, rows)
    quarter = w_hbm.shape[1] // 4
    count = route_refs[0].shape[1]
    expert0 = where_ref[0]
    x, core = where_ref[1], where_ref[2]
    order = [(1 - x, 1 - core), (x, 1 - core), (1 - x, core), (x, core)]

    def fetch(e):
        copies = []
        for j in range(4):
            f0 = pl.multiple_of((order[j][0] * 2 + order[j][1]) * quarter, quarter)
            copies.append(
                pltpu.make_async_copy(
                    w_hbm.at[chunk * group + e, pl.ds(f0, quarter)],
                    w_buf.at[e, pl.ds(j * quarter, quarter)],
                    sems.at[e, j],
                )
            )
        return copies

    def start(e):
        for copy in fetch(e):
            copy.start()

    start(0)
    rows_ref[...] = jnp.zeros_like(rows_ref)
    slot_of = lax.broadcasted_iota(jnp.int32, (CAP, count), 0).astype(F32)
    part = 0
    for i in range(n_blocks):
        table = [
            jnp.where(route_refs[i][pl.ds(expert0 + e, 1), :] == slot_of, 1.0, 0.0)
            for e in range(group)
        ]
        table = jnp.concatenate(table, axis=0).astype(BF16)
        tokens = token_refs[part][...]
        for extra in range(1, n_parts[i]):
            tokens = tokens + token_refs[part + extra][...]
        part += n_parts[i]
        placed = lax.dot_general(table, tokens, NN, preferred_element_type=F32).astype(BF16)
        for e in range(group):
            _, _, offset, base = found[e]
            at = base + offset + i * CAP
            rows_ref[at : at + CAP, :] = placed[e * CAP : (e + 1) * CAP]

    tiles = {}
    for e in range(group):
        first, width, _, base = found[e]
        if e + 1 < group:
            if e == 0:
                start(1)
            for copy in fetch(e):
                copy.wait()
            if e > 0:
                start(e + 1)
        else:
            for copy in fetch(e):
                copy.wait()
        w = w_buf[e].reshape(8 * quarter, w_buf.shape[3])
        r = rows_ref[base : base + width * LANES, :]
        part_sum = lax.dot_general(w, r, NT, preferred_element_type=F32)
        for n in range(width):
            piece = part_sum[:, n * LANES : (n + 1) * LANES]
            held = tiles.get(first + n)
            tiles[first + n] = piece if held is None else held + piece
        for n in sorted(tiles):
            if (n + 1) * LANES > (e + 1) * rows:
                continue
            tile = tiles.pop(n).astype(BF16)
            for j in range(4):
                target = send_ref if j < 2 else keep_ref
                target[j % 2, :, n * LANES : (n + 1) * LANES] = tile[
                    2 * j * quarter : 2 * (j + 1) * quarter
                ]


def gate_up(where, blocks, routes, gu_weight, chunk, group, after):
    n_parts = tuple(len(b) for b in blocks)
    tokens = [t for b in blocks for t in b]
    rows = len(blocks) * CAP
    _, total = windows(group, rows)
    units, width = gu_weight.shape[1], gu_weight.shape[3]
    half = jax.ShapeDtypeStruct((2, units // 2, group * rows), BF16)
    whole = pl.BlockSpec(memory_space=pltpu.VMEM)
    return pl.pallas_call(
        functools.partial(gate_up_kernel, group, len(blocks), n_parts, chunk),
        out_shape=(half, half),
        in_specs=[pl.BlockSpec(memory_space=pltpu.SMEM)]
        + [whole] * (len(tokens) + len(routes))
        + [pl.BlockSpec(memory_space=pl.ANY)] * 2,
        out_specs=(whole, whole),
        scratch_shapes=[
            pltpu.VMEM((total, width), BF16),
            pltpu.VMEM((group, units, 2, width), BF16),
            pltpu.SemaphoreType.DMA((group, 4)),
        ],
        compiler_params=params(44),
        cost_estimate=QUICK,
        name="gate_up",
    )(where, *tokens, *routes, gu_weight, after)


def hidden_kernel(keep_ref, near_ref, far_ref, _, out_ref, sums):
    units = out_ref.shape[1]
    for n in range(sums.shape[0]):
        lanes = slice(n * LANES, (n + 1) * LANES)
        total = keep_ref[0, :, lanes].astype(F32) + near_ref[0, :, lanes].astype(F32)
        sums[n] = total + far_ref[:, lanes].astype(F32)
        gate = sums[n, pl.ds(0, units, stride=2), :]
        up = sums[n, pl.ds(1, units, stride=2), :]
        out_ref[lanes, :] = (gate / (1.0 + jnp.exp(-gate)) * up).T.astype(BF16)


def hidden_quarter(keep, near, far, after):
    _, doubled, columns = keep.shape
    mine = pl.BlockSpec((1, doubled, columns), lambda i: (1, 0, 0))
    return pl.pallas_call(
        hidden_kernel,
        grid=(1,),
        out_shape=jax.ShapeDtypeStruct((columns, doubled // 2), BF16),
        in_specs=[
            mine,
            mine,
            pl.BlockSpec((doubled, columns), lambda i: (0, 0)),
            pl.BlockSpec(memory_space=pl.ANY),
        ],
        out_specs=pl.BlockSpec((columns, doubled // 2), lambda i: (0, 0)),
        scratch_shapes=[pltpu.VMEM((columns // LANES, doubled, LANES), F32)],
        compiler_params=params(24),
        cost_estimate=QUICK,
        name="hidden",
    )(keep, near, far, after)


def add_kernel(keep_ref, near_ref, _, out_ref):
    out_ref[...] = (keep_ref[0].astype(F32) + near_ref[0].astype(F32)).astype(BF16)


def chip_sum(keep, near, after):
    _, doubled, columns = keep.shape
    other = pl.BlockSpec((1, doubled, columns), lambda i: (0, 0, 0))
    return pl.pallas_call(
        add_kernel,
        grid=(1,),
        out_shape=jax.ShapeDtypeStruct((doubled, columns), BF16),
        in_specs=[other, other, pl.BlockSpec(memory_space=pl.ANY)],
        out_specs=pl.BlockSpec((doubled, columns), lambda i: (0, 0)),
        compiler_params=params(24),
        cost_estimate=QUICK,
        name="chip_sum",
    )(keep, near, after)


def down_kernel(group, n_blocks, chunk, has_carry, where_ref, *refs):
    hidden_refs, refs = refs[:4], refs[4:]
    route_refs, refs = refs[:n_blocks], refs[n_blocks:]
    w_hbm, refs = refs[0], refs[2:]
    carry_ref, refs = (refs[0], refs[1:]) if has_carry else (None, refs)
    out_refs, (held, w_buf, sems) = refs[:-3], refs[-3:]
    rows = n_blocks * CAP
    quarter = w_hbm.shape[1] // 4
    count = route_refs[0].shape[1]
    expert0 = where_ref[0]
    x, core = where_ref[1], where_ref[2]
    order = [(x, core), (1 - x, core), (x, 1 - core), (1 - x, 1 - core)]

    def fetch(e):
        copies = []
        for j in range(4):
            f0 = pl.multiple_of((order[j][0] * 2 + order[j][1]) * quarter, quarter)
            copies.append(
                pltpu.make_async_copy(
                    w_hbm.at[chunk * group + e, pl.ds(f0, quarter)],
                    w_buf.at[e, pl.ds(j * quarter, quarter)],
                    sems.at[e, j],
                )
            )
        return copies

    def start(e):
        for copy in fetch(e):
            copy.start()

    start(0)
    start(1)
    for e in range(group):
        for copy in fetch(e):
            copy.wait()
        if e + 2 < group:
            start(e + 2)
        units = jnp.concatenate([h[e * rows : (e + 1) * rows, :] for h in hidden_refs], axis=1)
        out = lax.dot_general(units, w_buf[e], NN, preferred_element_type=F32).astype(BF16)
        for i in range(n_blocks):
            held[i, e * CAP : (e + 1) * CAP, :] = out[i * CAP : (i + 1) * CAP]
    slot_of = lax.broadcasted_iota(jnp.int32, (CAP, count), 0).astype(F32)
    for i in range(n_blocks):
        table = [
            jnp.where(
                route_refs[i][pl.ds(expert0 + e, 1), :] == slot_of,
                route_refs[i][pl.ds(EXPERTS + expert0 + e, 1), :],
                0.0,
            )
            for e in range(group)
        ]
        table = jnp.concatenate(table, axis=0).astype(BF16)
        total = lax.dot_general(table, held[i], TN, preferred_element_type=F32)
        if has_carry:
            out_refs[i][...] = (total + carry_ref[i]).astype(BF16)
        else:
            out_refs[0][i] = total


def down(where, hidden, routes, down_weight, chunk, group, carry, after):
    n_blocks = len(routes)
    units = hidden[0].shape[1]
    count = routes[0].shape[1]
    width = down_weight.shape[2]
    whole = pl.BlockSpec(memory_space=pltpu.VMEM)
    carried = [] if carry is None else [carry]
    if carry is None:
        out_shape = (jax.ShapeDtypeStruct((n_blocks, count, width), F32),)
    else:
        out_shape = tuple(jax.ShapeDtypeStruct((count, width), BF16) for _ in routes)
    return pl.pallas_call(
        functools.partial(down_kernel, group, n_blocks, chunk, carry is not None),
        out_shape=out_shape,
        in_specs=[pl.BlockSpec(memory_space=pltpu.SMEM)]
        + [whole] * (4 + n_blocks)
        + [pl.BlockSpec(memory_space=pl.ANY)] * 2
        + [whole] * len(carried),
        out_specs=tuple(whole for _ in out_shape),
        scratch_shapes=[
            pltpu.VMEM((n_blocks, group * CAP, width), BF16),
            pltpu.VMEM((group, 4 * units, width), BF16),
            pltpu.SemaphoreType.DMA((group, 4)),
        ],
        compiler_params=params(40),
        cost_estimate=QUICK,
        name="down",
    )(where, *hidden, *routes, down_weight, after, *carried)


class Part:
    def __init__(self, place, blocks, routes, chunk, group):
        z, x, core, local = place
        self.where = jnp.stack([z * local + chunk * group, x, core]).astype(jnp.int32)
        self.blocks, self.routes, self.chunk, self.group = blocks, routes, chunk, group

    def sums(self, gu_weight, after):
        send, self.keep = gate_up(
            self.where, self.blocks, self.routes, gu_weight, self.chunk, self.group, after
        )
        self.near = lax.ppermute(send, "tp", ACROSS_CORE)
        return send

    def across(self, after):
        total = chip_sum(self.keep, self.near, after)
        self.far = lax.ppermute(total, "tp", ACROSS_X)
        return total

    def activate(self, after):
        own = hidden_quarter(self.keep, self.near, self.far, after)
        own_x = lax.ppermute(own, "tp", ACROSS_X)
        own_core = lax.ppermute(own, "tp", ACROSS_CORE)
        both = lax.ppermute(own_x, "tp", ACROSS_CORE)
        self.hidden = (own, own_x, own_core, both)
        return own

    def outputs(self, down_weight, carry, after):
        return down(
            self.where, self.hidden, self.routes, down_weight, self.chunk, self.group, carry, after
        )


def local_square(tokens, expert_ids, gate_weights, gu_weight, down_weight):
    z, t = lax.axis_index("ep"), lax.axis_index("tp")
    x, core = t // 2, t % 2
    group = 4

    def hop(array, pairs):
        return lax.ppermute(array, "ep", pairs)

    table = route(expert_ids, gate_weights)
    neighbour = hop(tokens, PAIR)
    table_1 = hop(table, PAIR)
    middle_1 = hop(tokens, MIDDLE)
    table_2 = hop(table, [(i, i ^ 2) for i in range(4)])
    table_3 = hop(table, [(i, i ^ 3) for i in range(4)])
    inner = (z == 1) | (z == 2)
    table_in = jnp.where(inner, table_3, table_2)
    table_out = jnp.where(inner, table_2, table_3)
    middle_2 = hop(neighbour, MIDDLE)
    end_1 = hop(middle_1, OUTWARD)
    end_2 = hop(middle_2, OUTWARD)

    place = (z, x, core, gu_weight.shape[0])
    close, close_tables = [(tokens,), (neighbour,)], [table, table_1]
    away, away_tables = [(middle_1, end_1), (middle_2, end_2)], [table_in, table_out]
    a0, a1 = (Part(place, close, close_tables, n, group) for n in range(2))
    b0, b1 = (Part(place, away, away_tables, n, group) for n in range(2))
    turn = a0.sums(gu_weight, table)
    turn = a0.across(turn)
    turn = a1.sums(gu_weight, turn)
    turn = a0.activate(turn)
    turn = a1.across(turn)
    turn = b0.sums(gu_weight, turn)
    turn = a1.activate(turn)
    turn = b0.across(turn)
    turn = b1.sums(gu_weight, turn)
    turn = b0.activate(turn)
    turn = b1.across(turn)
    (turn,) = a0.outputs(down_weight, None, turn)
    own, other = a1.outputs(down_weight, turn, turn)
    turn = b1.activate(own)
    (turn,) = b0.outputs(down_weight, None, turn)
    far_in, far_out = b1.outputs(down_weight, turn, turn)

    def plus(a, b):
        return (a.astype(F32) + b.astype(F32)).astype(BF16)

    from_neighbour = hop(other, PAIR)
    out_inner = hop(far_out, INWARD)
    in_inner = hop(far_in, INWARD)
    out_mid = hop(plus(far_out, out_inner), MIDDLE)
    in_mid = hop(plus(far_in, in_inner), MIDDLE)
    out_end = hop(out_mid, OUTWARD)
    total = own.astype(F32) + from_neighbour.astype(F32)
    return (total + in_mid.astype(F32) + out_end.astype(F32)).astype(BF16)


def local_general(tokens, expert_ids, gate_weights, gu_weight, down_weight):
    tok_rows, local_width = tokens.shape
    table = route(expert_ids, gate_weights)
    slots = jnp.arange(CAP, dtype=jnp.int32).astype(F32)
    matches = table[:EXPERTS, None, :] == slots[None, :, None]
    dispatch_table = matches.astype(BF16).reshape(EXPERTS * CAP, tok_rows)
    outgoing = jnp.dot(dispatch_table, tokens, preferred_element_type=F32)
    outgoing = outgoing.astype(BF16).reshape(EXPERTS, CAP, local_width)
    received = lax.all_to_all(outgoing, "ep", split_axis=0, concat_axis=1, tiled=True)
    terms = jnp.einsum("efgd,esd->fegs", gu_weight, received, preferred_element_type=F32)
    totals = lax.psum(terms.astype(BF16), "tp").astype(F32)
    hidden = (jax.nn.silu(totals[:, :, 0]) * totals[:, :, 1]).astype(BF16)
    expert_out = jnp.einsum("fes,efd->esd", hidden, down_weight, preferred_element_type=F32)
    returned = lax.all_to_all(
        expert_out.astype(BF16), "ep", split_axis=1, concat_axis=0, tiled=True
    )
    combine_table = jnp.where(matches, table[EXPERTS:, None, :], 0.0).astype(BF16)
    mixed = lax.dot_general(
        combine_table.reshape(EXPERTS * CAP, tok_rows),
        returned.reshape(EXPERTS * CAP, local_width),
        TN,
        preferred_element_type=F32,
    )
    return mixed.astype(BF16)


def solution(mesh):
    placed = (
        P(("grp", "ep"), "tp"),
        P(("grp", "ep"), None),
        P(("grp", "ep"), None),
        P("ep", None, None, "tp"),
        P("ep", None, "tp"),
    )
    square = mesh.shape["ep"] == 4 and mesh.shape["tp"] == 4
    return jax.shard_map(
        local_square if square else local_general,
        mesh=mesh,
        in_specs=placed,
        out_specs=P(("grp", "ep"), "tp"),
        check_vma=False,
    )
```

```python
import functools

import jax
import jax.numpy as jnp
from jax import lax
from jax.experimental import pallas as pl
from jax.experimental.pallas import tpu as pltpu
from jax.sharding import PartitionSpec as P

EXPERTS = 32
TOPK = 6
CAP = 48
LANES = 128
BF16, F32 = jnp.bfloat16, jnp.float32
NT = (((1,), (1,)), ((), ()))
TN = (((0,), (0,)), ((), ()))
NN = (((1,), (0,)), ((), ()))

PAIR = [(0, 1), (1, 0), (2, 3), (3, 2)]
MIDDLE = [(1, 2), (2, 1)]
OUTWARD = [(1, 0), (2, 3)]
INWARD = [(0, 1), (3, 2)]
ACROSS_X = [(0, 2), (1, 3), (2, 0), (3, 1)]
ACROSS_CORE = [(0, 1), (1, 0), (2, 3), (3, 2)]


QUICK = pl.CostEstimate(flops=1024, bytes_accessed=1024, transcendentals=0)


SLOW = pl.CostEstimate(flops=20_000_000_000, bytes_accessed=1024, transcendentals=0)


def params(mib):
    return pltpu.CompilerParams(vmem_limit_bytes=mib << 20)


def route_kernel(ids_ref, gates_ref, out_ref):
    count = ids_ref.shape[1]
    expert = lax.broadcasted_iota(jnp.int32, (EXPERTS, count), 0)
    weight = jnp.zeros((EXPERTS, count), F32)
    chosen = jnp.zeros((EXPERTS, count), F32)
    for k in range(TOPK):
        hit = ids_ref[k : k + 1, :] == expert
        chosen = jnp.where(hit, 1.0, chosen)
        weight = jnp.where(hit, gates_ref[k : k + 1, :], weight)
    first = lax.broadcasted_iota(jnp.int32, (count, count), 0)
    second = lax.broadcasted_iota(jnp.int32, (count, count), 1)
    before = jnp.where(first < second, 1.0, 0.0).astype(BF16)
    position = lax.dot_general(chosen.astype(BF16), before, NN, preferred_element_type=F32)
    out_ref[:EXPERTS, :] = jnp.where(chosen > 0.0, position, -1.0)
    out_ref[EXPERTS:, :] = weight


def route(expert_ids, gate_weights):
    return pl.pallas_call(
        route_kernel,
        out_shape=jax.ShapeDtypeStruct((2 * EXPERTS, expert_ids.shape[0]), F32),
        name="route",
    )(expert_ids.T, gate_weights.T.astype(F32))


def place_kernel(experts, where_ref, *refs):
    *token_refs, table_ref, out_ref = refs
    count = table_ref.shape[1]
    slot_of = lax.broadcasted_iota(jnp.int32, (CAP, count), 0).astype(F32)
    table = [
        jnp.where(table_ref[pl.ds(where_ref[0] + e, 1), :] == slot_of, 1.0, 0.0)
        for e in range(experts)
    ]
    tokens = token_refs[0][...]
    for extra in token_refs[1:]:
        tokens = tokens + extra[...]
    table = jnp.concatenate(table, axis=0).astype(BF16)
    rows = lax.dot_general(table, tokens, NN, preferred_element_type=F32).astype(BF16)
    for e in range(experts):
        out_ref[e] = rows[e * CAP : (e + 1) * CAP]


def place(where, tokens, table, experts):
    whole = pl.BlockSpec(memory_space=pltpu.VMEM)
    return pl.pallas_call(
        functools.partial(place_kernel, experts),
        out_shape=jax.ShapeDtypeStruct((experts, CAP, tokens[0].shape[1]), BF16),
        in_specs=[pl.BlockSpec(memory_space=pltpu.SMEM)] + [whole] * (len(tokens) + 1),
        out_specs=whole,
        compiler_params=params(24),
        cost_estimate=QUICK,
        name="place",
    )(where, *tokens, table)


def gate_up_kernel(n_blocks, where_ref, *refs):
    row_refs = refs[:n_blocks]
    w_ref, _, send_ref, keep_ref, rows_ref, carry = refs[n_blocks:]
    step = pl.program_id(0)
    rows = n_blocks * CAP
    spare = 2 * LANES - rows
    x, core = where_ref[1], where_ref[2]
    quarter = w_ref.shape[1] // 4

    @pl.when(step == 0)
    def _():
        rows_ref[...] = jnp.zeros_like(rows_ref)

    def product(parity):
        for i in range(n_blocks):
            at = parity * spare + i * CAP
            rows_ref[parity, at : at + CAP, :] = row_refs[i][0]
        w = w_ref[0].reshape(8 * quarter, w_ref.shape[3])
        return lax.dot_general(w, rows_ref[parity], NT, preferred_element_type=F32)

    def store(tile, lane):
        tile = tile.astype(BF16)
        for q in range(4):
            piece = tile[2 * q * quarter : 2 * (q + 1) * quarter]
            at = jnp.where(x == q // 2, 1, 0)

            @pl.when(core == q % 2)
            def _():
                keep_ref[at, :, lane : lane + LANES] = piece

            @pl.when(core != q % 2)
            def _():
                send_ref[at, :, lane : lane + LANES] = piece

    @pl.when(lax.rem(step, 2) == 0)
    def _():
        out = product(0)
        store(out[:, :LANES], 0)
        carry[...] = out[:, LANES:]

    @pl.when(lax.rem(step, 2) == 1)
    def _():
        out = product(1)
        store(carry[...] + out[:, :LANES], LANES)
        store(out[:, LANES:], 2 * LANES)


def gate_up(where, placed, gu_weight, chunk, group, after):
    _, units, _, width = gu_weight.shape
    n_blocks = len(placed)
    lanes = 2 * n_blocks * CAP
    half = jax.ShapeDtypeStruct((2, units // 2, group // 2 * lanes), BF16)
    pair = pl.BlockSpec((2, units // 2, lanes), lambda i: (0, 0, i // 2))
    return pl.pallas_call(
        functools.partial(gate_up_kernel, n_blocks),
        grid=(group,),
        out_shape=(half, half),
        in_specs=[pl.BlockSpec(memory_space=pltpu.SMEM)]
        + [pl.BlockSpec((1, CAP, width), lambda i: (chunk * group + i, 0, 0))] * n_blocks
        + [pl.BlockSpec((1, units, 2, width), lambda i: (chunk * group + i, 0, 0, 0))]
        + [pl.BlockSpec(memory_space=pl.ANY)],
        out_specs=(pair, pair),
        scratch_shapes=[
            pltpu.VMEM((2, 2 * LANES, width), BF16),
            pltpu.VMEM((2 * units, LANES), F32),
        ],
        compiler_params=params(48),
        cost_estimate=QUICK,
        name="gate_up",
    )(where, *placed, gu_weight, after)


def hidden_kernel(keep_ref, near_ref, far_ref, _, out_ref, sums):
    units = out_ref.shape[1]
    for n in range(sums.shape[0]):
        lanes = slice(n * LANES, (n + 1) * LANES)
        total = keep_ref[0, :, lanes].astype(F32) + near_ref[0, :, lanes].astype(F32)
        sums[n] = total + far_ref[:, lanes].astype(F32)
        gate = sums[n, pl.ds(0, units, stride=2), :]
        up = sums[n, pl.ds(1, units, stride=2), :]
        out_ref[lanes, :] = (gate / (1.0 + jnp.exp(-gate)) * up).T.astype(BF16)


def hidden_quarter(keep, near, far, after):
    _, doubled, columns = keep.shape
    mine = pl.BlockSpec((1, doubled, columns), lambda i: (1, 0, 0))
    return pl.pallas_call(
        hidden_kernel,
        grid=(1,),
        out_shape=jax.ShapeDtypeStruct((columns, doubled // 2), BF16),
        in_specs=[
            mine,
            mine,
            pl.BlockSpec((doubled, columns), lambda i: (0, 0)),
            pl.BlockSpec(memory_space=pl.ANY),
        ],
        out_specs=pl.BlockSpec((columns, doubled // 2), lambda i: (0, 0)),
        scratch_shapes=[pltpu.VMEM((columns // LANES, doubled, LANES), F32)],
        compiler_params=params(24),
        cost_estimate=SLOW,
        name="hidden",
    )(keep, near, far, after)


def add_kernel(keep_ref, near_ref, _, out_ref):
    out_ref[...] = (keep_ref[0].astype(F32) + near_ref[0].astype(F32)).astype(BF16)


def chip_sum(keep, near, after):
    _, doubled, columns = keep.shape
    other = pl.BlockSpec((1, doubled, columns), lambda i: (0, 0, 0))
    return pl.pallas_call(
        add_kernel,
        grid=(1,),
        out_shape=jax.ShapeDtypeStruct((doubled, columns), BF16),
        in_specs=[other, other, pl.BlockSpec(memory_space=pl.ANY)],
        out_specs=pl.BlockSpec((doubled, columns), lambda i: (0, 0)),
        compiler_params=params(24),
        cost_estimate=QUICK,
        name="chip_sum",
    )(keep, near, after)


def down_kernel(group, n_blocks, chunk, has_carry, where_ref, *refs):
    hidden_refs, refs = refs[:4], refs[4:]
    route_refs, refs = refs[:n_blocks], refs[n_blocks:]
    w_hbm, refs = refs[0], refs[2:]
    carry_ref, refs = (refs[0], refs[1:]) if has_carry else (None, refs)
    out_refs, (held, w_buf, sems) = refs[:-3], refs[-3:]
    rows = n_blocks * CAP
    quarter = w_hbm.shape[1] // 4
    count = route_refs[0].shape[1]
    expert0 = where_ref[0]
    x, core = where_ref[1], where_ref[2]
    order = [(x, core), (1 - x, core), (x, 1 - core), (1 - x, 1 - core)]

    def fetch(e):
        copies = []
        for j in range(4):
            f0 = pl.multiple_of((order[j][0] * 2 + order[j][1]) * quarter, quarter)
            copies.append(
                pltpu.make_async_copy(
                    w_hbm.at[chunk * group + e, pl.ds(f0, quarter)],
                    w_buf.at[e, pl.ds(j * quarter, quarter)],
                    sems.at[e, j],
                )
            )
        return copies

    def start(e):
        for copy in fetch(e):
            copy.start()

    start(0)
    start(1)
    for e in range(group):
        for copy in fetch(e):
            copy.wait()
        if e + 2 < group:
            start(e + 2)
        units = jnp.concatenate([h[e * rows : (e + 1) * rows, :] for h in hidden_refs], axis=1)
        out = lax.dot_general(units, w_buf[e], NN, preferred_element_type=F32).astype(BF16)
        for i in range(n_blocks):
            held[i, e * CAP : (e + 1) * CAP, :] = out[i * CAP : (i + 1) * CAP]
    slot_of = lax.broadcasted_iota(jnp.int32, (CAP, count), 0).astype(F32)
    for i in range(n_blocks):
        table = [
            jnp.where(
                route_refs[i][pl.ds(expert0 + e, 1), :] == slot_of,
                route_refs[i][pl.ds(EXPERTS + expert0 + e, 1), :],
                0.0,
            )
            for e in range(group)
        ]
        table = jnp.concatenate(table, axis=0).astype(BF16)
        total = lax.dot_general(table, held[i], TN, preferred_element_type=F32)
        if has_carry:
            out_refs[i][...] = (total + carry_ref[i]).astype(BF16)
        else:
            out_refs[0][i] = total


def down(where, hidden, routes, down_weight, chunk, group, carry, after):
    n_blocks = len(routes)
    units = hidden[0].shape[1]
    count = routes[0].shape[1]
    width = down_weight.shape[2]
    whole = pl.BlockSpec(memory_space=pltpu.VMEM)
    carried = [] if carry is None else [carry]
    if carry is None:
        out_shape = (jax.ShapeDtypeStruct((n_blocks, count, width), F32),)
    else:
        out_shape = tuple(jax.ShapeDtypeStruct((count, width), BF16) for _ in routes)
    return pl.pallas_call(
        functools.partial(down_kernel, group, n_blocks, chunk, carry is not None),
        out_shape=out_shape,
        in_specs=[pl.BlockSpec(memory_space=pltpu.SMEM)]
        + [whole] * (4 + n_blocks)
        + [pl.BlockSpec(memory_space=pl.ANY)] * 2
        + [whole] * len(carried),
        out_specs=tuple(whole for _ in out_shape),
        scratch_shapes=[
            pltpu.VMEM((n_blocks, group * CAP, width), BF16),
            pltpu.VMEM((group, 4 * units, width), BF16),
            pltpu.SemaphoreType.DMA((group, 4)),
        ],
        compiler_params=params(40),
        cost_estimate=QUICK,
        name="down",
    )(where, *hidden, *routes, down_weight, after, *carried)


def plus_kernel(a_ref, b_ref, _, out_ref, __):
    out_ref[...] = (a_ref[...].astype(F32) + b_ref[...].astype(F32)).astype(BF16)


def plus_then(a, b, other):
    whole = pl.BlockSpec(memory_space=pltpu.VMEM)
    free = pl.BlockSpec(memory_space=pl.ANY)
    return pl.pallas_call(
        plus_kernel,
        out_shape=(jax.ShapeDtypeStruct(a.shape, a.dtype), jax.ShapeDtypeStruct(a.shape, a.dtype)),
        in_specs=[whole, whole, free],
        out_specs=(whole, free),
        input_output_aliases={2: 1},
        compiler_params=params(16),
        cost_estimate=QUICK,
        name="plus",
    )(a, b, other)


def local_square(tokens, expert_ids, gate_weights, gu_weight, down_weight):
    z, t = lax.axis_index("ep"), lax.axis_index("tp")
    x, core = t // 2, t % 2
    local = gu_weight.shape[0]
    group = local // 2
    wheres = [jnp.stack([z * local + n * group, x, core]).astype(jnp.int32) for n in range(2)]

    def hop(array, pairs):
        return lax.ppermute(array, "ep", pairs)

    table = route(expert_ids, gate_weights)
    neighbour = hop(tokens, PAIR)
    table_1 = hop(table, PAIR)
    middle_1 = hop(tokens, MIDDLE)
    table_2 = hop(table, [(i, i ^ 2) for i in range(4)])
    table_3 = hop(table, [(i, i ^ 3) for i in range(4)])
    inner = (z == 1) | (z == 2)
    table_in = jnp.where(inner, table_3, table_2)
    table_out = jnp.where(inner, table_2, table_3)
    middle_2 = hop(neighbour, MIDDLE)
    end_1 = hop(middle_1, OUTWARD)
    end_2 = hop(middle_2, OUTWARD)

    tables = [table, table_1, table_in, table_out]
    blocks = [(tokens,), (neighbour,), (middle_1, end_1), (middle_2, end_2)]
    placed = [place(wheres[0], b, t, local) for b, t in zip(blocks, tables)]

    def sums(n, after):
        send, keep = gate_up(wheres[n], placed, gu_weight, n, group, after)
        return keep, lax.ppermute(send, "tp", ACROSS_CORE)

    def across(keep, near, after):
        total = chip_sum(keep, near, after)
        return total, lax.ppermute(total, "tp", ACROSS_X)

    def gathered(own):
        own_x = lax.ppermute(own, "tp", ACROSS_X)
        own_core = lax.ppermute(own, "tp", ACROSS_CORE)
        return own, own_x, own_core, lax.ppermute(own_x, "tp", ACROSS_CORE)

    keep_0, near_0 = sums(0, placed[3])
    turn, far_0 = across(keep_0, near_0, keep_0)
    keep_1, near_1 = sums(1, turn)
    own_0 = hidden_quarter(keep_0, near_0, far_0, keep_1)
    hidden_0 = gathered(own_0)
    turn, far_1 = across(keep_1, near_1, own_0)
    (carry,) = down(wheres[0], hidden_0, tables, down_weight, 0, group, None, turn)
    own_1 = hidden_quarter(keep_1, near_1, far_1, carry)
    hidden_1 = gathered(own_1)
    own, other, far_in, far_out = down(
        wheres[1], hidden_1, tables, down_weight, 1, group, carry, own_1
    )

    def plus(a, b):
        return (a.astype(F32) + b.astype(F32)).astype(BF16)

    out_inner = hop(far_out, INWARD)
    far_out, far_in = plus_then(far_out, out_inner, far_in)
    out_mid = hop(far_out, MIDDLE)
    in_inner = hop(far_in, INWARD)
    last = hop(plus(other, out_mid), PAIR)
    in_mid = hop(plus(far_in, in_inner), MIDDLE)
    return (own.astype(F32) + in_mid.astype(F32) + last.astype(F32)).astype(BF16)


def local_general(tokens, expert_ids, gate_weights, gu_weight, down_weight):
    tok_rows, local_width = tokens.shape
    table = route(expert_ids, gate_weights)
    slots = jnp.arange(CAP, dtype=jnp.int32).astype(F32)
    matches = table[:EXPERTS, None, :] == slots[None, :, None]
    dispatch_table = matches.astype(BF16).reshape(EXPERTS * CAP, tok_rows)
    outgoing = jnp.dot(dispatch_table, tokens, preferred_element_type=F32)
    outgoing = outgoing.astype(BF16).reshape(EXPERTS, CAP, local_width)
    received = lax.all_to_all(outgoing, "ep", split_axis=0, concat_axis=1, tiled=True)
    terms = jnp.einsum("efgd,esd->fegs", gu_weight, received, preferred_element_type=F32)
    totals = lax.psum(terms.astype(BF16), "tp").astype(F32)
    hidden = (jax.nn.silu(totals[:, :, 0]) * totals[:, :, 1]).astype(BF16)
    expert_out = jnp.einsum("fes,efd->esd", hidden, down_weight, preferred_element_type=F32)
    returned = lax.all_to_all(
        expert_out.astype(BF16), "ep", split_axis=1, concat_axis=0, tiled=True
    )
    combine_table = jnp.where(matches, table[EXPERTS:, None, :], 0.0).astype(BF16)
    mixed = lax.dot_general(
        combine_table.reshape(EXPERTS * CAP, tok_rows),
        returned.reshape(EXPERTS * CAP, local_width),
        TN,
        preferred_element_type=F32,
    )
    return mixed.astype(BF16)


def solution(mesh):
    placed = (
        P(("grp", "ep"), "tp"),
        P(("grp", "ep"), None),
        P(("grp", "ep"), None),
        P("ep", None, None, "tp"),
        P("ep", None, "tp"),
    )
    square = mesh.shape["ep"] == 4 and mesh.shape["tp"] == 4
    return jax.shard_map(
        local_square if square else local_general,
        mesh=mesh,
        in_specs=placed,
        out_specs=P(("grp", "ep"), "tp"),
        check_vma=False,
    )
```

```python
import functools

import jax
import jax.numpy as jnp
from jax import lax
from jax.experimental import pallas as pl
from jax.experimental.pallas import tpu as pltpu
from jax.sharding import PartitionSpec as P

EXPERTS = 32
TOPK = 6
CAP = 48
LANES = 128
BF16, F32 = jnp.bfloat16, jnp.float32
NT = (((1,), (1,)), ((), ()))
TN = (((0,), (0,)), ((), ()))
NN = (((1,), (0,)), ((), ()))

PAIR = [(0, 1), (1, 0), (2, 3), (3, 2)]
MIDDLE = [(1, 2), (2, 1)]
OUTWARD = [(1, 0), (2, 3)]
INWARD = [(0, 1), (3, 2)]
ACROSS_X = [(0, 2), (1, 3), (2, 0), (3, 1)]
ACROSS_CORE = [(0, 1), (1, 0), (2, 3), (3, 2)]


QUICK = pl.CostEstimate(flops=1024, bytes_accessed=1024, transcendentals=0)


SLOW = pl.CostEstimate(flops=20_000_000_000, bytes_accessed=1024, transcendentals=0)


def params(mib):
    return pltpu.CompilerParams(vmem_limit_bytes=mib << 20)


def route_kernel(ids_ref, gates_ref, out_ref):
    count = ids_ref.shape[1]
    expert = lax.broadcasted_iota(jnp.int32, (EXPERTS, count), 0)
    weight = jnp.zeros((EXPERTS, count), F32)
    chosen = jnp.zeros((EXPERTS, count), F32)
    for k in range(TOPK):
        hit = ids_ref[k : k + 1, :] == expert
        chosen = jnp.where(hit, 1.0, chosen)
        weight = jnp.where(hit, gates_ref[k : k + 1, :], weight)
    first = lax.broadcasted_iota(jnp.int32, (count, count), 0)
    second = lax.broadcasted_iota(jnp.int32, (count, count), 1)
    before = jnp.where(first < second, 1.0, 0.0).astype(BF16)
    position = lax.dot_general(chosen.astype(BF16), before, NN, preferred_element_type=F32)
    out_ref[:EXPERTS, :] = jnp.where(chosen > 0.0, position, -1.0)
    out_ref[EXPERTS:, :] = weight


def route(expert_ids, gate_weights):
    return pl.pallas_call(
        route_kernel,
        out_shape=jax.ShapeDtypeStruct((2 * EXPERTS, expert_ids.shape[0]), F32),
        name="route",
    )(expert_ids.T, gate_weights.T.astype(F32))


def place_kernel(experts, where_ref, *refs):
    *token_refs, table_ref, out_ref = refs
    count = table_ref.shape[1]
    slot_of = lax.broadcasted_iota(jnp.int32, (CAP, count), 0).astype(F32)
    table = [
        jnp.where(table_ref[pl.ds(where_ref[0] + e, 1), :] == slot_of, 1.0, 0.0)
        for e in range(experts)
    ]
    tokens = token_refs[0][...]
    for extra in token_refs[1:]:
        tokens = tokens + extra[...]
    table = jnp.concatenate(table, axis=0).astype(BF16)
    rows = lax.dot_general(table, tokens, NN, preferred_element_type=F32).astype(BF16)
    for e in range(experts):
        out_ref[e] = rows[e * CAP : (e + 1) * CAP]


def place(where, tokens, table, experts):
    whole = pl.BlockSpec(memory_space=pltpu.VMEM)
    return pl.pallas_call(
        functools.partial(place_kernel, experts),
        out_shape=jax.ShapeDtypeStruct((experts, CAP, tokens[0].shape[1]), BF16),
        in_specs=[pl.BlockSpec(memory_space=pltpu.SMEM)] + [whole] * (len(tokens) + 1),
        out_specs=whole,
        compiler_params=params(8),
        cost_estimate=QUICK,
        name="place",
    )(where, *tokens, table)


def gate_up_kernel(n_blocks, where_ref, *refs):
    row_refs = refs[:n_blocks]
    w_ref, _, send_ref, keep_ref, rows_ref, carry = refs[n_blocks:]
    step = pl.program_id(0)
    rows = n_blocks * CAP
    spare = 2 * LANES - rows
    x, core = where_ref[1], where_ref[2]
    quarter = w_ref.shape[1] // 4

    @pl.when(step == 0)
    def _():
        rows_ref[...] = jnp.zeros_like(rows_ref)

    def product(parity):
        for i in range(n_blocks):
            at = parity * spare + i * CAP
            rows_ref[parity, at : at + CAP, :] = row_refs[i][0]
        w = w_ref[0].reshape(8 * quarter, w_ref.shape[3])
        return lax.dot_general(w, rows_ref[parity], NT, preferred_element_type=F32)

    def store(tile, lane):
        tile = tile.astype(BF16)
        for q in range(4):
            piece = tile[2 * q * quarter : 2 * (q + 1) * quarter]
            at = jnp.where(x == q // 2, 1, 0)

            @pl.when(core == q % 2)
            def _():
                keep_ref[at, :, lane : lane + LANES] = piece

            @pl.when(core != q % 2)
            def _():
                send_ref[at, :, lane : lane + LANES] = piece

    @pl.when(lax.rem(step, 2) == 0)
    def _():
        out = product(0)
        store(out[:, :LANES], 0)
        carry[...] = out[:, LANES:]

    @pl.when(lax.rem(step, 2) == 1)
    def _():
        out = product(1)
        store(carry[...] + out[:, :LANES], LANES)
        store(out[:, LANES:], 2 * LANES)


def gate_up(where, placed, gu_weight, chunk, group, after):
    _, units, _, width = gu_weight.shape
    n_blocks = len(placed)
    lanes = 2 * n_blocks * CAP
    half = jax.ShapeDtypeStruct((2, units // 2, group // 2 * lanes), BF16)
    pair = pl.BlockSpec((2, units // 2, lanes), lambda i: (0, 0, i // 2))
    return pl.pallas_call(
        functools.partial(gate_up_kernel, n_blocks),
        grid=(group,),
        out_shape=(half, half),
        in_specs=[pl.BlockSpec(memory_space=pltpu.SMEM)]
        + [pl.BlockSpec((1, CAP, width), lambda i: (chunk * group + i, 0, 0))] * n_blocks
        + [pl.BlockSpec((1, units, 2, width), lambda i: (chunk * group + i, 0, 0, 0))]
        + [pl.BlockSpec(memory_space=pl.ANY)],
        out_specs=(pair, pair),
        scratch_shapes=[
            pltpu.VMEM((2, 2 * LANES, width), BF16),
            pltpu.VMEM((2 * units, LANES), F32),
        ],
        compiler_params=params(28),
        cost_estimate=QUICK,
        name="gate_up",
    )(where, *placed, gu_weight, after)


def hidden_kernel(keep_ref, near_ref, far_ref, _, out_ref, sums):
    units = out_ref.shape[1]
    for n in range(sums.shape[0]):
        lanes = slice(n * LANES, (n + 1) * LANES)
        total = keep_ref[0, :, lanes].astype(F32) + near_ref[0, :, lanes].astype(F32)
        sums[n] = total + far_ref[:, lanes].astype(F32)
        gate = sums[n, pl.ds(0, units, stride=2), :]
        up = sums[n, pl.ds(1, units, stride=2), :]
        out_ref[lanes, :] = (gate / (1.0 + jnp.exp(-gate)) * up).T.astype(BF16)


def hidden_quarter(keep, near, far, after):
    _, doubled, columns = keep.shape
    mine = pl.BlockSpec((1, doubled, columns), lambda i: (1, 0, 0))
    return pl.pallas_call(
        hidden_kernel,
        grid=(1,),
        out_shape=jax.ShapeDtypeStruct((columns, doubled // 2), BF16),
        in_specs=[
            mine,
            mine,
            pl.BlockSpec((doubled, columns), lambda i: (0, 0)),
            pl.BlockSpec(memory_space=pl.ANY),
        ],
        out_specs=pl.BlockSpec((columns, doubled // 2), lambda i: (0, 0)),
        scratch_shapes=[pltpu.VMEM((columns // LANES, doubled, LANES), F32)],
        compiler_params=params(10),
        cost_estimate=SLOW,
        name="hidden",
    )(keep, near, far, after)


def add_kernel(keep_ref, near_ref, _, out_ref):
    out_ref[...] = (keep_ref[0].astype(F32) + near_ref[0].astype(F32)).astype(BF16)


def chip_sum(keep, near, after):
    _, doubled, columns = keep.shape
    other = pl.BlockSpec((1, doubled, columns), lambda i: (0, 0, 0))
    return pl.pallas_call(
        add_kernel,
        grid=(1,),
        out_shape=jax.ShapeDtypeStruct((doubled, columns), BF16),
        in_specs=[other, other, pl.BlockSpec(memory_space=pl.ANY)],
        out_specs=pl.BlockSpec((doubled, columns), lambda i: (0, 0)),
        compiler_params=params(8),
        cost_estimate=QUICK,
        name="chip_sum",
    )(keep, near, after)


def down_kernel(group, n_blocks, chunk, has_carry, where_ref, *refs):
    hidden_refs, refs = refs[:4], refs[4:]
    route_refs, refs = refs[:n_blocks], refs[n_blocks:]
    w_hbm, refs = refs[0], refs[2:]
    carry_ref, refs = (refs[0], refs[1:]) if has_carry else (None, refs)
    out_refs, (held, w_buf, sems) = refs[:-3], refs[-3:]
    rows = n_blocks * CAP
    quarter = w_hbm.shape[1] // 4
    count = route_refs[0].shape[1]
    expert0 = where_ref[0]
    x, core = where_ref[1], where_ref[2]
    order = [(x, core), (1 - x, core), (x, 1 - core), (1 - x, 1 - core)]

    def fetch(e):
        copies = []
        for j in range(4):
            f0 = pl.multiple_of((order[j][0] * 2 + order[j][1]) * quarter, quarter)
            copies.append(
                pltpu.make_async_copy(
                    w_hbm.at[chunk * group + e, pl.ds(f0, quarter)],
                    w_buf.at[e, pl.ds(j * quarter, quarter)],
                    sems.at[e, j],
                )
            )
        return copies

    def start(e):
        for copy in fetch(e):
            copy.start()

    start(0)
    start(1)
    for e in range(group):
        for copy in fetch(e):
            copy.wait()
        if e + 2 < group:
            start(e + 2)
        units = jnp.concatenate([h[e * rows : (e + 1) * rows, :] for h in hidden_refs], axis=1)
        out = lax.dot_general(units, w_buf[e], NN, preferred_element_type=F32).astype(BF16)
        for i in range(n_blocks):
            held[i, e * CAP : (e + 1) * CAP, :] = out[i * CAP : (i + 1) * CAP]
    slot_of = lax.broadcasted_iota(jnp.int32, (CAP, count), 0).astype(F32)
    for i in range(n_blocks):
        table = [
            jnp.where(
                route_refs[i][pl.ds(expert0 + e, 1), :] == slot_of,
                route_refs[i][pl.ds(EXPERTS + expert0 + e, 1), :],
                0.0,
            )
            for e in range(group)
        ]
        table = jnp.concatenate(table, axis=0).astype(BF16)
        total = lax.dot_general(table, held[i], TN, preferred_element_type=F32)
        if has_carry:
            out_refs[i][...] = (total + carry_ref[i]).astype(BF16)
        else:
            out_refs[0][i] = total


def down(where, hidden, routes, down_weight, chunk, group, carry, after):
    n_blocks = len(routes)
    units = hidden[0].shape[1]
    count = routes[0].shape[1]
    width = down_weight.shape[2]
    whole = pl.BlockSpec(memory_space=pltpu.VMEM)
    carried = [] if carry is None else [carry]
    if carry is None:
        out_shape = (jax.ShapeDtypeStruct((n_blocks, count, width), F32),)
    else:
        out_shape = tuple(jax.ShapeDtypeStruct((count, width), BF16) for _ in routes)
    return pl.pallas_call(
        functools.partial(down_kernel, group, n_blocks, chunk, carry is not None),
        out_shape=out_shape,
        in_specs=[pl.BlockSpec(memory_space=pltpu.SMEM)]
        + [whole] * (4 + n_blocks)
        + [pl.BlockSpec(memory_space=pl.ANY)] * 2
        + [whole] * len(carried),
        out_specs=tuple(whole for _ in out_shape),
        scratch_shapes=[
            pltpu.VMEM((n_blocks, group * CAP, width), BF16),
            pltpu.VMEM((group, 4 * units, width), BF16),
            pltpu.SemaphoreType.DMA((group, 4)),
        ],
        compiler_params=params(28),
        cost_estimate=QUICK,
        name="down",
    )(where, *hidden, *routes, down_weight, after, *carried)


def hold_kernel(*_):
    pass


def hold(arrays, until):
    free = pl.BlockSpec(memory_space=pl.ANY)
    return pl.pallas_call(
        hold_kernel,
        out_shape=tuple(jax.ShapeDtypeStruct(a.shape, a.dtype) for a in arrays),
        in_specs=[free] * (len(arrays) + len(until)),
        out_specs=(free,) * len(arrays),
        input_output_aliases={i: i for i in range(len(arrays))},
        compiler_params=params(1),
        cost_estimate=QUICK,
        name="hold",
    )(*arrays, *until)


def plus_kernel(a_ref, b_ref, _, out_ref, __):
    out_ref[...] = (a_ref[...].astype(F32) + b_ref[...].astype(F32)).astype(BF16)


def plus_then(a, b, other):
    whole = pl.BlockSpec(memory_space=pltpu.VMEM)
    free = pl.BlockSpec(memory_space=pl.ANY)
    return pl.pallas_call(
        plus_kernel,
        out_shape=(jax.ShapeDtypeStruct(a.shape, a.dtype), jax.ShapeDtypeStruct(a.shape, a.dtype)),
        in_specs=[whole, whole, free],
        out_specs=(whole, free),
        input_output_aliases={2: 1},
        compiler_params=params(4),
        cost_estimate=QUICK,
        name="plus",
    )(a, b, other)


def local_square(tokens, expert_ids, gate_weights, gu_weight, down_weight):
    z, t = lax.axis_index("ep"), lax.axis_index("tp")
    x, core = t // 2, t % 2
    local = gu_weight.shape[0]
    group = local // 2
    wheres = [jnp.stack([z * local + n * group, x, core]).astype(jnp.int32) for n in range(2)]

    def hop(array, pairs):
        return lax.ppermute(array, "ep", pairs)

    neighbour = hop(tokens, PAIR)
    middle_1 = hop(tokens, MIDDLE)
    table = route(expert_ids, gate_weights)
    table_1 = hop(table, PAIR)
    table_2 = hop(table, [(i, i ^ 2) for i in range(4)])
    table_3 = hop(table, [(i, i ^ 3) for i in range(4)])
    neighbour, middle_1 = hold((neighbour, middle_1), (table_1, table_2, table_3))
    inner = (z == 1) | (z == 2)
    table_in = jnp.where(inner, table_3, table_2)
    table_out = jnp.where(inner, table_2, table_3)
    middle_2 = hop(neighbour, MIDDLE)
    end_1 = hop(middle_1, OUTWARD)
    end_2 = hop(middle_2, OUTWARD)

    tables = [table, table_1, table_in, table_out]
    blocks = [(tokens,), (neighbour,), (middle_1, end_1), (middle_2, end_2)]
    placed = [place(wheres[0], b, t, local) for b, t in zip(blocks, tables)]

    def sums(n, after):
        send, keep = gate_up(wheres[n], placed, gu_weight, n, group, after)
        return keep, lax.ppermute(send, "tp", ACROSS_CORE)

    def across(keep, near, after):
        total = chip_sum(keep, near, after)
        return total, lax.ppermute(total, "tp", ACROSS_X)

    def gathered(own):
        own_x = lax.ppermute(own, "tp", ACROSS_X)
        own_core = lax.ppermute(own, "tp", ACROSS_CORE)
        return own, own_x, own_core, lax.ppermute(own_x, "tp", ACROSS_CORE)

    keep_0, near_0 = sums(0, placed[3])
    turn, far_0 = across(keep_0, near_0, keep_0)
    keep_1, near_1 = sums(1, turn)
    own_0 = hidden_quarter(keep_0, near_0, far_0, keep_1)
    hidden_0 = gathered(own_0)
    turn, far_1 = across(keep_1, near_1, own_0)
    (carry,) = down(wheres[0], hidden_0, tables, down_weight, 0, group, None, turn)
    own_1 = hidden_quarter(keep_1, near_1, far_1, carry)
    hidden_1 = gathered(own_1)
    own, other, far_in, far_out = down(
        wheres[1], hidden_1, tables, down_weight, 1, group, carry, own_1
    )

    def plus(a, b):
        return (a.astype(F32) + b.astype(F32)).astype(BF16)

    out_inner = hop(far_out, INWARD)
    far_out, far_in = plus_then(far_out, out_inner, far_in)
    out_mid = hop(far_out, MIDDLE)
    in_inner = hop(far_in, INWARD)
    last = hop(plus(other, out_mid), PAIR)
    in_mid = hop(plus(far_in, in_inner), MIDDLE)
    return (own.astype(F32) + in_mid.astype(F32) + last.astype(F32)).astype(BF16)


def local_general(tokens, expert_ids, gate_weights, gu_weight, down_weight):
    tok_rows, local_width = tokens.shape
    table = route(expert_ids, gate_weights)
    slots = jnp.arange(CAP, dtype=jnp.int32).astype(F32)
    matches = table[:EXPERTS, None, :] == slots[None, :, None]
    dispatch_table = matches.astype(BF16).reshape(EXPERTS * CAP, tok_rows)
    outgoing = jnp.dot(dispatch_table, tokens, preferred_element_type=F32)
    outgoing = outgoing.astype(BF16).reshape(EXPERTS, CAP, local_width)
    received = lax.all_to_all(outgoing, "ep", split_axis=0, concat_axis=1, tiled=True)
    terms = jnp.einsum("efgd,esd->fegs", gu_weight, received, preferred_element_type=F32)
    totals = lax.psum(terms.astype(BF16), "tp").astype(F32)
    hidden = (jax.nn.silu(totals[:, :, 0]) * totals[:, :, 1]).astype(BF16)
    expert_out = jnp.einsum("fes,efd->esd", hidden, down_weight, preferred_element_type=F32)
    returned = lax.all_to_all(
        expert_out.astype(BF16), "ep", split_axis=1, concat_axis=0, tiled=True
    )
    combine_table = jnp.where(matches, table[EXPERTS:, None, :], 0.0).astype(BF16)
    mixed = lax.dot_general(
        combine_table.reshape(EXPERTS * CAP, tok_rows),
        returned.reshape(EXPERTS * CAP, local_width),
        TN,
        preferred_element_type=F32,
    )
    return mixed.astype(BF16)


def solution(mesh):
    placed = (
        P(("grp", "ep"), "tp"),
        P(("grp", "ep"), None),
        P(("grp", "ep"), None),
        P("ep", None, None, "tp"),
        P("ep", None, "tp"),
    )
    square = mesh.shape["ep"] == 4 and mesh.shape["tp"] == 4
    return jax.shard_map(
        local_square if square else local_general,
        mesh=mesh,
        in_specs=placed,
        out_specs=P(("grp", "ep"), "tp"),
        check_vma=False,
    )
```

```python
import functools

import jax
import jax.numpy as jnp
from jax import lax
from jax.experimental import pallas as pl
from jax.experimental.pallas import tpu as pltpu
from jax.sharding import PartitionSpec as P

EXPERTS = 32
TOPK = 6
CAP = 48
LANES = 128
BF16, F32 = jnp.bfloat16, jnp.float32
NT = (((1,), (1,)), ((), ()))
TN = (((0,), (0,)), ((), ()))
NN = (((1,), (0,)), ((), ()))

PAIR = [(0, 1), (1, 0), (2, 3), (3, 2)]
MIDDLE = [(1, 2), (2, 1)]
OUTWARD = [(1, 0), (2, 3)]
INWARD = [(0, 1), (3, 2)]
ACROSS_X = [(0, 2), (1, 3), (2, 0), (3, 1)]
ACROSS_CORE = [(0, 1), (1, 0), (2, 3), (3, 2)]


QUICK = pl.CostEstimate(flops=1024, bytes_accessed=1024, transcendentals=0)


SLOW = pl.CostEstimate(flops=20_000_000_000, bytes_accessed=1024, transcendentals=0)


def params(mib):
    return pltpu.CompilerParams(vmem_limit_bytes=mib << 20)


def route_kernel(ids_ref, gates_ref, out_ref):
    count = ids_ref.shape[1]
    expert = lax.broadcasted_iota(jnp.int32, (EXPERTS, count), 0)
    weight = jnp.zeros((EXPERTS, count), F32)
    chosen = jnp.zeros((EXPERTS, count), F32)
    for k in range(TOPK):
        hit = ids_ref[k : k + 1, :] == expert
        chosen = jnp.where(hit, 1.0, chosen)
        weight = jnp.where(hit, gates_ref[k : k + 1, :], weight)
    first = lax.broadcasted_iota(jnp.int32, (count, count), 0)
    second = lax.broadcasted_iota(jnp.int32, (count, count), 1)
    before = jnp.where(first < second, 1.0, 0.0).astype(BF16)
    position = lax.dot_general(chosen.astype(BF16), before, NN, preferred_element_type=F32)
    out_ref[:EXPERTS, :] = jnp.where(chosen > 0.0, position, -1.0)
    out_ref[EXPERTS:, :] = weight


def route(expert_ids, gate_weights):
    return pl.pallas_call(
        route_kernel,
        out_shape=jax.ShapeDtypeStruct((2 * EXPERTS, expert_ids.shape[0]), F32),
        name="route",
    )(expert_ids.T, gate_weights.T.astype(F32))


def place_kernel(experts, where_ref, *refs):
    *token_refs, table_ref, _, out_ref = refs
    count = table_ref.shape[1]
    slot_of = lax.broadcasted_iota(jnp.int32, (CAP, count), 0).astype(F32)
    table = [
        jnp.where(table_ref[pl.ds(where_ref[0] + e, 1), :] == slot_of, 1.0, 0.0)
        for e in range(experts)
    ]
    tokens = token_refs[0][...]
    for extra in token_refs[1:]:
        tokens = tokens + extra[...]
    table = jnp.concatenate(table, axis=0).astype(BF16)
    rows = lax.dot_general(table, tokens, NN, preferred_element_type=F32).astype(BF16)
    for e in range(experts):
        out_ref[e] = rows[e * CAP : (e + 1) * CAP]


def place(where, tokens, table, experts, after, cost):
    whole = pl.BlockSpec(memory_space=pltpu.VMEM)
    return pl.pallas_call(
        functools.partial(place_kernel, experts),
        out_shape=jax.ShapeDtypeStruct((experts, CAP, tokens[0].shape[1]), BF16),
        in_specs=[pl.BlockSpec(memory_space=pltpu.SMEM)]
        + [whole] * (len(tokens) + 1)
        + [pl.BlockSpec(memory_space=pl.ANY)],
        out_specs=whole,
        compiler_params=params(8),
        cost_estimate=cost,
        name="place",
    )(where, *tokens, table, after)


FOUR = 4


def gate_up_kernel(n_blocks, where_ref, *refs):
    row_refs = refs[:n_blocks]
    w_ref, send_ref, keep_ref, rows_ref, carry = refs[n_blocks], *refs[-4:]
    step = pl.program_id(0)
    rows = n_blocks * CAP
    x, core = where_ref[1], where_ref[2]
    quarter = w_ref.shape[1] // 4

    @pl.when(step == 0)
    def _():
        rows_ref[...] = jnp.zeros_like(rows_ref)

    def store(tile, lane):
        tile = tile.astype(BF16)
        for q in range(4):
            piece = tile[2 * q * quarter : 2 * (q + 1) * quarter]
            at = jnp.where(x == q // 2, 1, 0)

            @pl.when(core == q % 2)
            def _():
                keep_ref[at, :, lane : lane + LANES] = piece

            @pl.when(core != q % 2)
            def _():
                send_ref[at, :, lane : lane + LANES] = piece

    def one(e):
        first, last = e * rows // LANES, -(-(e + 1) * rows // LANES)
        for i in range(n_blocks):
            at = e * rows - first * LANES + i * CAP
            rows_ref[e, at : at + CAP, :] = row_refs[i][0]
        w = w_ref[0].reshape(8 * quarter, w_ref.shape[3])
        r = rows_ref[e, : (last - first) * LANES, :]
        out = lax.dot_general(w, r, NT, preferred_element_type=F32)
        for n in range(first, last):
            tile = out[:, (n - first) * LANES : (n - first + 1) * LANES]
            if n * LANES < e * rows:
                tile = tile + carry[...]
            if (n + 1) * LANES <= (e + 1) * rows:
                store(tile, n * LANES)
            else:
                carry[...] = tile

    for e in range(FOUR):
        pl.when(step == e)(functools.partial(one, e))


def gate_up(where, placed, gu_weight, chunk, after):
    _, units, _, width = gu_weight.shape
    n_blocks = len(placed)
    lanes = FOUR * n_blocks * CAP
    half = jax.ShapeDtypeStruct((2, units // 2, lanes), BF16)
    whole = pl.BlockSpec((2, units // 2, lanes), lambda i: (0, 0, 0))
    return pl.pallas_call(
        functools.partial(gate_up_kernel, n_blocks),
        grid=(FOUR,),
        out_shape=(half, half),
        in_specs=[pl.BlockSpec(memory_space=pltpu.SMEM)]
        + [pl.BlockSpec((1, CAP, width), lambda i: (chunk * FOUR + i, 0, 0))] * n_blocks
        + [pl.BlockSpec((1, units, 2, width), lambda i: (chunk * FOUR + i, 0, 0, 0))]
        + [pl.BlockSpec(memory_space=pl.ANY)] * len(after),
        out_specs=(whole, whole),
        scratch_shapes=[
            pltpu.VMEM((FOUR, 2 * LANES, width), BF16),
            pltpu.VMEM((2 * units, LANES), F32),
        ],
        compiler_params=params(28),
        cost_estimate=QUICK,
        name="gate_up",
    )(where, *placed, gu_weight, *after)


def hidden_kernel(parts, *refs):
    keep_refs, near_refs = refs[:parts], refs[parts : 2 * parts]
    far_ref, _, out_ref, sums = refs[2 * parts :]
    units = out_ref.shape[1]
    tiles = sums.shape[0] // parts
    for n in range(sums.shape[0]):
        part, lanes = n // tiles, slice(n % tiles * LANES, (n % tiles + 1) * LANES)
        whole = slice(n * LANES, (n + 1) * LANES)
        total = keep_refs[part][0, :, lanes].astype(F32) + near_refs[part][0, :, lanes].astype(F32)
        sums[n] = total + far_ref[:, whole].astype(F32)
        gate = sums[n, pl.ds(0, units, stride=2), :]
        up = sums[n, pl.ds(1, units, stride=2), :]
        out_ref[whole, :] = (gate / (1.0 + jnp.exp(-gate)) * up).T.astype(BF16)


def hidden_quarter(keep, near, far, after):
    _, doubled, lanes = keep[0].shape
    columns = lanes * len(keep)
    mine = pl.BlockSpec((1, doubled, lanes), lambda i: (1, 0, 0))
    return pl.pallas_call(
        functools.partial(hidden_kernel, len(keep)),
        grid=(1,),
        out_shape=jax.ShapeDtypeStruct((columns, doubled // 2), BF16),
        in_specs=[mine] * (2 * len(keep))
        + [pl.BlockSpec((doubled, columns), lambda i: (0, 0)), pl.BlockSpec(memory_space=pl.ANY)],
        out_specs=pl.BlockSpec((columns, doubled // 2), lambda i: (0, 0)),
        scratch_shapes=[pltpu.VMEM((columns // LANES, doubled, LANES), F32)],
        compiler_params=params(12),
        cost_estimate=SLOW,
        name="hidden",
    )(*keep, *near, far, after)


def add_kernel(parts, *refs):
    keep_refs, near_refs, out_ref = refs[:parts], refs[parts : 2 * parts], refs[-1]
    lanes = keep_refs[0].shape[2]
    for n in range(parts):
        total = keep_refs[n][0].astype(F32) + near_refs[n][0].astype(F32)
        out_ref[:, n * lanes : (n + 1) * lanes] = total.astype(BF16)


def chip_sum(keep, near, after):
    _, doubled, lanes = keep[0].shape
    columns = lanes * len(keep)
    other = pl.BlockSpec((1, doubled, lanes), lambda i: (0, 0, 0))
    return pl.pallas_call(
        functools.partial(add_kernel, len(keep)),
        grid=(1,),
        out_shape=jax.ShapeDtypeStruct((doubled, columns), BF16),
        in_specs=[other] * (2 * len(keep)) + [pl.BlockSpec(memory_space=pl.ANY)],
        out_specs=pl.BlockSpec((doubled, columns), lambda i: (0, 0)),
        compiler_params=params(10),
        cost_estimate=QUICK,
        name="chip_sum",
    )(*keep, *near, after)


SLOTS = 3


def down_kernel(experts, n_blocks, n_after, where_ref, *refs):
    hidden_refs, route_refs = refs[:4], refs[4 : 4 + n_blocks]
    w_hbm = refs[4 + n_blocks]
    out_refs = refs[5 + n_blocks + n_after : -3]
    held, w_buf, sems = refs[-3:]
    rows = n_blocks * CAP
    quarter = w_hbm.shape[1] // 4
    count = route_refs[0].shape[1]
    expert0 = where_ref[0]
    x, core = where_ref[1], where_ref[2]
    order = [(x, core), (1 - x, core), (x, 1 - core), (1 - x, 1 - core)]

    def fetch(e):
        copies = []
        for j in range(4):
            f0 = pl.multiple_of((order[j][0] * 2 + order[j][1]) * quarter, quarter)
            copies.append(
                pltpu.make_async_copy(
                    w_hbm.at[e, pl.ds(f0, quarter)],
                    w_buf.at[e % SLOTS, pl.ds(j * quarter, quarter)],
                    sems.at[e % SLOTS, j],
                )
            )
        return copies

    def start(e):
        for copy in fetch(e):
            copy.start()

    for e in range(SLOTS - 1):
        start(e)
    for e in range(experts):
        for copy in fetch(e):
            copy.wait()
        if e + SLOTS - 1 < experts:
            start(e + SLOTS - 1)
        units = jnp.concatenate([h[e * rows : (e + 1) * rows, :] for h in hidden_refs], axis=1)
        out = lax.dot_general(units, w_buf[e % SLOTS], NN, preferred_element_type=F32).astype(BF16)
        for i in range(n_blocks):
            held[i, e * CAP : (e + 1) * CAP, :] = out[i * CAP : (i + 1) * CAP]
    slot_of = lax.broadcasted_iota(jnp.int32, (CAP, count), 0).astype(F32)
    for i in range(n_blocks):
        table = [
            jnp.where(
                route_refs[i][pl.ds(expert0 + e, 1), :] == slot_of,
                route_refs[i][pl.ds(EXPERTS + expert0 + e, 1), :],
                0.0,
            )
            for e in range(experts)
        ]
        table = jnp.concatenate(table, axis=0).astype(BF16)
        total = lax.dot_general(table, held[i], TN, preferred_element_type=F32)
        out_refs[i][...] = total.astype(BF16)


def down(where, hidden, routes, down_weight, after):
    n_blocks = len(routes)
    count = routes[0].shape[1]
    experts, units, width = down_weight.shape
    whole = pl.BlockSpec(memory_space=pltpu.VMEM)
    return pl.pallas_call(
        functools.partial(down_kernel, experts, n_blocks, len(after)),
        out_shape=tuple(jax.ShapeDtypeStruct((count, width), BF16) for _ in routes),
        in_specs=[pl.BlockSpec(memory_space=pltpu.SMEM)]
        + [whole] * (4 + n_blocks)
        + [pl.BlockSpec(memory_space=pl.ANY)] * (1 + len(after)),
        out_specs=tuple(whole for _ in routes),
        scratch_shapes=[
            pltpu.VMEM((n_blocks, experts * CAP, width), BF16),
            pltpu.VMEM((SLOTS, units, width), BF16),
            pltpu.SemaphoreType.DMA((SLOTS, 4)),
        ],
        compiler_params=params(24),
        cost_estimate=QUICK,
        name="down",
    )(where, *hidden, *routes, down_weight, *after)


def hold_kernel(*_):
    pass


def hold(arrays, until):
    free = pl.BlockSpec(memory_space=pl.ANY)
    return pl.pallas_call(
        hold_kernel,
        out_shape=tuple(jax.ShapeDtypeStruct(a.shape, a.dtype) for a in arrays),
        in_specs=[free] * (len(arrays) + len(until)),
        out_specs=(free,) * len(arrays),
        input_output_aliases={i: i for i in range(len(arrays))},
        compiler_params=params(1),
        cost_estimate=QUICK,
        name="hold",
    )(*arrays, *until)


def plus_kernel(a_ref, b_ref, _, out_ref, __):
    out_ref[...] = (a_ref[...].astype(F32) + b_ref[...].astype(F32)).astype(BF16)


def plus_then(a, b, other):
    whole = pl.BlockSpec(memory_space=pltpu.VMEM)
    free = pl.BlockSpec(memory_space=pl.ANY)
    return pl.pallas_call(
        plus_kernel,
        out_shape=(jax.ShapeDtypeStruct(a.shape, a.dtype), jax.ShapeDtypeStruct(a.shape, a.dtype)),
        in_specs=[whole, whole, free],
        out_specs=(whole, free),
        input_output_aliases={2: 1},
        compiler_params=params(4),
        cost_estimate=QUICK,
        name="plus",
    )(a, b, other)


def local_square(tokens, expert_ids, gate_weights, gu_weight, down_weight):
    z, t = lax.axis_index("ep"), lax.axis_index("tp")
    x, core = t // 2, t % 2
    local = gu_weight.shape[0]
    where = jnp.stack([z * local, x, core]).astype(jnp.int32)

    def hop(array, pairs):
        return lax.ppermute(array, "ep", pairs)

    neighbour = hop(tokens, PAIR)
    middle_1 = hop(tokens, MIDDLE)
    table = route(expert_ids, gate_weights)
    table_1 = hop(table, PAIR)
    table_2 = hop(table, [(i, i ^ 2) for i in range(4)])
    table_3 = hop(table, [(i, i ^ 3) for i in range(4)])
    inner = (z == 1) | (z == 2)
    table_in = jnp.where(inner, table_3, table_2)
    table_out = jnp.where(inner, table_2, table_3)
    near_tables, far_tables = [table, table_1], [table_in, table_out]
    placed_own = place(where, (tokens,), table, local, table, QUICK)
    neighbour, middle_1 = hold((neighbour, middle_1), (table_1, placed_own))
    middle_2 = hop(neighbour, MIDDLE)
    end_1 = hop(middle_1, OUTWARD)

    def across(keep, near, after):
        total = chip_sum(keep, near, after)
        return total, lax.ppermute(total, "tp", ACROSS_X)

    def sums(placed, chunk, after):
        send, keep = gate_up(where, placed, gu_weight, chunk, after)
        return keep, lax.ppermute(send, "tp", ACROSS_CORE)

    def gathered(own):
        own_x = lax.ppermute(own, "tp", ACROSS_X)
        own_core = lax.ppermute(own, "tp", ACROSS_CORE)
        return own, own_x, own_core, lax.ppermute(own_x, "tp", ACROSS_CORE)

    placed_next = place(where, (neighbour,), table_1, local, placed_own, QUICK)
    close = [placed_own, placed_next]
    keep_0, near_0 = sums(close, 0, [])
    (middle_2,) = hold((middle_2,), (keep_0, table_2, table_3))
    end_2 = hop(middle_2, OUTWARD)
    keep_1, near_1 = sums(close, 1, [middle_2])
    keep_a, near_a = [keep_0, keep_1], [near_0, near_1]
    placed_in = place(where, (middle_1, end_1), table_in, local, keep_a[-1], QUICK)
    placed_out = place(where, (middle_2, end_2), table_out, local, placed_in, SLOW)
    total_a, far_a = across(keep_a, near_a, placed_out)
    away = [placed_in, placed_out]
    keep_2, near_2 = sums(away, 0, [total_a])
    keep_3, near_3 = sums(away, 1, [keep_2])
    keep_b, near_b = [keep_2, keep_3], [near_2, near_3]
    own_a = hidden_quarter(keep_a, near_a, far_a, keep_b[-1])
    hidden_a = gathered(own_a)
    total_b, far_b = across(keep_b, near_b, own_a)
    own, other = down(where, hidden_a, near_tables, down_weight, (total_b,))
    from_next = hop(other, PAIR)
    own_b = hidden_quarter(keep_b, near_b, far_b, own)
    hidden_b = gathered(own_b)
    far_in, far_out = down(where, hidden_b, far_tables, down_weight, (own_b, from_next))

    def plus(a, b):
        return (a.astype(F32) + b.astype(F32)).astype(BF16)

    out_inner = hop(far_out, INWARD)
    far_out, far_in = plus_then(far_out, out_inner, far_in)
    out_mid = hop(far_out, MIDDLE)
    in_inner = hop(far_in, INWARD)
    last = hop(out_mid, OUTWARD)
    in_mid = hop(plus(far_in, in_inner), MIDDLE)
    near_sum = own.astype(F32) + from_next.astype(F32)
    return (near_sum + in_mid.astype(F32) + last.astype(F32)).astype(BF16)


def local_general(tokens, expert_ids, gate_weights, gu_weight, down_weight):
    tok_rows, local_width = tokens.shape
    table = route(expert_ids, gate_weights)
    slots = jnp.arange(CAP, dtype=jnp.int32).astype(F32)
    matches = table[:EXPERTS, None, :] == slots[None, :, None]
    dispatch_table = matches.astype(BF16).reshape(EXPERTS * CAP, tok_rows)
    outgoing = jnp.dot(dispatch_table, tokens, preferred_element_type=F32)
    outgoing = outgoing.astype(BF16).reshape(EXPERTS, CAP, local_width)
    received = lax.all_to_all(outgoing, "ep", split_axis=0, concat_axis=1, tiled=True)
    terms = jnp.einsum("efgd,esd->fegs", gu_weight, received, preferred_element_type=F32)
    totals = lax.psum(terms.astype(BF16), "tp").astype(F32)
    hidden = (jax.nn.silu(totals[:, :, 0]) * totals[:, :, 1]).astype(BF16)
    expert_out = jnp.einsum("fes,efd->esd", hidden, down_weight, preferred_element_type=F32)
    returned = lax.all_to_all(
        expert_out.astype(BF16), "ep", split_axis=1, concat_axis=0, tiled=True
    )
    combine_table = jnp.where(matches, table[EXPERTS:, None, :], 0.0).astype(BF16)
    mixed = lax.dot_general(
        combine_table.reshape(EXPERTS * CAP, tok_rows),
        returned.reshape(EXPERTS * CAP, local_width),
        TN,
        preferred_element_type=F32,
    )
    return mixed.astype(BF16)


def solution(mesh):
    placed = (
        P(("grp", "ep"), "tp"),
        P(("grp", "ep"), None),
        P(("grp", "ep"), None),
        P("ep", None, None, "tp"),
        P("ep", None, "tp"),
    )
    square = mesh.shape["ep"] == 4 and mesh.shape["tp"] == 4
    return jax.shard_map(
        local_square if square else local_general,
        mesh=mesh,
        in_specs=placed,
        out_specs=P(("grp", "ep"), "tp"),
        check_vma=False,
    )
```

```python
import functools

import jax
import jax.numpy as jnp
from jax import lax
from jax.experimental import pallas as pl
from jax.experimental.pallas import tpu as pltpu
from jax.sharding import PartitionSpec as P

EXPERTS = 32
TOPK = 6
CAP = 48
LANES = 128
BF16, F32 = jnp.bfloat16, jnp.float32
NT = (((1,), (1,)), ((), ()))
TN = (((0,), (0,)), ((), ()))
NN = (((1,), (0,)), ((), ()))

PAIR = [(0, 1), (1, 0), (2, 3), (3, 2)]
MIDDLE = [(1, 2), (2, 1)]
OUTWARD = [(1, 0), (2, 3)]
INWARD = [(0, 1), (3, 2)]
ACROSS_X = [(0, 2), (1, 3), (2, 0), (3, 1)]
ACROSS_CORE = [(0, 1), (1, 0), (2, 3), (3, 2)]


QUICK = pl.CostEstimate(flops=1024, bytes_accessed=1024, transcendentals=0)


SLOW = pl.CostEstimate(flops=20_000_000_000, bytes_accessed=1024, transcendentals=0)


def params(mib):
    return pltpu.CompilerParams(vmem_limit_bytes=mib << 20)


def route_kernel(ids_ref, gates_ref, out_ref):
    count = ids_ref.shape[1]
    expert = lax.broadcasted_iota(jnp.int32, (EXPERTS, count), 0)
    weight = jnp.zeros((EXPERTS, count), F32)
    chosen = jnp.zeros((EXPERTS, count), F32)
    for k in range(TOPK):
        hit = ids_ref[k : k + 1, :] == expert
        chosen = jnp.where(hit, 1.0, chosen)
        weight = jnp.where(hit, gates_ref[k : k + 1, :], weight)
    first = lax.broadcasted_iota(jnp.int32, (count, count), 0)
    second = lax.broadcasted_iota(jnp.int32, (count, count), 1)
    before = jnp.where(first < second, 1.0, 0.0).astype(BF16)
    position = lax.dot_general(chosen.astype(BF16), before, NN, preferred_element_type=F32)
    out_ref[:EXPERTS, :] = jnp.where(chosen > 0.0, position, -1.0)
    out_ref[EXPERTS:, :] = weight


def route(expert_ids, gate_weights):
    return pl.pallas_call(
        route_kernel,
        out_shape=jax.ShapeDtypeStruct((2 * EXPERTS, expert_ids.shape[0]), F32),
        name="route",
    )(expert_ids.T, gate_weights.T.astype(F32))


def place_kernel(experts, where_ref, *refs):
    *token_refs, table_ref, out_ref = refs
    count = table_ref.shape[1]
    slot_of = lax.broadcasted_iota(jnp.int32, (CAP, count), 0).astype(F32)
    table = [
        jnp.where(table_ref[pl.ds(where_ref[0] + e, 1), :] == slot_of, 1.0, 0.0)
        for e in range(experts)
    ]
    tokens = token_refs[0][...]
    for extra in token_refs[1:]:
        tokens = tokens + extra[...]
    table = jnp.concatenate(table, axis=0).astype(BF16)
    rows = lax.dot_general(table, tokens, NN, preferred_element_type=F32).astype(BF16)
    for e in range(experts):
        out_ref[e] = rows[e * CAP : (e + 1) * CAP]


def place(where, tokens, table, experts):
    whole = pl.BlockSpec(memory_space=pltpu.VMEM)
    return pl.pallas_call(
        functools.partial(place_kernel, experts),
        out_shape=jax.ShapeDtypeStruct((experts, CAP, tokens[0].shape[1]), BF16),
        in_specs=[pl.BlockSpec(memory_space=pltpu.SMEM)] + [whole] * (len(tokens) + 1),
        out_specs=whole,
        compiler_params=params(8),
        cost_estimate=QUICK,
        name="place",
    )(where, *tokens, table)


def gate_up_kernel(n_blocks, where_ref, *refs):
    row_refs = refs[:n_blocks]
    w_ref, _, send_ref, keep_ref, rows_ref, carry = refs[n_blocks:]
    step = pl.program_id(0)
    rows = n_blocks * CAP
    spare = 2 * LANES - rows
    x, core = where_ref[1], where_ref[2]
    quarter = w_ref.shape[1] // 4

    @pl.when(step == 0)
    def _():
        rows_ref[...] = jnp.zeros_like(rows_ref)

    def product(parity):
        for i in range(n_blocks):
            at = parity * spare + i * CAP
            rows_ref[parity, at : at + CAP, :] = row_refs[i][0]
        w = w_ref[0].reshape(8 * quarter, w_ref.shape[3])
        return lax.dot_general(w, rows_ref[parity], NT, preferred_element_type=F32)

    def store(tile, lane):
        tile = tile.astype(BF16)
        for q in range(4):
            piece = tile[2 * q * quarter : 2 * (q + 1) * quarter]
            at = jnp.where(x == q // 2, 1, 0)

            @pl.when(core == q % 2)
            def _():
                keep_ref[at, :, lane : lane + LANES] = piece

            @pl.when(core != q % 2)
            def _():
                send_ref[at, :, lane : lane + LANES] = piece

    @pl.when(lax.rem(step, 2) == 0)
    def _():
        out = product(0)
        store(out[:, :LANES], 0)
        carry[...] = out[:, LANES:]

    @pl.when(lax.rem(step, 2) == 1)
    def _():
        out = product(1)
        store(carry[...] + out[:, :LANES], LANES)
        store(out[:, LANES:], 2 * LANES)


def gate_up(where, placed, gu_weight, start, group, after):
    _, units, _, width = gu_weight.shape
    n_blocks = len(placed)
    lanes = 2 * n_blocks * CAP
    half = jax.ShapeDtypeStruct((2, units // 2, group // 2 * lanes), BF16)
    pair = pl.BlockSpec((2, units // 2, lanes), lambda i: (0, 0, i // 2))
    return pl.pallas_call(
        functools.partial(gate_up_kernel, n_blocks),
        grid=(group,),
        out_shape=(half, half),
        in_specs=[pl.BlockSpec(memory_space=pltpu.SMEM)]
        + [pl.BlockSpec((1, CAP, width), lambda i: (start + i, 0, 0))] * n_blocks
        + [pl.BlockSpec((1, units, 2, width), lambda i: (start + i, 0, 0, 0))]
        + [pl.BlockSpec(memory_space=pl.ANY)],
        out_specs=(pair, pair),
        scratch_shapes=[
            pltpu.VMEM((2, 2 * LANES, width), BF16),
            pltpu.VMEM((2 * units, LANES), F32),
        ],
        compiler_params=params(28),
        cost_estimate=QUICK,
        name="gate_up",
    )(where, *placed, gu_weight, after)


def hidden_kernel(keep_ref, near_ref, far_ref, _, out_ref, sums):
    units = out_ref.shape[1]
    for n in range(sums.shape[0]):
        lanes = slice(n * LANES, (n + 1) * LANES)
        total = keep_ref[0, :, lanes].astype(F32) + near_ref[0, :, lanes].astype(F32)
        sums[n] = total + far_ref[:, lanes].astype(F32)
        gate = sums[n, pl.ds(0, units, stride=2), :]
        up = sums[n, pl.ds(1, units, stride=2), :]
        out_ref[lanes, :] = (gate / (1.0 + jnp.exp(-gate)) * up).T.astype(BF16)


def hidden_quarter(keep, near, far, after):
    _, doubled, columns = keep.shape
    mine = pl.BlockSpec((1, doubled, columns), lambda i: (1, 0, 0))
    return pl.pallas_call(
        hidden_kernel,
        grid=(1,),
        out_shape=jax.ShapeDtypeStruct((columns, doubled // 2), BF16),
        in_specs=[
            mine,
            mine,
            pl.BlockSpec((doubled, columns), lambda i: (0, 0)),
            pl.BlockSpec(memory_space=pl.ANY),
        ],
        out_specs=pl.BlockSpec((columns, doubled // 2), lambda i: (0, 0)),
        scratch_shapes=[pltpu.VMEM((columns // LANES, doubled, LANES), F32)],
        compiler_params=params(10),
        cost_estimate=SLOW,
        name="hidden",
    )(keep, near, far, after)


def add_kernel(keep_ref, near_ref, _, out_ref):
    out_ref[...] = (keep_ref[0].astype(F32) + near_ref[0].astype(F32)).astype(BF16)


def chip_sum(keep, near, after):
    _, doubled, columns = keep.shape
    other = pl.BlockSpec((1, doubled, columns), lambda i: (0, 0, 0))
    return pl.pallas_call(
        add_kernel,
        grid=(1,),
        out_shape=jax.ShapeDtypeStruct((doubled, columns), BF16),
        in_specs=[other, other, pl.BlockSpec(memory_space=pl.ANY)],
        out_specs=pl.BlockSpec((doubled, columns), lambda i: (0, 0)),
        compiler_params=params(8),
        cost_estimate=QUICK,
        name="chip_sum",
    )(keep, near, after)


def down_kernel(group, n_blocks, first, has_carry, final, where_ref, *refs):
    hidden_refs, refs = refs[:4], refs[4:]
    route_refs, refs = refs[:n_blocks], refs[n_blocks:]
    w_hbm, refs = refs[0], refs[2:]
    carry_ref, refs = (refs[0], refs[1:]) if has_carry else (None, refs)
    out_refs, (held, w_buf, sems) = refs[:-3], refs[-3:]
    rows = n_blocks * CAP
    quarter = w_hbm.shape[1] // 4
    count = route_refs[0].shape[1]
    expert0 = where_ref[0]
    x, core = where_ref[1], where_ref[2]
    order = [(x, core), (1 - x, core), (x, 1 - core), (1 - x, 1 - core)]

    def fetch(e):
        copies = []
        for j in range(4):
            f0 = pl.multiple_of((order[j][0] * 2 + order[j][1]) * quarter, quarter)
            copies.append(
                pltpu.make_async_copy(
                    w_hbm.at[first + e, pl.ds(f0, quarter)],
                    w_buf.at[e, pl.ds(j * quarter, quarter)],
                    sems.at[e, j],
                )
            )
        return copies

    def start(e):
        for copy in fetch(e):
            copy.start()

    for e in range(min(2, group)):
        start(e)
    for e in range(group):
        for copy in fetch(e):
            copy.wait()
        if e + 2 < group:
            start(e + 2)
        units = jnp.concatenate([h[e * rows : (e + 1) * rows, :] for h in hidden_refs], axis=1)
        out = lax.dot_general(units, w_buf[e], NN, preferred_element_type=F32).astype(BF16)
        for i in range(n_blocks):
            held[i, e * CAP : (e + 1) * CAP, :] = out[i * CAP : (i + 1) * CAP]
    slot_of = lax.broadcasted_iota(jnp.int32, (CAP, count), 0).astype(F32)
    for i in range(n_blocks):
        table = [
            jnp.where(
                route_refs[i][pl.ds(expert0 + e, 1), :] == slot_of,
                route_refs[i][pl.ds(EXPERTS + expert0 + e, 1), :],
                0.0,
            )
            for e in range(group)
        ]
        table = jnp.concatenate(table, axis=0).astype(BF16)
        total = lax.dot_general(table, held[i], TN, preferred_element_type=F32)
        if has_carry:
            total = total + carry_ref[i]
        if final:
            out_refs[i][...] = total.astype(BF16)
        else:
            out_refs[0][i] = total


def down(where, hidden, routes, down_weight, first, group, carry, after):
    n_blocks = len(routes)
    units = hidden[0].shape[1]
    count = routes[0].shape[1]
    width = down_weight.shape[2]
    whole = pl.BlockSpec(memory_space=pltpu.VMEM)
    carried = [] if carry is None else [carry]
    final = first + group == down_weight.shape[0]
    if not final:
        out_shape = (jax.ShapeDtypeStruct((n_blocks, count, width), F32),)
    else:
        out_shape = tuple(jax.ShapeDtypeStruct((count, width), BF16) for _ in routes)
    return pl.pallas_call(
        functools.partial(down_kernel, group, n_blocks, first, carry is not None, final),
        out_shape=out_shape,
        in_specs=[pl.BlockSpec(memory_space=pltpu.SMEM)]
        + [whole] * (4 + n_blocks)
        + [pl.BlockSpec(memory_space=pl.ANY)] * 2
        + [whole] * len(carried),
        out_specs=tuple(whole for _ in out_shape),
        scratch_shapes=[
            pltpu.VMEM((n_blocks, group * CAP, width), BF16),
            pltpu.VMEM((group, 4 * units, width), BF16),
            pltpu.SemaphoreType.DMA((group, 4)),
        ],
        compiler_params=params(28),
        cost_estimate=QUICK,
        name="down",
    )(where, *hidden, *routes, down_weight, after, *carried)


def hold_kernel(*_):
    pass


def hold(arrays, until):
    free = pl.BlockSpec(memory_space=pl.ANY)
    return pl.pallas_call(
        hold_kernel,
        out_shape=tuple(jax.ShapeDtypeStruct(a.shape, a.dtype) for a in arrays),
        in_specs=[free] * (len(arrays) + len(until)),
        out_specs=(free,) * len(arrays),
        input_output_aliases={i: i for i in range(len(arrays))},
        compiler_params=params(1),
        cost_estimate=QUICK,
        name="hold",
    )(*arrays, *until)


def plus_kernel(a_ref, b_ref, _, out_ref, __):
    out_ref[...] = (a_ref[...].astype(F32) + b_ref[...].astype(F32)).astype(BF16)


def plus_then(a, b, other):
    whole = pl.BlockSpec(memory_space=pltpu.VMEM)
    free = pl.BlockSpec(memory_space=pl.ANY)
    return pl.pallas_call(
        plus_kernel,
        out_shape=(jax.ShapeDtypeStruct(a.shape, a.dtype), jax.ShapeDtypeStruct(a.shape, a.dtype)),
        in_specs=[whole, whole, free],
        out_specs=(whole, free),
        input_output_aliases={2: 1},
        compiler_params=params(4),
        cost_estimate=QUICK,
        name="plus",
    )(a, b, other)


def local_square(tokens, expert_ids, gate_weights, gu_weight, down_weight):
    z, t = lax.axis_index("ep"), lax.axis_index("tp")
    x, core = t // 2, t % 2
    local = gu_weight.shape[0]
    groups = [(0, local // 4), (local // 4, local // 2), (local * 3 // 4, local // 4)]
    wheres = [jnp.stack([z * local + first, x, core]).astype(jnp.int32) for first, _ in groups]

    def hop(array, pairs):
        return lax.ppermute(array, "ep", pairs)

    neighbour = hop(tokens, PAIR)
    middle_1 = hop(tokens, MIDDLE)
    table = route(expert_ids, gate_weights)
    table_1 = hop(table, PAIR)
    table_2 = hop(table, [(i, i ^ 2) for i in range(4)])
    table_3 = hop(table, [(i, i ^ 3) for i in range(4)])
    placed = [place(wheres[0], (tokens,), table, local)]
    neighbour, middle_1 = hold((neighbour, middle_1), placed)
    inner = (z == 1) | (z == 2)
    table_in = jnp.where(inner, table_3, table_2)
    table_out = jnp.where(inner, table_2, table_3)
    middle_2 = hop(neighbour, MIDDLE)
    end_1 = hop(middle_1, OUTWARD)
    (middle_2,) = hold((middle_2,), (table_1, table_2, table_3))
    end_2 = hop(middle_2, OUTWARD)
    tables = [table, table_1, table_in, table_out]
    blocks = [(neighbour,), (middle_1, end_1), (middle_2, end_2)]
    placed += [place(wheres[0], b, t, local) for b, t in zip(blocks, tables[1:])]

    def sums(n, after):
        send, keep = gate_up(wheres[n], placed, gu_weight, *groups[n], after)
        return keep, lax.ppermute(send, "tp", ACROSS_CORE)

    def across(keep, near, after):
        total = chip_sum(keep, near, after)
        return total, lax.ppermute(total, "tp", ACROSS_X)

    def gathered(own):
        own_x = lax.ppermute(own, "tp", ACROSS_X)
        own_core = lax.ppermute(own, "tp", ACROSS_CORE)
        return own, own_x, own_core, lax.ppermute(own_x, "tp", ACROSS_CORE)

    def outputs(n, hidden, carry, after):
        return down(wheres[n], hidden, tables, down_weight, *groups[n], carry, after)

    keep_0, near_0 = sums(0, placed[3])
    turn, far_0 = across(keep_0, near_0, keep_0)
    keep_1, near_1 = sums(1, turn)
    own_0 = hidden_quarter(keep_0, near_0, far_0, keep_1)
    hidden_0 = gathered(own_0)
    turn, far_1 = across(keep_1, near_1, own_0)
    keep_2, near_2 = sums(2, turn)
    (carry,) = outputs(0, hidden_0, None, keep_2)
    own_1 = hidden_quarter(keep_1, near_1, far_1, carry)
    hidden_1 = gathered(own_1)
    turn, far_2 = across(keep_2, near_2, own_1)
    (carry,) = outputs(1, hidden_1, carry, turn)
    own_2 = hidden_quarter(keep_2, near_2, far_2, carry)
    own, other, far_in, far_out = outputs(2, gathered(own_2), carry, own_2)

    def plus(a, b):
        return (a.astype(F32) + b.astype(F32)).astype(BF16)

    out_inner = hop(far_out, INWARD)
    far_out, far_in = plus_then(far_out, out_inner, far_in)
    out_mid = hop(far_out, MIDDLE)
    in_inner = hop(far_in, INWARD)
    last = hop(plus(other, out_mid), PAIR)
    in_mid = hop(plus(far_in, in_inner), MIDDLE)
    return (own.astype(F32) + in_mid.astype(F32) + last.astype(F32)).astype(BF16)


def local_general(tokens, expert_ids, gate_weights, gu_weight, down_weight):
    tok_rows, local_width = tokens.shape
    table = route(expert_ids, gate_weights)
    slots = jnp.arange(CAP, dtype=jnp.int32).astype(F32)
    matches = table[:EXPERTS, None, :] == slots[None, :, None]
    dispatch_table = matches.astype(BF16).reshape(EXPERTS * CAP, tok_rows)
    outgoing = jnp.dot(dispatch_table, tokens, preferred_element_type=F32)
    outgoing = outgoing.astype(BF16).reshape(EXPERTS, CAP, local_width)
    received = lax.all_to_all(outgoing, "ep", split_axis=0, concat_axis=1, tiled=True)
    terms = jnp.einsum("efgd,esd->fegs", gu_weight, received, preferred_element_type=F32)
    totals = lax.psum(terms.astype(BF16), "tp").astype(F32)
    hidden = (jax.nn.silu(totals[:, :, 0]) * totals[:, :, 1]).astype(BF16)
    expert_out = jnp.einsum("fes,efd->esd", hidden, down_weight, preferred_element_type=F32)
    returned = lax.all_to_all(
        expert_out.astype(BF16), "ep", split_axis=1, concat_axis=0, tiled=True
    )
    combine_table = jnp.where(matches, table[EXPERTS:, None, :], 0.0).astype(BF16)
    mixed = lax.dot_general(
        combine_table.reshape(EXPERTS * CAP, tok_rows),
        returned.reshape(EXPERTS * CAP, local_width),
        TN,
        preferred_element_type=F32,
    )
    return mixed.astype(BF16)


def solution(mesh):
    placed = (
        P(("grp", "ep"), "tp"),
        P(("grp", "ep"), None),
        P(("grp", "ep"), None),
        P("ep", None, None, "tp"),
        P("ep", None, "tp"),
    )
    square = mesh.shape["ep"] == 4 and mesh.shape["tp"] == 4
    return jax.shard_map(
        local_square if square else local_general,
        mesh=mesh,
        in_specs=placed,
        out_specs=P(("grp", "ep"), "tp"),
        check_vma=False,
    )
```

```python
import functools

import jax
import jax.numpy as jnp
from jax import lax
from jax.experimental import pallas as pl
from jax.experimental.pallas import tpu as pltpu
from jax.sharding import PartitionSpec as P

EXPERTS = 32
TOPK = 6
CAP = 48
LANES = 128
BF16, F32 = jnp.bfloat16, jnp.float32
NT = (((1,), (1,)), ((), ()))
TN = (((0,), (0,)), ((), ()))
NN = (((1,), (0,)), ((), ()))

PAIR = [(0, 1), (1, 0), (2, 3), (3, 2)]
MIDDLE = [(1, 2), (2, 1)]
OUTWARD = [(1, 0), (2, 3)]
INWARD = [(0, 1), (3, 2)]
ACROSS_X = [(0, 2), (1, 3), (2, 0), (3, 1)]
ACROSS_CORE = [(0, 1), (1, 0), (2, 3), (3, 2)]


QUICK = pl.CostEstimate(flops=1024, bytes_accessed=1024, transcendentals=0)


SLOW = pl.CostEstimate(flops=20_000_000_000, bytes_accessed=1024, transcendentals=0)


def params(mib):
    return pltpu.CompilerParams(vmem_limit_bytes=mib << 20)


def route_kernel(ids_ref, gates_ref, out_ref):
    count = ids_ref.shape[1]
    expert = lax.broadcasted_iota(jnp.int32, (EXPERTS, count), 0)
    weight = jnp.zeros((EXPERTS, count), F32)
    chosen = jnp.zeros((EXPERTS, count), F32)
    for k in range(TOPK):
        hit = ids_ref[k : k + 1, :] == expert
        chosen = jnp.where(hit, 1.0, chosen)
        weight = jnp.where(hit, gates_ref[k : k + 1, :], weight)
    first = lax.broadcasted_iota(jnp.int32, (count, count), 0)
    second = lax.broadcasted_iota(jnp.int32, (count, count), 1)
    before = jnp.where(first < second, 1.0, 0.0).astype(BF16)
    position = lax.dot_general(chosen.astype(BF16), before, NN, preferred_element_type=F32)
    out_ref[:EXPERTS, :] = jnp.where(chosen > 0.0, position, -1.0)
    out_ref[EXPERTS:, :] = weight


def route(expert_ids, gate_weights):
    return pl.pallas_call(
        route_kernel,
        out_shape=jax.ShapeDtypeStruct((2 * EXPERTS, expert_ids.shape[0]), F32),
        name="route",
    )(expert_ids.T, gate_weights.T.astype(F32))


def place_kernel(experts, where_ref, *refs):
    *token_refs, table_ref, out_ref = refs
    count = table_ref.shape[1]
    slot_of = lax.broadcasted_iota(jnp.int32, (CAP, count), 0).astype(F32)
    table = [
        jnp.where(table_ref[pl.ds(where_ref[0] + e, 1), :] == slot_of, 1.0, 0.0)
        for e in range(experts)
    ]
    tokens = token_refs[0][...]
    for extra in token_refs[1:]:
        tokens = tokens + extra[...]
    table = jnp.concatenate(table, axis=0).astype(BF16)
    rows = lax.dot_general(table, tokens, NN, preferred_element_type=F32).astype(BF16)
    for e in range(experts):
        out_ref[e] = rows[e * CAP : (e + 1) * CAP]


def place(where, tokens, table, experts):
    whole = pl.BlockSpec(memory_space=pltpu.VMEM)
    return pl.pallas_call(
        functools.partial(place_kernel, experts),
        out_shape=jax.ShapeDtypeStruct((experts, CAP, tokens[0].shape[1]), BF16),
        in_specs=[pl.BlockSpec(memory_space=pltpu.SMEM)] + [whole] * (len(tokens) + 1),
        out_specs=whole,
        compiler_params=params(8),
        cost_estimate=QUICK,
        name="place",
    )(where, *tokens, table)


def gate_up_kernel(n_blocks, where_ref, *refs):
    row_refs = refs[:n_blocks]
    w_ref, _, send_ref, keep_ref, rows_ref, carry = refs[n_blocks:]
    step = pl.program_id(0)
    rows = n_blocks * CAP
    spare = 2 * LANES - rows
    x, core = where_ref[1], where_ref[2]
    quarter = w_ref.shape[1] // 4

    @pl.when(step == 0)
    def _():
        rows_ref[...] = jnp.zeros_like(rows_ref)

    def product(parity):
        for i in range(n_blocks):
            at = parity * spare + i * CAP
            rows_ref[parity, at : at + CAP, :] = row_refs[i][0]
        w = w_ref[0].reshape(8 * quarter, w_ref.shape[3])
        return lax.dot_general(w, rows_ref[parity], NT, preferred_element_type=F32)

    def store(tile, lane):
        tile = tile.astype(BF16)
        for q in range(4):
            piece = tile[2 * q * quarter : 2 * (q + 1) * quarter]
            at = jnp.where(x == q // 2, 1, 0)

            @pl.when(core == q % 2)
            def _():
                keep_ref[at, :, lane : lane + LANES] = piece

            @pl.when(core != q % 2)
            def _():
                send_ref[at, :, lane : lane + LANES] = piece

    @pl.when(lax.rem(step, 2) == 0)
    def _():
        out = product(0)
        store(out[:, :LANES], 0)
        carry[...] = out[:, LANES:]

    @pl.when(lax.rem(step, 2) == 1)
    def _():
        out = product(1)
        store(carry[...] + out[:, :LANES], LANES)
        store(out[:, LANES:], 2 * LANES)


def gate_up(where, placed, gu_weight, start, group, after):
    _, units, _, width = gu_weight.shape
    n_blocks = len(placed)
    lanes = 2 * n_blocks * CAP
    half = jax.ShapeDtypeStruct((2, units // 2, group // 2 * lanes), BF16)
    pair = pl.BlockSpec((2, units // 2, lanes), lambda i: (0, 0, i // 2))
    return pl.pallas_call(
        functools.partial(gate_up_kernel, n_blocks),
        grid=(group,),
        out_shape=(half, half),
        in_specs=[pl.BlockSpec(memory_space=pltpu.SMEM)]
        + [pl.BlockSpec((1, CAP, width), lambda i: (start + i, 0, 0))] * n_blocks
        + [pl.BlockSpec((1, units, 2, width), lambda i: (start + i, 0, 0, 0))]
        + [pl.BlockSpec(memory_space=pl.ANY)],
        out_specs=(pair, pair),
        scratch_shapes=[
            pltpu.VMEM((2, 2 * LANES, width), BF16),
            pltpu.VMEM((2 * units, LANES), F32),
        ],
        compiler_params=params(28),
        cost_estimate=QUICK,
        name="gate_up",
    )(where, *placed, gu_weight, after)


def hidden_kernel(keep_ref, near_ref, far_ref, _, out_ref, sums):
    units = out_ref.shape[1]
    for n in range(sums.shape[0]):
        lanes = slice(n * LANES, (n + 1) * LANES)
        total = keep_ref[0, :, lanes].astype(F32) + near_ref[0, :, lanes].astype(F32)
        sums[n] = total + far_ref[:, lanes].astype(F32)
        gate = sums[n, pl.ds(0, units, stride=2), :]
        up = sums[n, pl.ds(1, units, stride=2), :]
        out_ref[lanes, :] = (gate / (1.0 + jnp.exp(-gate)) * up).T.astype(BF16)


def hidden_quarter(keep, near, far, after):
    _, doubled, columns = keep.shape
    mine = pl.BlockSpec((1, doubled, columns), lambda i: (1, 0, 0))
    return pl.pallas_call(
        hidden_kernel,
        grid=(1,),
        out_shape=jax.ShapeDtypeStruct((columns, doubled // 2), BF16),
        in_specs=[
            mine,
            mine,
            pl.BlockSpec((doubled, columns), lambda i: (0, 0)),
            pl.BlockSpec(memory_space=pl.ANY),
        ],
        out_specs=pl.BlockSpec((columns, doubled // 2), lambda i: (0, 0)),
        scratch_shapes=[pltpu.VMEM((columns // LANES, doubled, LANES), F32)],
        compiler_params=params(10),
        cost_estimate=SLOW,
        name="hidden",
    )(keep, near, far, after)


def add_kernel(keep_ref, near_ref, _, out_ref):
    out_ref[...] = (keep_ref[0].astype(F32) + near_ref[0].astype(F32)).astype(BF16)


def chip_sum(keep, near, after):
    _, doubled, columns = keep.shape
    other = pl.BlockSpec((1, doubled, columns), lambda i: (0, 0, 0))
    return pl.pallas_call(
        add_kernel,
        grid=(1,),
        out_shape=jax.ShapeDtypeStruct((doubled, columns), BF16),
        in_specs=[other, other, pl.BlockSpec(memory_space=pl.ANY)],
        out_specs=pl.BlockSpec((doubled, columns), lambda i: (0, 0)),
        compiler_params=params(8),
        cost_estimate=QUICK,
        name="chip_sum",
    )(keep, near, after)


def down_kernel(group, n_blocks, first, has_carry, final, where_ref, *refs):
    hidden_refs, refs = refs[:4], refs[4:]
    route_refs, refs = refs[:n_blocks], refs[n_blocks:]
    w_hbm, refs = refs[0], refs[2:]
    carry_ref, refs = (refs[0], refs[1:]) if has_carry else (None, refs)
    out_refs, (held, w_buf, sems) = refs[:-3], refs[-3:]
    rows = n_blocks * CAP
    quarter = w_hbm.shape[1] // 4
    count = route_refs[0].shape[1]
    expert0 = where_ref[0]
    x, core = where_ref[1], where_ref[2]
    order = [(x, core), (1 - x, core), (x, 1 - core), (1 - x, 1 - core)]

    def fetch(e):
        copies = []
        for j in range(4):
            f0 = pl.multiple_of((order[j][0] * 2 + order[j][1]) * quarter, quarter)
            copies.append(
                pltpu.make_async_copy(
                    w_hbm.at[first + e, pl.ds(f0, quarter)],
                    w_buf.at[e, pl.ds(j * quarter, quarter)],
                    sems.at[e, j],
                )
            )
        return copies

    def start(e):
        for copy in fetch(e):
            copy.start()

    for e in range(min(2, group)):
        start(e)
    for e in range(group):
        for copy in fetch(e):
            copy.wait()
        if e + 2 < group:
            start(e + 2)
        units = jnp.concatenate([h[e * rows : (e + 1) * rows, :] for h in hidden_refs], axis=1)
        out = lax.dot_general(units, w_buf[e], NN, preferred_element_type=F32).astype(BF16)
        for i in range(n_blocks):
            held[i, e * CAP : (e + 1) * CAP, :] = out[i * CAP : (i + 1) * CAP]
    slot_of = lax.broadcasted_iota(jnp.int32, (CAP, count), 0).astype(F32)
    for i in range(n_blocks):
        table = [
            jnp.where(
                route_refs[i][pl.ds(expert0 + e, 1), :] == slot_of,
                route_refs[i][pl.ds(EXPERTS + expert0 + e, 1), :],
                0.0,
            )
            for e in range(group)
        ]
        table = jnp.concatenate(table, axis=0).astype(BF16)
        total = lax.dot_general(table, held[i], TN, preferred_element_type=F32)
        if has_carry:
            total = total + carry_ref[i]
        if final:
            out_refs[i][...] = total.astype(BF16)
        else:
            out_refs[0][i] = total


def down(where, hidden, routes, down_weight, first, group, carry, after):
    n_blocks = len(routes)
    units = hidden[0].shape[1]
    count = routes[0].shape[1]
    width = down_weight.shape[2]
    whole = pl.BlockSpec(memory_space=pltpu.VMEM)
    carried = [] if carry is None else [carry]
    final = first + group == down_weight.shape[0]
    if not final:
        out_shape = (jax.ShapeDtypeStruct((n_blocks, count, width), F32),)
    else:
        out_shape = tuple(jax.ShapeDtypeStruct((count, width), BF16) for _ in routes)
    return pl.pallas_call(
        functools.partial(down_kernel, group, n_blocks, first, carry is not None, final),
        out_shape=out_shape,
        in_specs=[pl.BlockSpec(memory_space=pltpu.SMEM)]
        + [whole] * (4 + n_blocks)
        + [pl.BlockSpec(memory_space=pl.ANY)] * 2
        + [whole] * len(carried),
        out_specs=tuple(whole for _ in out_shape),
        scratch_shapes=[
            pltpu.VMEM((n_blocks, group * CAP, width), BF16),
            pltpu.VMEM((group, 4 * units, width), BF16),
            pltpu.SemaphoreType.DMA((group, 4)),
        ],
        compiler_params=params(28),
        cost_estimate=QUICK,
        name="down",
    )(where, *hidden, *routes, down_weight, after, *carried)


def hold_kernel(*_):
    pass


def hold(arrays, until):
    free = pl.BlockSpec(memory_space=pl.ANY)
    return pl.pallas_call(
        hold_kernel,
        out_shape=tuple(jax.ShapeDtypeStruct(a.shape, a.dtype) for a in arrays),
        in_specs=[free] * (len(arrays) + len(until)),
        out_specs=(free,) * len(arrays),
        input_output_aliases={i: i for i in range(len(arrays))},
        compiler_params=params(1),
        cost_estimate=QUICK,
        name="hold",
    )(*arrays, *until)


def plus_kernel(a_ref, b_ref, _, out_ref, __):
    out_ref[...] = (a_ref[...].astype(F32) + b_ref[...].astype(F32)).astype(BF16)


def plus_then(a, b, other):
    whole = pl.BlockSpec(memory_space=pltpu.VMEM)
    free = pl.BlockSpec(memory_space=pl.ANY)
    return pl.pallas_call(
        plus_kernel,
        out_shape=(jax.ShapeDtypeStruct(a.shape, a.dtype), jax.ShapeDtypeStruct(a.shape, a.dtype)),
        in_specs=[whole, whole, free],
        out_specs=(whole, free),
        input_output_aliases={2: 1},
        compiler_params=params(4),
        cost_estimate=QUICK,
        name="plus",
    )(a, b, other)


def local_square(tokens, expert_ids, gate_weights, gu_weight, down_weight):
    z, t = lax.axis_index("ep"), lax.axis_index("tp")
    x, core = t // 2, t % 2
    local = gu_weight.shape[0]
    groups = [(0, local // 4), (local // 4, local // 2), (local * 3 // 4, local // 4)]
    wheres = [jnp.stack([z * local + first, x, core]).astype(jnp.int32) for first, _ in groups]

    def hop(array, pairs):
        return lax.ppermute(array, "ep", pairs)

    neighbour = hop(tokens, PAIR)
    middle_1 = hop(tokens, MIDDLE)
    table = route(expert_ids, gate_weights)
    table_1 = hop(table, PAIR)
    table_2 = hop(table, [(i, i ^ 2) for i in range(4)])
    table_3 = hop(table, [(i, i ^ 3) for i in range(4)])
    placed = [place(wheres[0], (tokens,), table, local)]
    neighbour, middle_1 = hold((neighbour, middle_1), placed)
    inner = (z == 1) | (z == 2)
    table_in = jnp.where(inner, table_3, table_2)
    table_out = jnp.where(inner, table_2, table_3)
    middle_2 = hop(neighbour, MIDDLE)
    end_1 = hop(middle_1, OUTWARD)
    end_2 = hop(middle_2, OUTWARD)
    tables = [table, table_1, table_in, table_out]
    blocks = [(neighbour,), (middle_1, end_1), (middle_2, end_2)]
    placed += [place(wheres[0], b, t, local) for b, t in zip(blocks, tables[1:])]

    def sums(n, after):
        send, keep = gate_up(wheres[n], placed, gu_weight, *groups[n], after)
        return keep, lax.ppermute(send, "tp", ACROSS_CORE)

    def across(keep, near, after):
        total = chip_sum(keep, near, after)
        return total, lax.ppermute(total, "tp", ACROSS_X)

    def halves(own):
        own_x = lax.ppermute(own, "tp", ACROSS_X)
        return own, own_x, lax.ppermute(own, "tp", ACROSS_CORE)

    def gathered(own, own_x, own_core):
        return own, own_x, own_core, lax.ppermute(own_x, "tp", ACROSS_CORE)

    def outputs(n, hidden, carry, after):
        return down(wheres[n], hidden, tables, down_weight, *groups[n], carry, after)

    keep_0, near_0 = sums(0, placed[3])
    turn, far_0 = across(keep_0, near_0, keep_0)
    keep_1, near_1 = sums(1, turn)
    own_0 = hidden_quarter(keep_0, near_0, far_0, keep_1)
    halves_0 = halves(own_0)
    turn, far_1 = across(keep_1, near_1, own_0)
    keep_2, near_2 = sums(2, turn)
    own_1 = hidden_quarter(keep_1, near_1, far_1, keep_2)
    halves_1 = halves(own_1)
    turn, far_2 = across(keep_2, near_2, own_1)
    own_0, x_0, core_0 = halves_0
    (x_0,) = hold((x_0,), (own_1,))
    (carry,) = outputs(0, gathered(own_0, x_0, core_0), None, turn)
    own_2 = hidden_quarter(keep_2, near_2, far_2, carry)
    halves_2 = halves(own_2)
    own_1, x_1, core_1 = halves_1
    (x_1,) = hold((x_1,), (own_2,))
    (carry,) = outputs(1, gathered(own_1, x_1, core_1), carry, own_2)
    own, other, far_in, far_out = outputs(2, gathered(*halves_2), carry, carry)

    def plus(a, b):
        return (a.astype(F32) + b.astype(F32)).astype(BF16)

    out_inner = hop(far_out, INWARD)
    far_out, far_in = plus_then(far_out, out_inner, far_in)
    out_mid = hop(far_out, MIDDLE)
    in_inner = hop(far_in, INWARD)
    last = hop(plus(other, out_mid), PAIR)
    in_mid = hop(plus(far_in, in_inner), MIDDLE)
    return (own.astype(F32) + in_mid.astype(F32) + last.astype(F32)).astype(BF16)


def local_general(tokens, expert_ids, gate_weights, gu_weight, down_weight):
    tok_rows, local_width = tokens.shape
    table = route(expert_ids, gate_weights)
    slots = jnp.arange(CAP, dtype=jnp.int32).astype(F32)
    matches = table[:EXPERTS, None, :] == slots[None, :, None]
    dispatch_table = matches.astype(BF16).reshape(EXPERTS * CAP, tok_rows)
    outgoing = jnp.dot(dispatch_table, tokens, preferred_element_type=F32)
    outgoing = outgoing.astype(BF16).reshape(EXPERTS, CAP, local_width)
    received = lax.all_to_all(outgoing, "ep", split_axis=0, concat_axis=1, tiled=True)
    terms = jnp.einsum("efgd,esd->fegs", gu_weight, received, preferred_element_type=F32)
    totals = lax.psum(terms.astype(BF16), "tp").astype(F32)
    hidden = (jax.nn.silu(totals[:, :, 0]) * totals[:, :, 1]).astype(BF16)
    expert_out = jnp.einsum("fes,efd->esd", hidden, down_weight, preferred_element_type=F32)
    returned = lax.all_to_all(
        expert_out.astype(BF16), "ep", split_axis=1, concat_axis=0, tiled=True
    )
    combine_table = jnp.where(matches, table[EXPERTS:, None, :], 0.0).astype(BF16)
    mixed = lax.dot_general(
        combine_table.reshape(EXPERTS * CAP, tok_rows),
        returned.reshape(EXPERTS * CAP, local_width),
        TN,
        preferred_element_type=F32,
    )
    return mixed.astype(BF16)


def solution(mesh):
    placed = (
        P(("grp", "ep"), "tp"),
        P(("grp", "ep"), None),
        P(("grp", "ep"), None),
        P("ep", None, None, "tp"),
        P("ep", None, "tp"),
    )
    square = mesh.shape["ep"] == 4 and mesh.shape["tp"] == 4
    return jax.shard_map(
        local_square if square else local_general,
        mesh=mesh,
        in_specs=placed,
        out_specs=P(("grp", "ep"), "tp"),
        check_vma=False,
    )
```

```python
import functools

import jax
import jax.numpy as jnp
from jax import lax
from jax.experimental import pallas as pl
from jax.experimental.pallas import tpu as pltpu
from jax.sharding import PartitionSpec as P

EXPERTS = 32
TOPK = 6
CAP = 48
LANES = 128
BF16, F32 = jnp.bfloat16, jnp.float32
NT = (((1,), (1,)), ((), ()))
TN = (((0,), (0,)), ((), ()))
NN = (((1,), (0,)), ((), ()))

PAIR = [(0, 1), (1, 0), (2, 3), (3, 2)]
MIDDLE = [(1, 2), (2, 1)]
OUTWARD = [(1, 0), (2, 3)]
INWARD = [(0, 1), (3, 2)]
ACROSS_X = [(0, 2), (1, 3), (2, 0), (3, 1)]
ACROSS_CORE = [(0, 1), (1, 0), (2, 3), (3, 2)]


QUICK = pl.CostEstimate(flops=1024, bytes_accessed=1024, transcendentals=0)


SLOW = pl.CostEstimate(flops=20_000_000_000, bytes_accessed=1024, transcendentals=0)


def params(mib):
    return pltpu.CompilerParams(vmem_limit_bytes=mib << 20)


def route_kernel(ids_ref, gates_ref, out_ref):
    count = ids_ref.shape[1]
    expert = lax.broadcasted_iota(jnp.int32, (EXPERTS, count), 0)
    weight = jnp.zeros((EXPERTS, count), F32)
    chosen = jnp.zeros((EXPERTS, count), F32)
    for k in range(TOPK):
        hit = ids_ref[k : k + 1, :] == expert
        chosen = jnp.where(hit, 1.0, chosen)
        weight = jnp.where(hit, gates_ref[k : k + 1, :], weight)
    first = lax.broadcasted_iota(jnp.int32, (count, count), 0)
    second = lax.broadcasted_iota(jnp.int32, (count, count), 1)
    before = jnp.where(first < second, 1.0, 0.0).astype(BF16)
    position = lax.dot_general(chosen.astype(BF16), before, NN, preferred_element_type=F32)
    out_ref[:EXPERTS, :] = jnp.where(chosen > 0.0, position, -1.0)
    out_ref[EXPERTS:, :] = weight


def route(expert_ids, gate_weights):
    return pl.pallas_call(
        route_kernel,
        out_shape=jax.ShapeDtypeStruct((2 * EXPERTS, expert_ids.shape[0]), F32),
        name="route",
    )(expert_ids.T, gate_weights.T.astype(F32))


EXTRA = 16


def pack_kernel(tokens_ref, extra_ref, out_ref):
    count, lanes = tokens_ref.shape[0], extra_ref.shape[1]
    out_ref[:count, :] = tokens_ref[...]
    out_ref[count:, lanes:] = jnp.zeros((EXTRA, out_ref.shape[1] - lanes), BF16)
    out_ref[count:, :lanes] = extra_ref[...]


def pack(tokens, expert_ids, gate_weights):
    count, width = tokens.shape
    spare = -count % LANES
    extra = [
        jnp.pad(a.T.astype(BF16), ((0, EXTRA - TOPK), (0, spare)))
        for a in (expert_ids, gate_weights)
    ]
    return pl.pallas_call(
        pack_kernel,
        out_shape=jax.ShapeDtypeStruct((count + EXTRA, width), BF16),
        compiler_params=params(8),
        cost_estimate=QUICK,
        name="pack",
    )(tokens, jnp.concatenate(extra, axis=1))


def place_kernel(experts, where_ref, *refs):
    *message_refs, out_ref, table_ref = refs
    count = table_ref.shape[1]
    lanes = count + -count % LANES
    message = message_refs[0][...]
    for more in message_refs[1:]:
        message = message + more[...]
    ids = message[count:, :count].astype(F32)
    gates = message[count:, lanes : lanes + count].astype(F32)
    expert = lax.broadcasted_iota(jnp.int32, (experts, count), 0) + where_ref[0]
    expert = expert.astype(F32)
    weight = jnp.zeros((experts, count), F32)
    chosen = jnp.zeros((experts, count), F32)
    for k in range(TOPK):
        hit = ids[k : k + 1, :] == expert
        chosen = jnp.where(hit, 1.0, chosen)
        weight = jnp.where(hit, gates[k : k + 1, :], weight)
    first = lax.broadcasted_iota(jnp.int32, (count, count), 0)
    second = lax.broadcasted_iota(jnp.int32, (count, count), 1)
    before = jnp.where(first < second, 1.0, 0.0).astype(BF16)
    position = lax.dot_general(chosen.astype(BF16), before, NN, preferred_element_type=F32)
    position = jnp.where(chosen > 0.0, position, -1.0)
    table_ref[:experts, :] = position
    table_ref[experts:, :] = weight
    slot_of = lax.broadcasted_iota(jnp.int32, (CAP, count), 0).astype(F32)
    table = [jnp.where(position[e : e + 1, :] == slot_of, 1.0, 0.0) for e in range(experts)]
    table = jnp.concatenate(table, axis=0).astype(BF16)
    rows = lax.dot_general(table, message[:count], NN, preferred_element_type=F32).astype(BF16)
    for e in range(experts):
        out_ref[e] = rows[e * CAP : (e + 1) * CAP]


def place(where, messages, experts):
    whole = pl.BlockSpec(memory_space=pltpu.VMEM)
    length, width = messages[0].shape
    return pl.pallas_call(
        functools.partial(place_kernel, experts),
        out_shape=(
            jax.ShapeDtypeStruct((experts, CAP, width), BF16),
            jax.ShapeDtypeStruct((2 * experts, length - EXTRA), F32),
        ),
        in_specs=[pl.BlockSpec(memory_space=pltpu.SMEM)] + [whole] * len(messages),
        out_specs=(whole, whole),
        compiler_params=params(12),
        cost_estimate=QUICK,
        name="place",
    )(where, *messages)


def gate_up_kernel(n_blocks, where_ref, *refs):
    row_refs = refs[:n_blocks]
    w_ref, _, send_ref, keep_ref, rows_ref, carry = refs[n_blocks:]
    step = pl.program_id(0)
    rows = n_blocks * CAP
    spare = 2 * LANES - rows
    x, core = where_ref[1], where_ref[2]
    quarter = w_ref.shape[1] // 4

    @pl.when(step == 0)
    def _():
        rows_ref[...] = jnp.zeros_like(rows_ref)

    def product(parity):
        for i in range(n_blocks):
            at = parity * spare + i * CAP
            rows_ref[parity, at : at + CAP, :] = row_refs[i][0]
        w = w_ref[0].reshape(8 * quarter, w_ref.shape[3])
        return lax.dot_general(w, rows_ref[parity], NT, preferred_element_type=F32)

    def store(tile, lane):
        tile = tile.astype(BF16)
        for q in range(4):
            piece = tile[2 * q * quarter : 2 * (q + 1) * quarter]
            at = jnp.where(x == q // 2, 1, 0)

            @pl.when(core == q % 2)
            def _():
                keep_ref[at, :, lane : lane + LANES] = piece

            @pl.when(core != q % 2)
            def _():
                send_ref[at, :, lane : lane + LANES] = piece

    @pl.when(lax.rem(step, 2) == 0)
    def _():
        out = product(0)
        store(out[:, :LANES], 0)
        carry[...] = out[:, LANES:]

    @pl.when(lax.rem(step, 2) == 1)
    def _():
        out = product(1)
        store(carry[...] + out[:, :LANES], LANES)
        store(out[:, LANES:], 2 * LANES)


def gate_up(where, placed, gu_weight, chunk, group, after):
    _, units, _, width = gu_weight.shape
    n_blocks = len(placed)
    lanes = 2 * n_blocks * CAP
    half = jax.ShapeDtypeStruct((2, units // 2, group // 2 * lanes), BF16)
    pair = pl.BlockSpec((2, units // 2, lanes), lambda i: (0, 0, i // 2))
    return pl.pallas_call(
        functools.partial(gate_up_kernel, n_blocks),
        grid=(group,),
        out_shape=(half, half),
        in_specs=[pl.BlockSpec(memory_space=pltpu.SMEM)]
        + [pl.BlockSpec((1, CAP, width), lambda i: (chunk * group + i, 0, 0))] * n_blocks
        + [pl.BlockSpec((1, units, 2, width), lambda i: (chunk * group + i, 0, 0, 0))]
        + [pl.BlockSpec(memory_space=pl.ANY)],
        out_specs=(pair, pair),
        scratch_shapes=[
            pltpu.VMEM((2, 2 * LANES, width), BF16),
            pltpu.VMEM((2 * units, LANES), F32),
        ],
        compiler_params=params(28),
        cost_estimate=QUICK,
        name="gate_up",
    )(where, *placed, gu_weight, after)


def hidden_kernel(keep_ref, near_ref, far_ref, _, out_ref, sums):
    units = out_ref.shape[1]
    for n in range(sums.shape[0]):
        lanes = slice(n * LANES, (n + 1) * LANES)
        total = keep_ref[0, :, lanes].astype(F32) + near_ref[0, :, lanes].astype(F32)
        sums[n] = total + far_ref[:, lanes].astype(F32)
        gate = sums[n, pl.ds(0, units, stride=2), :]
        up = sums[n, pl.ds(1, units, stride=2), :]
        out_ref[lanes, :] = (gate / (1.0 + jnp.exp(-gate)) * up).T.astype(BF16)


def hidden_quarter(keep, near, far, after):
    _, doubled, columns = keep.shape
    mine = pl.BlockSpec((1, doubled, columns), lambda i: (1, 0, 0))
    return pl.pallas_call(
        hidden_kernel,
        grid=(1,),
        out_shape=jax.ShapeDtypeStruct((columns, doubled // 2), BF16),
        in_specs=[
            mine,
            mine,
            pl.BlockSpec((doubled, columns), lambda i: (0, 0)),
            pl.BlockSpec(memory_space=pl.ANY),
        ],
        out_specs=pl.BlockSpec((columns, doubled // 2), lambda i: (0, 0)),
        scratch_shapes=[pltpu.VMEM((columns // LANES, doubled, LANES), F32)],
        compiler_params=params(10),
        cost_estimate=SLOW,
        name="hidden",
    )(keep, near, far, after)


def add_kernel(keep_ref, near_ref, _, out_ref):
    out_ref[...] = (keep_ref[0].astype(F32) + near_ref[0].astype(F32)).astype(BF16)


def chip_sum(keep, near, after):
    _, doubled, columns = keep.shape
    other = pl.BlockSpec((1, doubled, columns), lambda i: (0, 0, 0))
    return pl.pallas_call(
        add_kernel,
        grid=(1,),
        out_shape=jax.ShapeDtypeStruct((doubled, columns), BF16),
        in_specs=[other, other, pl.BlockSpec(memory_space=pl.ANY)],
        out_specs=pl.BlockSpec((doubled, columns), lambda i: (0, 0)),
        compiler_params=params(8),
        cost_estimate=QUICK,
        name="chip_sum",
    )(keep, near, after)


def down_kernel(group, n_blocks, chunk, has_carry, where_ref, *refs):
    hidden_refs, refs = refs[:4], refs[4:]
    route_refs, refs = refs[:n_blocks], refs[n_blocks:]
    w_hbm, refs = refs[0], refs[2:]
    carry_ref, refs = (refs[0], refs[1:]) if has_carry else (None, refs)
    out_refs, (held, w_buf, sems) = refs[:-3], refs[-3:]
    rows = n_blocks * CAP
    quarter = w_hbm.shape[1] // 4
    count = route_refs[0].shape[1]
    local = w_hbm.shape[0]
    x, core = where_ref[1], where_ref[2]
    order = [(x, core), (1 - x, core), (x, 1 - core), (1 - x, 1 - core)]

    def fetch(e):
        copies = []
        for j in range(4):
            f0 = pl.multiple_of((order[j][0] * 2 + order[j][1]) * quarter, quarter)
            copies.append(
                pltpu.make_async_copy(
                    w_hbm.at[chunk * group + e, pl.ds(f0, quarter)],
                    w_buf.at[e, pl.ds(j * quarter, quarter)],
                    sems.at[e, j],
                )
            )
        return copies

    def start(e):
        for copy in fetch(e):
            copy.start()

    start(0)
    start(1)
    for e in range(group):
        for copy in fetch(e):
            copy.wait()
        if e + 2 < group:
            start(e + 2)
        units = jnp.concatenate([h[e * rows : (e + 1) * rows, :] for h in hidden_refs], axis=1)
        out = lax.dot_general(units, w_buf[e], NN, preferred_element_type=F32).astype(BF16)
        for i in range(n_blocks):
            held[i, e * CAP : (e + 1) * CAP, :] = out[i * CAP : (i + 1) * CAP]
    slot_of = lax.broadcasted_iota(jnp.int32, (CAP, count), 0).astype(F32)
    for i in range(n_blocks):
        table = [
            jnp.where(
                route_refs[i][chunk * group + e : chunk * group + e + 1, :] == slot_of,
                route_refs[i][local + chunk * group + e : local + chunk * group + e + 1, :],
                0.0,
            )
            for e in range(group)
        ]
        table = jnp.concatenate(table, axis=0).astype(BF16)
        total = lax.dot_general(table, held[i], TN, preferred_element_type=F32)
        if has_carry:
            out_refs[i][...] = (total + carry_ref[i]).astype(BF16)
        else:
            out_refs[0][i] = total


def down(where, hidden, routes, down_weight, chunk, group, carry, after):
    n_blocks = len(routes)
    units = hidden[0].shape[1]
    count = routes[0].shape[1]
    width = down_weight.shape[2]
    whole = pl.BlockSpec(memory_space=pltpu.VMEM)
    carried = [] if carry is None else [carry]
    if carry is None:
        out_shape = (jax.ShapeDtypeStruct((n_blocks, count, width), F32),)
    else:
        out_shape = tuple(jax.ShapeDtypeStruct((count, width), BF16) for _ in routes)
    return pl.pallas_call(
        functools.partial(down_kernel, group, n_blocks, chunk, carry is not None),
        out_shape=out_shape,
        in_specs=[pl.BlockSpec(memory_space=pltpu.SMEM)]
        + [whole] * (4 + n_blocks)
        + [pl.BlockSpec(memory_space=pl.ANY)] * 2
        + [whole] * len(carried),
        out_specs=tuple(whole for _ in out_shape),
        scratch_shapes=[
            pltpu.VMEM((n_blocks, group * CAP, width), BF16),
            pltpu.VMEM((group, 4 * units, width), BF16),
            pltpu.SemaphoreType.DMA((group, 4)),
        ],
        compiler_params=params(28),
        cost_estimate=QUICK,
        name="down",
    )(where, *hidden, *routes, down_weight, after, *carried)


def plus_kernel(a_ref, b_ref, _, out_ref, __):
    out_ref[...] = (a_ref[...].astype(F32) + b_ref[...].astype(F32)).astype(BF16)


def plus_then(a, b, other):
    whole = pl.BlockSpec(memory_space=pltpu.VMEM)
    free = pl.BlockSpec(memory_space=pl.ANY)
    return pl.pallas_call(
        plus_kernel,
        out_shape=(jax.ShapeDtypeStruct(a.shape, a.dtype), jax.ShapeDtypeStruct(a.shape, a.dtype)),
        in_specs=[whole, whole, free],
        out_specs=(whole, free),
        input_output_aliases={2: 1},
        compiler_params=params(4),
        cost_estimate=QUICK,
        name="plus",
    )(a, b, other)


def local_square(tokens, expert_ids, gate_weights, gu_weight, down_weight):
    z, t = lax.axis_index("ep"), lax.axis_index("tp")
    x, core = t // 2, t % 2
    local = gu_weight.shape[0]
    group = local // 2
    where = jnp.stack([z * local, x, core]).astype(jnp.int32)

    def hop(array, pairs):
        return lax.ppermute(array, "ep", pairs)

    message = pack(tokens, expert_ids, gate_weights)
    neighbour = hop(message, PAIR)
    middle_1 = hop(message, MIDDLE)
    middle_2 = hop(neighbour, MIDDLE)
    end_1 = hop(middle_1, OUTWARD)
    end_2 = hop(middle_2, OUTWARD)
    blocks = [(message,), (neighbour,), (middle_1, end_1), (middle_2, end_2)]
    placed, tables = zip(*(place(where, b, local) for b in blocks))

    def sums(n, after):
        send, keep = gate_up(where, placed, gu_weight, n, group, after)
        return keep, lax.ppermute(send, "tp", ACROSS_CORE)

    def across(keep, near, after):
        total = chip_sum(keep, near, after)
        return total, lax.ppermute(total, "tp", ACROSS_X)

    def gathered(own):
        own_x = lax.ppermute(own, "tp", ACROSS_X)
        own_core = lax.ppermute(own, "tp", ACROSS_CORE)
        return own, own_x, own_core, lax.ppermute(own_x, "tp", ACROSS_CORE)

    keep_0, near_0 = sums(0, placed[3])
    turn, far_0 = across(keep_0, near_0, keep_0)
    keep_1, near_1 = sums(1, turn)
    own_0 = hidden_quarter(keep_0, near_0, far_0, keep_1)
    hidden_0 = gathered(own_0)
    turn, far_1 = across(keep_1, near_1, own_0)
    (carry,) = down(where, hidden_0, tables, down_weight, 0, group, None, turn)
    own_1 = hidden_quarter(keep_1, near_1, far_1, carry)
    hidden_1 = gathered(own_1)
    own, other, far_in, far_out = down(
        where, hidden_1, tables, down_weight, 1, group, carry, own_1
    )

    def plus(a, b):
        return (a.astype(F32) + b.astype(F32)).astype(BF16)

    out_inner = hop(far_out, INWARD)
    far_out, far_in = plus_then(far_out, out_inner, far_in)
    out_mid = hop(far_out, MIDDLE)
    in_inner = hop(far_in, INWARD)
    last = hop(plus(other, out_mid), PAIR)
    in_mid = hop(plus(far_in, in_inner), MIDDLE)
    return (own.astype(F32) + in_mid.astype(F32) + last.astype(F32)).astype(BF16)


def local_general(tokens, expert_ids, gate_weights, gu_weight, down_weight):
    tok_rows, local_width = tokens.shape
    table = route(expert_ids, gate_weights)
    slots = jnp.arange(CAP, dtype=jnp.int32).astype(F32)
    matches = table[:EXPERTS, None, :] == slots[None, :, None]
    dispatch_table = matches.astype(BF16).reshape(EXPERTS * CAP, tok_rows)
    outgoing = jnp.dot(dispatch_table, tokens, preferred_element_type=F32)
    outgoing = outgoing.astype(BF16).reshape(EXPERTS, CAP, local_width)
    received = lax.all_to_all(outgoing, "ep", split_axis=0, concat_axis=1, tiled=True)
    terms = jnp.einsum("efgd,esd->fegs", gu_weight, received, preferred_element_type=F32)
    totals = lax.psum(terms.astype(BF16), "tp").astype(F32)
    hidden = (jax.nn.silu(totals[:, :, 0]) * totals[:, :, 1]).astype(BF16)
    expert_out = jnp.einsum("fes,efd->esd", hidden, down_weight, preferred_element_type=F32)
    returned = lax.all_to_all(
        expert_out.astype(BF16), "ep", split_axis=1, concat_axis=0, tiled=True
    )
    combine_table = jnp.where(matches, table[EXPERTS:, None, :], 0.0).astype(BF16)
    mixed = lax.dot_general(
        combine_table.reshape(EXPERTS * CAP, tok_rows),
        returned.reshape(EXPERTS * CAP, local_width),
        TN,
        preferred_element_type=F32,
    )
    return mixed.astype(BF16)


def solution(mesh):
    placed = (
        P(("grp", "ep"), "tp"),
        P(("grp", "ep"), None),
        P(("grp", "ep"), None),
        P("ep", None, None, "tp"),
        P("ep", None, "tp"),
    )
    square = mesh.shape["ep"] == 4 and mesh.shape["tp"] == 4
    return jax.shard_map(
        local_square if square else local_general,
        mesh=mesh,
        in_specs=placed,
        out_specs=P(("grp", "ep"), "tp"),
        check_vma=False,
    )
```

```python
import functools

import jax
import jax.numpy as jnp
from jax import lax
from jax.experimental import pallas as pl
from jax.experimental.pallas import tpu as pltpu
from jax.sharding import PartitionSpec as P

EXPERTS = 32
TOPK = 6
CAP = 48
LANES = 128
BF16, F32 = jnp.bfloat16, jnp.float32
NT = (((1,), (1,)), ((), ()))
TN = (((0,), (0,)), ((), ()))
NN = (((1,), (0,)), ((), ()))

PAIR = [(0, 1), (1, 0), (2, 3), (3, 2)]
MIDDLE = [(1, 2), (2, 1)]
OUTWARD = [(1, 0), (2, 3)]
INWARD = [(0, 1), (3, 2)]
ACROSS_X = [(0, 2), (1, 3), (2, 0), (3, 1)]
ACROSS_CORE = [(0, 1), (1, 0), (2, 3), (3, 2)]


QUICK = pl.CostEstimate(flops=1024, bytes_accessed=1024, transcendentals=0)


SLOW = pl.CostEstimate(flops=20_000_000_000, bytes_accessed=1024, transcendentals=0)


def params(mib):
    return pltpu.CompilerParams(vmem_limit_bytes=mib << 20)


def route_kernel(ids_ref, gates_ref, out_ref):
    count = ids_ref.shape[1]
    expert = lax.broadcasted_iota(jnp.int32, (EXPERTS, count), 0)
    weight = jnp.zeros((EXPERTS, count), F32)
    chosen = jnp.zeros((EXPERTS, count), F32)
    for k in range(TOPK):
        hit = ids_ref[k : k + 1, :] == expert
        chosen = jnp.where(hit, 1.0, chosen)
        weight = jnp.where(hit, gates_ref[k : k + 1, :], weight)
    first = lax.broadcasted_iota(jnp.int32, (count, count), 0)
    second = lax.broadcasted_iota(jnp.int32, (count, count), 1)
    before = jnp.where(first < second, 1.0, 0.0).astype(BF16)
    position = lax.dot_general(chosen.astype(BF16), before, NN, preferred_element_type=F32)
    out_ref[:EXPERTS, :] = jnp.where(chosen > 0.0, position, -1.0)
    out_ref[EXPERTS:, :] = weight


def route(expert_ids, gate_weights):
    return pl.pallas_call(
        route_kernel,
        out_shape=jax.ShapeDtypeStruct((2 * EXPERTS, expert_ids.shape[0]), F32),
        name="route",
    )(expert_ids.T, gate_weights.T.astype(F32))


EXTRA = 16


def pack_kernel(tokens_ref, extra_ref, out_ref):
    count, lanes = tokens_ref.shape[0], extra_ref.shape[1]
    out_ref[:count, :] = tokens_ref[...]
    out_ref[count:, lanes:] = jnp.zeros((EXTRA, out_ref.shape[1] - lanes), BF16)
    out_ref[count:, :lanes] = extra_ref[...]


def pack(tokens, expert_ids, gate_weights):
    count, width = tokens.shape
    spare = -count % LANES
    extra = [
        jnp.pad(a.T.astype(BF16), ((0, EXTRA - TOPK), (0, spare)))
        for a in (expert_ids, gate_weights)
    ]
    return pl.pallas_call(
        pack_kernel,
        out_shape=jax.ShapeDtypeStruct((count + EXTRA, width), BF16),
        compiler_params=params(8),
        cost_estimate=QUICK,
        name="pack",
    )(tokens, jnp.concatenate(extra, axis=1))


def place_kernel(experts, where_ref, *refs):
    *message_refs, _, out_ref, table_ref = refs
    count = table_ref.shape[1]
    lanes = count + -count % LANES
    message = message_refs[0][...]
    for more in message_refs[1:]:
        message = message + more[...]
    ids = message[count:, :count].astype(F32)
    gates = message[count:, lanes : lanes + count].astype(F32)
    expert = lax.broadcasted_iota(jnp.int32, (experts, count), 0) + where_ref[0]
    expert = expert.astype(F32)
    weight = jnp.zeros((experts, count), F32)
    chosen = jnp.zeros((experts, count), F32)
    for k in range(TOPK):
        hit = ids[k : k + 1, :] == expert
        chosen = jnp.where(hit, 1.0, chosen)
        weight = jnp.where(hit, gates[k : k + 1, :], weight)
    first = lax.broadcasted_iota(jnp.int32, (count, count), 0)
    second = lax.broadcasted_iota(jnp.int32, (count, count), 1)
    before = jnp.where(first < second, 1.0, 0.0).astype(BF16)
    position = lax.dot_general(chosen.astype(BF16), before, NN, preferred_element_type=F32)
    position = jnp.where(chosen > 0.0, position, -1.0)
    table_ref[:experts, :] = position
    table_ref[experts:, :] = weight
    slot_of = lax.broadcasted_iota(jnp.int32, (CAP, count), 0).astype(F32)
    table = [jnp.where(position[e : e + 1, :] == slot_of, 1.0, 0.0) for e in range(experts)]
    table = jnp.concatenate(table, axis=0).astype(BF16)
    rows = lax.dot_general(table, message[:count], NN, preferred_element_type=F32).astype(BF16)
    for e in range(experts):
        out_ref[e] = rows[e * CAP : (e + 1) * CAP]


def place(where, messages, experts, after, cost):
    whole = pl.BlockSpec(memory_space=pltpu.VMEM)
    length, width = messages[0].shape
    return pl.pallas_call(
        functools.partial(place_kernel, experts),
        out_shape=(
            jax.ShapeDtypeStruct((experts, CAP, width), BF16),
            jax.ShapeDtypeStruct((2 * experts, length - EXTRA), F32),
        ),
        in_specs=[pl.BlockSpec(memory_space=pltpu.SMEM)]
        + [whole] * len(messages)
        + [pl.BlockSpec(memory_space=pl.ANY)],
        out_specs=(whole, whole),
        compiler_params=params(12),
        cost_estimate=cost,
        name="place",
    )(where, *messages, after)


FOUR = 4


def gate_up_kernel(n_blocks, where_ref, *refs):
    row_refs = refs[:n_blocks]
    w_ref, send_ref, keep_ref, rows_ref, carry = refs[n_blocks], *refs[-4:]
    step = pl.program_id(0)
    rows = n_blocks * CAP
    x, core = where_ref[1], where_ref[2]
    quarter = w_ref.shape[1] // 4

    @pl.when(step == 0)
    def _():
        rows_ref[...] = jnp.zeros_like(rows_ref)

    def store(tile, lane):
        tile = tile.astype(BF16)
        for q in range(4):
            piece = tile[2 * q * quarter : 2 * (q + 1) * quarter]
            at = jnp.where(x == q // 2, 1, 0)

            @pl.when(core == q % 2)
            def _():
                keep_ref[at, :, lane : lane + LANES] = piece

            @pl.when(core != q % 2)
            def _():
                send_ref[at, :, lane : lane + LANES] = piece

    def one(e):
        first, last = e * rows // LANES, -(-(e + 1) * rows // LANES)
        for i in range(n_blocks):
            at = e * rows - first * LANES + i * CAP
            rows_ref[e, at : at + CAP, :] = row_refs[i][0]
        w = w_ref[0].reshape(8 * quarter, w_ref.shape[3])
        r = rows_ref[e, : (last - first) * LANES, :]
        out = lax.dot_general(w, r, NT, preferred_element_type=F32)
        for n in range(first, last):
            tile = out[:, (n - first) * LANES : (n - first + 1) * LANES]
            if n * LANES < e * rows:
                tile = tile + carry[...]
            if (n + 1) * LANES <= (e + 1) * rows:
                store(tile, n * LANES)
            else:
                carry[...] = tile

    for e in range(FOUR):
        pl.when(step == e)(functools.partial(one, e))


def gate_up(where, placed, gu_weight, chunk, after):
    _, units, _, width = gu_weight.shape
    n_blocks = len(placed)
    lanes = FOUR * n_blocks * CAP
    half = jax.ShapeDtypeStruct((2, units // 2, lanes), BF16)
    whole = pl.BlockSpec((2, units // 2, lanes), lambda i: (0, 0, 0))
    return pl.pallas_call(
        functools.partial(gate_up_kernel, n_blocks),
        grid=(FOUR,),
        out_shape=(half, half),
        in_specs=[pl.BlockSpec(memory_space=pltpu.SMEM)]
        + [pl.BlockSpec((1, CAP, width), lambda i: (chunk * FOUR + i, 0, 0))] * n_blocks
        + [pl.BlockSpec((1, units, 2, width), lambda i: (chunk * FOUR + i, 0, 0, 0))]
        + [pl.BlockSpec(memory_space=pl.ANY)] * len(after),
        out_specs=(whole, whole),
        scratch_shapes=[
            pltpu.VMEM((FOUR, 2 * LANES, width), BF16),
            pltpu.VMEM((2 * units, LANES), F32),
        ],
        compiler_params=params(28),
        cost_estimate=QUICK,
        name="gate_up",
    )(where, *placed, gu_weight, *after)


def activate(keep_ref, near_ref, far_ref, out_ref, row0, sums):
    units = out_ref.shape[1]
    for n in range(sums.shape[0]):
        lanes = slice(n * LANES, (n + 1) * LANES)
        total = keep_ref[0, :, lanes].astype(F32) + near_ref[0, :, lanes].astype(F32)
        sums[n] = total + far_ref[:, lanes].astype(F32)
        gate = sums[n, pl.ds(0, units, stride=2), :]
        up = sums[n, pl.ds(1, units, stride=2), :]
        hidden = (gate / (1.0 + jnp.exp(-gate)) * up).T.astype(BF16)
        out_ref[row0 + n * LANES : row0 + (n + 1) * LANES, :] = hidden


def hidden_kernel(n_parts, has_first, *refs):
    parts = [refs[3 * n : 3 * n + 3] for n in range(n_parts)]
    outs, sums = refs[-1 - n_parts : -1], refs[-1]
    row0 = 0
    if has_first:
        first_ref = refs[3 * n_parts]
        row0 = first_ref.shape[0]
        outs[0][:row0, :] = first_ref[...]
    for part, out_ref in zip(parts, outs):
        activate(*part, out_ref, row0, sums)


def hidden_quarter(parts, first, after):
    _, doubled, lanes = parts[0][0].shape
    rows = lanes + (0 if first is None else first.shape[0])
    mine = pl.BlockSpec((1, doubled, lanes), lambda i: (1, 0, 0))
    whole = pl.BlockSpec((rows, doubled // 2), lambda i: (0, 0))
    early = [] if first is None else [first]
    return pl.pallas_call(
        functools.partial(hidden_kernel, len(parts), first is not None),
        grid=(1,),
        out_shape=[jax.ShapeDtypeStruct((rows, doubled // 2), BF16)] * len(parts),
        in_specs=[mine, mine, pl.BlockSpec((doubled, lanes), lambda i: (0, 0))] * len(parts)
        + [pl.BlockSpec(f.shape, lambda i: (0, 0)) for f in early]
        + [pl.BlockSpec(memory_space=pl.ANY)],
        out_specs=[whole] * len(parts),
        scratch_shapes=[pltpu.VMEM((lanes // LANES, doubled, LANES), F32)],
        compiler_params=params(14),
        cost_estimate=SLOW,
        name="hidden",
    )(*(array for part in parts for array in part), *early, after)


def add_kernel(keep_ref, near_ref, _, out_ref):
    out_ref[...] = (keep_ref[0].astype(F32) + near_ref[0].astype(F32)).astype(BF16)


def chip_sum(keep, near, after):
    _, doubled, columns = keep.shape
    other = pl.BlockSpec((1, doubled, columns), lambda i: (0, 0, 0))
    return pl.pallas_call(
        add_kernel,
        grid=(1,),
        out_shape=jax.ShapeDtypeStruct((doubled, columns), BF16),
        in_specs=[other, other, pl.BlockSpec(memory_space=pl.ANY)],
        out_specs=pl.BlockSpec((doubled, columns), lambda i: (0, 0)),
        compiler_params=params(8),
        cost_estimate=QUICK,
        name="chip_sum",
    )(keep, near, after)


def down_kernel(group, n_blocks, chunk, has_carry, where_ref, *refs):
    hidden_refs, refs = refs[:4], refs[4:]
    route_refs, refs = refs[:n_blocks], refs[n_blocks:]
    w_hbm, refs = refs[0], refs[2:]
    carry_ref, refs = (refs[0], refs[1:]) if has_carry else (None, refs)
    out_refs, (held, w_buf, sems) = refs[:-3], refs[-3:]
    rows = n_blocks * CAP
    quarter = w_hbm.shape[1] // 4
    count = route_refs[0].shape[1]
    local = w_hbm.shape[0]
    x, core = where_ref[1], where_ref[2]
    order = [(x, core), (1 - x, core), (x, 1 - core), (1 - x, 1 - core)]

    def fetch(e):
        copies = []
        for j in range(4):
            f0 = pl.multiple_of((order[j][0] * 2 + order[j][1]) * quarter, quarter)
            copies.append(
                pltpu.make_async_copy(
                    w_hbm.at[chunk * group + e, pl.ds(f0, quarter)],
                    w_buf.at[e, pl.ds(j * quarter, quarter)],
                    sems.at[e, j],
                )
            )
        return copies

    def start(e):
        for copy in fetch(e):
            copy.start()

    def rows_of(ref, e):
        far = group * (rows // 2)
        at = e * (rows // 2)
        return jnp.concatenate(
            [ref[at : at + rows // 2, :], ref[far + at : far + at + rows // 2, :]], axis=0
        )

    start(0)
    start(1)
    for e in range(group):
        for copy in fetch(e):
            copy.wait()
        if e + 2 < group:
            start(e + 2)
        units = jnp.concatenate([rows_of(h, e) for h in hidden_refs], axis=1)
        out = lax.dot_general(units, w_buf[e], NN, preferred_element_type=F32).astype(BF16)
        for i in range(n_blocks):
            held[i, e * CAP : (e + 1) * CAP, :] = out[i * CAP : (i + 1) * CAP]
    slot_of = lax.broadcasted_iota(jnp.int32, (CAP, count), 0).astype(F32)
    for i in range(n_blocks):
        table = [
            jnp.where(
                route_refs[i][chunk * group + e : chunk * group + e + 1, :] == slot_of,
                route_refs[i][local + chunk * group + e : local + chunk * group + e + 1, :],
                0.0,
            )
            for e in range(group)
        ]
        table = jnp.concatenate(table, axis=0).astype(BF16)
        total = lax.dot_general(table, held[i], TN, preferred_element_type=F32)
        if has_carry:
            out_refs[i][...] = (total + carry_ref[i]).astype(BF16)
        else:
            out_refs[0][i] = total


def down(where, hidden, routes, down_weight, chunk, group, carry, after):
    n_blocks = len(routes)
    units = hidden[0].shape[1]
    count = routes[0].shape[1]
    width = down_weight.shape[2]
    whole = pl.BlockSpec(memory_space=pltpu.VMEM)
    carried = [] if carry is None else [carry]
    if carry is None:
        out_shape = (jax.ShapeDtypeStruct((n_blocks, count, width), F32),)
    else:
        out_shape = tuple(jax.ShapeDtypeStruct((count, width), BF16) for _ in routes)
    return pl.pallas_call(
        functools.partial(down_kernel, group, n_blocks, chunk, carry is not None),
        out_shape=out_shape,
        in_specs=[pl.BlockSpec(memory_space=pltpu.SMEM)]
        + [whole] * (4 + n_blocks)
        + [pl.BlockSpec(memory_space=pl.ANY)] * 2
        + [whole] * len(carried),
        out_specs=tuple(whole for _ in out_shape),
        scratch_shapes=[
            pltpu.VMEM((n_blocks, group * CAP, width), BF16),
            pltpu.VMEM((group, 4 * units, width), BF16),
            pltpu.SemaphoreType.DMA((group, 4)),
        ],
        compiler_params=params(28),
        cost_estimate=QUICK,
        name="down",
    )(where, *hidden, *routes, down_weight, after, *carried)


def hold_kernel(*_):
    pass


def hold(arrays, until):
    free = pl.BlockSpec(memory_space=pl.ANY)
    return pl.pallas_call(
        hold_kernel,
        out_shape=tuple(jax.ShapeDtypeStruct(a.shape, a.dtype) for a in arrays),
        in_specs=[free] * (len(arrays) + len(until)),
        out_specs=(free,) * len(arrays),
        input_output_aliases={i: i for i in range(len(arrays))},
        compiler_params=params(1),
        cost_estimate=QUICK,
        name="hold",
    )(*arrays, *until)


def plus_kernel(a_ref, b_ref, _, out_ref, __):
    out_ref[...] = (a_ref[...].astype(F32) + b_ref[...].astype(F32)).astype(BF16)


def plus_then(a, b, other):
    whole = pl.BlockSpec(memory_space=pltpu.VMEM)
    free = pl.BlockSpec(memory_space=pl.ANY)
    return pl.pallas_call(
        plus_kernel,
        out_shape=(jax.ShapeDtypeStruct(a.shape, a.dtype), jax.ShapeDtypeStruct(a.shape, a.dtype)),
        in_specs=[whole, whole, free],
        out_specs=(whole, free),
        input_output_aliases={2: 1},
        compiler_params=params(4),
        cost_estimate=QUICK,
        name="plus",
    )(a, b, other)


def local_square(tokens, expert_ids, gate_weights, gu_weight, down_weight):
    z, t = lax.axis_index("ep"), lax.axis_index("tp")
    x, core = t // 2, t % 2
    local = gu_weight.shape[0]
    group = local // 2
    where = jnp.stack([z * local, x, core]).astype(jnp.int32)

    def hop(array, pairs):
        return lax.ppermute(array, "ep", pairs)

    def sums(placed, chunk, after):
        send, keep = gate_up(where, placed, gu_weight, chunk, after)
        return keep, lax.ppermute(send, "tp", ACROSS_CORE)

    def across(keep, near, after):
        total = chip_sum(keep, near, after)
        return total, lax.ppermute(total, "tp", ACROSS_X)

    def gathered(own):
        own_x = lax.ppermute(own, "tp", ACROSS_X)
        own_core = lax.ppermute(own, "tp", ACROSS_CORE)
        return own, own_x, own_core, lax.ppermute(own_x, "tp", ACROSS_CORE)

    message = pack(tokens, expert_ids, gate_weights)
    neighbour = hop(message, PAIR)
    middle_1 = hop(message, MIDDLE)
    own_rows, own_table = place(where, (message,), local, message, QUICK)
    neighbour, middle_1 = hold((neighbour, middle_1), (own_rows,))
    middle_2 = hop(neighbour, MIDDLE)
    end_1 = hop(middle_1, OUTWARD)
    next_rows, next_table = place(where, (neighbour,), local, own_rows, QUICK)
    close = [own_rows, next_rows]
    keep_n0, near_n0 = sums(close, 0, [])
    middle_2, end_1 = hold((middle_2, end_1), (keep_n0,))
    end_2 = hop(middle_2, OUTWARD)
    keep_n1, near_n1 = sums(close, 1, [middle_2])
    turn, far_n0 = across(keep_n0, near_n0, keep_n1)
    in_rows, in_table = place(where, (middle_1, end_1), local, turn, QUICK)
    out_rows, out_table = place(where, (middle_2, end_2), local, in_rows, SLOW)
    turn, far_n1 = across(keep_n1, near_n1, out_rows)
    away = [in_rows, out_rows]
    tables = [own_table, next_table, in_table, out_table]
    keep_f0, near_f0 = sums(away, 0, [turn])
    first_0, first_1 = hidden_quarter(
        [(keep_n0, near_n0, far_n0), (keep_n1, near_n1, far_n1)], None, keep_f0
    )
    turn, far_f0 = across(keep_f0, near_f0, first_0)
    keep_f1, near_f1 = sums(away, 1, [turn])
    (own_0,) = hidden_quarter([(keep_f0, near_f0, far_f0)], first_0, keep_f1)
    hidden_0 = gathered(own_0)
    turn, far_f1 = across(keep_f1, near_f1, own_0)
    (carry,) = down(where, hidden_0, tables, down_weight, 0, group, None, turn)
    (own_1,) = hidden_quarter([(keep_f1, near_f1, far_f1)], first_1, carry)
    hidden_1 = gathered(own_1)
    own, other, far_in, far_out = down(
        where, hidden_1, tables, down_weight, 1, group, carry, own_1
    )

    def plus(a, b):
        return (a.astype(F32) + b.astype(F32)).astype(BF16)

    out_inner = hop(far_out, INWARD)
    far_out, far_in = plus_then(far_out, out_inner, far_in)
    out_mid = hop(far_out, MIDDLE)
    in_inner = hop(far_in, INWARD)
    last = hop(plus(other, out_mid), PAIR)
    in_mid = hop(plus(far_in, in_inner), MIDDLE)
    return (own.astype(F32) + in_mid.astype(F32) + last.astype(F32)).astype(BF16)


def local_general(tokens, expert_ids, gate_weights, gu_weight, down_weight):
    tok_rows, local_width = tokens.shape
    table = route(expert_ids, gate_weights)
    slots = jnp.arange(CAP, dtype=jnp.int32).astype(F32)
    matches = table[:EXPERTS, None, :] == slots[None, :, None]
    dispatch_table = matches.astype(BF16).reshape(EXPERTS * CAP, tok_rows)
    outgoing = jnp.dot(dispatch_table, tokens, preferred_element_type=F32)
    outgoing = outgoing.astype(BF16).reshape(EXPERTS, CAP, local_width)
    received = lax.all_to_all(outgoing, "ep", split_axis=0, concat_axis=1, tiled=True)
    terms = jnp.einsum("efgd,esd->fegs", gu_weight, received, preferred_element_type=F32)
    totals = lax.psum(terms.astype(BF16), "tp").astype(F32)
    hidden = (jax.nn.silu(totals[:, :, 0]) * totals[:, :, 1]).astype(BF16)
    expert_out = jnp.einsum("fes,efd->esd", hidden, down_weight, preferred_element_type=F32)
    returned = lax.all_to_all(
        expert_out.astype(BF16), "ep", split_axis=1, concat_axis=0, tiled=True
    )
    combine_table = jnp.where(matches, table[EXPERTS:, None, :], 0.0).astype(BF16)
    mixed = lax.dot_general(
        combine_table.reshape(EXPERTS * CAP, tok_rows),
        returned.reshape(EXPERTS * CAP, local_width),
        TN,
        preferred_element_type=F32,
    )
    return mixed.astype(BF16)


def solution(mesh):
    placed = (
        P(("grp", "ep"), "tp"),
        P(("grp", "ep"), None),
        P(("grp", "ep"), None),
        P("ep", None, None, "tp"),
        P("ep", None, "tp"),
    )
    square = mesh.shape["ep"] == 4 and mesh.shape["tp"] == 4
    return jax.shard_map(
        local_square if square else local_general,
        mesh=mesh,
        in_specs=placed,
        out_specs=P(("grp", "ep"), "tp"),
        check_vma=False,
    )
```

```python
import functools

import jax
import jax.numpy as jnp
from jax import lax
from jax.experimental import pallas as pl
from jax.experimental.pallas import tpu as pltpu
from jax.sharding import PartitionSpec as P

EXPERTS = 32
TOPK = 6
CAP = 48
LANES = 128
BF16, F32 = jnp.bfloat16, jnp.float32
NT = (((1,), (1,)), ((), ()))
TN = (((0,), (0,)), ((), ()))
NN = (((1,), (0,)), ((), ()))

PAIR = [(0, 1), (1, 0), (2, 3), (3, 2)]
MIDDLE = [(1, 2), (2, 1)]
OUTWARD = [(1, 0), (2, 3)]
INWARD = [(0, 1), (3, 2)]
ACROSS_X = [(0, 2), (1, 3), (2, 0), (3, 1)]
ACROSS_CORE = [(0, 1), (1, 0), (2, 3), (3, 2)]


QUICK = pl.CostEstimate(flops=1024, bytes_accessed=1024, transcendentals=0)


SLOW = pl.CostEstimate(flops=20_000_000_000, bytes_accessed=1024, transcendentals=0)


def params(mib):
    return pltpu.CompilerParams(vmem_limit_bytes=mib << 20)


def route_kernel(ids_ref, gates_ref, out_ref):
    count = ids_ref.shape[1]
    expert = lax.broadcasted_iota(jnp.int32, (EXPERTS, count), 0)
    weight = jnp.zeros((EXPERTS, count), F32)
    chosen = jnp.zeros((EXPERTS, count), F32)
    for k in range(TOPK):
        hit = ids_ref[k : k + 1, :] == expert
        chosen = jnp.where(hit, 1.0, chosen)
        weight = jnp.where(hit, gates_ref[k : k + 1, :], weight)
    first = lax.broadcasted_iota(jnp.int32, (count, count), 0)
    second = lax.broadcasted_iota(jnp.int32, (count, count), 1)
    before = jnp.where(first < second, 1.0, 0.0).astype(BF16)
    position = lax.dot_general(chosen.astype(BF16), before, NN, preferred_element_type=F32)
    out_ref[:EXPERTS, :] = jnp.where(chosen > 0.0, position, -1.0)
    out_ref[EXPERTS:, :] = weight


def route(expert_ids, gate_weights):
    return pl.pallas_call(
        route_kernel,
        out_shape=jax.ShapeDtypeStruct((2 * EXPERTS, expert_ids.shape[0]), F32),
        name="route",
    )(expert_ids.T, gate_weights.T.astype(F32))


EXTRA = 16


def pack_kernel(tokens_ref, extra_ref, out_ref):
    count, lanes = tokens_ref.shape[0], extra_ref.shape[1]
    out_ref[:count, :] = tokens_ref[...]
    out_ref[count:, lanes:] = jnp.zeros((EXTRA, out_ref.shape[1] - lanes), BF16)
    out_ref[count:, :lanes] = extra_ref[...]


def pack(tokens, expert_ids, gate_weights):
    count, width = tokens.shape
    spare = -count % LANES
    extra = [
        jnp.pad(a.T.astype(BF16), ((0, EXTRA - TOPK), (0, spare)))
        for a in (expert_ids, gate_weights)
    ]
    return pl.pallas_call(
        pack_kernel,
        out_shape=jax.ShapeDtypeStruct((count + EXTRA, width), BF16),
        compiler_params=params(8),
        cost_estimate=QUICK,
        name="pack",
    )(tokens, jnp.concatenate(extra, axis=1))


def place_kernel(experts, where_ref, *refs):
    *message_refs, out_ref, table_ref = refs
    count = table_ref.shape[1]
    lanes = count + -count % LANES
    message = message_refs[0][...]
    for more in message_refs[1:]:
        message = message + more[...]
    ids = message[count:, :count].astype(F32)
    gates = message[count:, lanes : lanes + count].astype(F32)
    expert = lax.broadcasted_iota(jnp.int32, (experts, count), 0) + where_ref[0]
    expert = expert.astype(F32)
    weight = jnp.zeros((experts, count), F32)
    chosen = jnp.zeros((experts, count), F32)
    for k in range(TOPK):
        hit = ids[k : k + 1, :] == expert
        chosen = jnp.where(hit, 1.0, chosen)
        weight = jnp.where(hit, gates[k : k + 1, :], weight)
    first = lax.broadcasted_iota(jnp.int32, (count, count), 0)
    second = lax.broadcasted_iota(jnp.int32, (count, count), 1)
    before = jnp.where(first < second, 1.0, 0.0).astype(BF16)
    position = lax.dot_general(chosen.astype(BF16), before, NN, preferred_element_type=F32)
    position = jnp.where(chosen > 0.0, position, -1.0)
    table_ref[:experts, :] = position
    table_ref[experts:, :] = weight
    slot_of = lax.broadcasted_iota(jnp.int32, (CAP, count), 0).astype(F32)
    table = [jnp.where(position[e : e + 1, :] == slot_of, 1.0, 0.0) for e in range(experts)]
    table = jnp.concatenate(table, axis=0).astype(BF16)
    rows = lax.dot_general(table, message[:count], NN, preferred_element_type=F32).astype(BF16)
    for e in range(experts):
        out_ref[e] = rows[e * CAP : (e + 1) * CAP]


def place(where, messages, experts):
    whole = pl.BlockSpec(memory_space=pltpu.VMEM)
    length, width = messages[0].shape
    return pl.pallas_call(
        functools.partial(place_kernel, experts),
        out_shape=(
            jax.ShapeDtypeStruct((experts, CAP, width), BF16),
            jax.ShapeDtypeStruct((2 * experts, length - EXTRA), F32),
        ),
        in_specs=[pl.BlockSpec(memory_space=pltpu.SMEM)] + [whole] * len(messages),
        out_specs=(whole, whole),
        compiler_params=params(12),
        cost_estimate=QUICK,
        name="place",
    )(where, *messages)


def gate_up_kernel(n_blocks, where_ref, *refs):
    row_refs = refs[:n_blocks]
    w_ref, _, send_ref, keep_ref, rows_ref, carry = refs[n_blocks:]
    step = pl.program_id(0)
    rows = n_blocks * CAP
    spare = 2 * LANES - rows
    x, core = where_ref[1], where_ref[2]
    quarter = w_ref.shape[1] // 4

    @pl.when(step == 0)
    def _():
        rows_ref[...] = jnp.zeros_like(rows_ref)

    def product(parity):
        for i in range(n_blocks):
            at = parity * spare + i * CAP
            rows_ref[parity, at : at + CAP, :] = row_refs[i][0]
        w = w_ref[0].reshape(8 * quarter, w_ref.shape[3])
        return lax.dot_general(w, rows_ref[parity], NT, preferred_element_type=F32)

    def store(tile, lane):
        tile = tile.astype(BF16)
        for q in range(4):
            piece = tile[2 * q * quarter : 2 * (q + 1) * quarter]
            at = jnp.where(x == q // 2, 1, 0)

            @pl.when(core == q % 2)
            def _():
                keep_ref[at, :, lane : lane + LANES] = piece

            @pl.when(core != q % 2)
            def _():
                send_ref[at, :, lane : lane + LANES] = piece

    @pl.when(lax.rem(step, 2) == 0)
    def _():
        out = product(0)
        store(out[:, :LANES], 0)
        carry[...] = out[:, LANES:]

    @pl.when(lax.rem(step, 2) == 1)
    def _():
        out = product(1)
        store(carry[...] + out[:, :LANES], LANES)
        store(out[:, LANES:], 2 * LANES)


def gate_up(where, placed, gu_weight, chunk, group, after):
    _, units, _, width = gu_weight.shape
    n_blocks = len(placed)
    lanes = 2 * n_blocks * CAP
    half = jax.ShapeDtypeStruct((2, units // 2, group // 2 * lanes), BF16)
    pair = pl.BlockSpec((2, units // 2, lanes), lambda i: (0, 0, i // 2))
    return pl.pallas_call(
        functools.partial(gate_up_kernel, n_blocks),
        grid=(group,),
        out_shape=(half, half),
        in_specs=[pl.BlockSpec(memory_space=pltpu.SMEM)]
        + [pl.BlockSpec((1, CAP, width), lambda i: (chunk * group + i, 0, 0))] * n_blocks
        + [pl.BlockSpec((1, units, 2, width), lambda i: (chunk * group + i, 0, 0, 0))]
        + [pl.BlockSpec(memory_space=pl.ANY)],
        out_specs=(pair, pair),
        scratch_shapes=[
            pltpu.VMEM((2, 2 * LANES, width), BF16),
            pltpu.VMEM((2 * units, LANES), F32),
        ],
        compiler_params=params(28),
        cost_estimate=QUICK,
        name="gate_up",
    )(where, *placed, gu_weight, after)


def hidden_kernel(keep_ref, near_ref, far_ref, _, out_ref, sums):
    units = out_ref.shape[1]
    for n in range(sums.shape[0]):
        lanes = slice(n * LANES, (n + 1) * LANES)
        total = keep_ref[0, :, lanes].astype(F32) + near_ref[0, :, lanes].astype(F32)
        sums[n] = total + far_ref[:, lanes].astype(F32)
        gate = sums[n, pl.ds(0, units, stride=2), :]
        up = sums[n, pl.ds(1, units, stride=2), :]
        out_ref[lanes, :] = (gate / (1.0 + jnp.exp(-gate)) * up).T.astype(BF16)


def hidden_quarter(keep, near, far, after):
    _, doubled, columns = keep.shape
    mine = pl.BlockSpec((1, doubled, columns), lambda i: (1, 0, 0))
    return pl.pallas_call(
        hidden_kernel,
        grid=(1,),
        out_shape=jax.ShapeDtypeStruct((columns, doubled // 2), BF16),
        in_specs=[
            mine,
            mine,
            pl.BlockSpec((doubled, columns), lambda i: (0, 0)),
            pl.BlockSpec(memory_space=pl.ANY),
        ],
        out_specs=pl.BlockSpec((columns, doubled // 2), lambda i: (0, 0)),
        scratch_shapes=[pltpu.VMEM((columns // LANES, doubled, LANES), F32)],
        compiler_params=params(10),
        cost_estimate=SLOW,
        name="hidden",
    )(keep, near, far, after)


def add_kernel(keep_ref, near_ref, _, out_ref):
    out_ref[...] = (keep_ref[0].astype(F32) + near_ref[0].astype(F32)).astype(BF16)


def chip_sum(keep, near, after):
    _, doubled, columns = keep.shape
    other = pl.BlockSpec((1, doubled, columns), lambda i: (0, 0, 0))
    return pl.pallas_call(
        add_kernel,
        grid=(1,),
        out_shape=jax.ShapeDtypeStruct((doubled, columns), BF16),
        in_specs=[other, other, pl.BlockSpec(memory_space=pl.ANY)],
        out_specs=pl.BlockSpec((doubled, columns), lambda i: (0, 0)),
        compiler_params=params(8),
        cost_estimate=QUICK,
        name="chip_sum",
    )(keep, near, after)


def down_kernel(group, n_blocks, chunk, quarters, has_carry, has_part, is_part, where_ref, *refs):
    hidden_refs, refs = refs[: len(quarters)], refs[len(quarters) :]
    route_refs, refs = refs[:n_blocks], refs[n_blocks:]
    w_hbm, refs = refs[0], refs[2:]
    carry_ref, refs = (refs[0], refs[1:]) if has_carry else (None, refs)
    part_ref, refs = (refs[0], refs[1:]) if has_part else (None, refs)
    out_refs, (held, w_buf, sems) = refs[:-3], refs[-3:]
    rows = n_blocks * CAP
    quarter = w_hbm.shape[1] // 4
    count = route_refs[0].shape[1]
    local = w_hbm.shape[0]
    x, core = where_ref[1], where_ref[2]
    order = [(x, core), (x, 1 - core), (1 - x, core), (1 - x, 1 - core)]

    def fetch(e):
        copies = []
        for n, j in enumerate(quarters):
            f0 = pl.multiple_of((order[j][0] * 2 + order[j][1]) * quarter, quarter)
            copies.append(
                pltpu.make_async_copy(
                    w_hbm.at[chunk * group + e, pl.ds(f0, quarter)],
                    w_buf.at[e, pl.ds(n * quarter, quarter)],
                    sems.at[e, n],
                )
            )
        return copies

    def start(e):
        for copy in fetch(e):
            copy.start()

    start(0)
    start(1)
    for e in range(group):
        for copy in fetch(e):
            copy.wait()
        if e + 2 < group:
            start(e + 2)
        units = jnp.concatenate([h[e * rows : (e + 1) * rows, :] for h in hidden_refs], axis=1)
        out = lax.dot_general(units, w_buf[e], NN, preferred_element_type=F32)
        if is_part:
            out_refs[0][e] = out
            continue
        if has_part:
            out = out + part_ref[e]
        out = out.astype(BF16)
        for i in range(n_blocks):
            held[i, e * CAP : (e + 1) * CAP, :] = out[i * CAP : (i + 1) * CAP]
    if is_part:
        return
    slot_of = lax.broadcasted_iota(jnp.int32, (CAP, count), 0).astype(F32)
    for i in range(n_blocks):
        table = [
            jnp.where(
                route_refs[i][chunk * group + e : chunk * group + e + 1, :] == slot_of,
                route_refs[i][local + chunk * group + e : local + chunk * group + e + 1, :],
                0.0,
            )
            for e in range(group)
        ]
        table = jnp.concatenate(table, axis=0).astype(BF16)
        total = lax.dot_general(table, held[i], TN, preferred_element_type=F32)
        if has_carry:
            out_refs[i][...] = (total + carry_ref[i]).astype(BF16)
        else:
            out_refs[0][i] = total


def down(where, hidden, routes, down_weight, chunk, group, carry, after, part=None, is_part=False):
    n_blocks = len(routes)
    quarters = tuple(sorted(hidden))
    units = hidden[quarters[0]].shape[1]
    count = routes[0].shape[1]
    width = down_weight.shape[2]
    whole = pl.BlockSpec(memory_space=pltpu.VMEM)
    extra = [a for a in (carry, part) if a is not None]
    if is_part:
        out_shape = (jax.ShapeDtypeStruct((group, n_blocks * CAP, width), F32),)
    elif carry is None:
        out_shape = (jax.ShapeDtypeStruct((n_blocks, count, width), F32),)
    else:
        out_shape = tuple(jax.ShapeDtypeStruct((count, width), BF16) for _ in routes)
    return pl.pallas_call(
        functools.partial(
            down_kernel, group, n_blocks, chunk, quarters, carry is not None, part is not None, is_part
        ),
        out_shape=out_shape,
        in_specs=[pl.BlockSpec(memory_space=pltpu.SMEM)]
        + [whole] * (len(quarters) + n_blocks)
        + [pl.BlockSpec(memory_space=pl.ANY)] * 2
        + [whole] * len(extra),
        out_specs=tuple(whole for _ in out_shape),
        scratch_shapes=[
            pltpu.VMEM((n_blocks, group * CAP, width), BF16),
            pltpu.VMEM((group, len(quarters) * units, width), BF16),
            pltpu.SemaphoreType.DMA((group, len(quarters))),
        ],
        compiler_params=params(28),
        cost_estimate=QUICK,
        name="down",
    )(where, *(hidden[j] for j in quarters), *routes, down_weight, after, *extra)


def hold_kernel(*_):
    pass


def hold(arrays, until):
    free = pl.BlockSpec(memory_space=pl.ANY)
    return pl.pallas_call(
        hold_kernel,
        out_shape=tuple(jax.ShapeDtypeStruct(a.shape, a.dtype) for a in arrays),
        in_specs=[free] * (len(arrays) + len(until)),
        out_specs=(free,) * len(arrays),
        input_output_aliases={i: i for i in range(len(arrays))},
        compiler_params=params(1),
        cost_estimate=QUICK,
        name="hold",
    )(*arrays, *until)


def plus_kernel(a_ref, b_ref, _, out_ref, __):
    out_ref[...] = (a_ref[...].astype(F32) + b_ref[...].astype(F32)).astype(BF16)


def plus_then(a, b, other):
    whole = pl.BlockSpec(memory_space=pltpu.VMEM)
    free = pl.BlockSpec(memory_space=pl.ANY)
    return pl.pallas_call(
        plus_kernel,
        out_shape=(jax.ShapeDtypeStruct(a.shape, a.dtype), jax.ShapeDtypeStruct(a.shape, a.dtype)),
        in_specs=[whole, whole, free],
        out_specs=(whole, free),
        input_output_aliases={2: 1},
        compiler_params=params(4),
        cost_estimate=QUICK,
        name="plus",
    )(a, b, other)


def local_square(tokens, expert_ids, gate_weights, gu_weight, down_weight):
    z, t = lax.axis_index("ep"), lax.axis_index("tp")
    x, core = t // 2, t % 2
    local = gu_weight.shape[0]
    group = local // 2
    where = jnp.stack([z * local, x, core]).astype(jnp.int32)

    def hop(array, pairs):
        return lax.ppermute(array, "ep", pairs)

    message = pack(tokens, expert_ids, gate_weights)
    neighbour = hop(message, PAIR)
    middle_1 = hop(message, MIDDLE)
    middle_2 = hop(neighbour, MIDDLE)
    end_1 = hop(middle_1, OUTWARD)
    end_2 = hop(middle_2, OUTWARD)
    blocks = [(message,), (neighbour,), (middle_1, end_1), (middle_2, end_2)]
    placed, tables = zip(*(place(where, b, local) for b in blocks))

    def sums(n, after):
        send, keep = gate_up(where, placed, gu_weight, n, group, after)
        return keep, lax.ppermute(send, "tp", ACROSS_CORE)

    def across(keep, near, after):
        total = chip_sum(keep, near, after)
        return total, lax.ppermute(total, "tp", ACROSS_X)

    def halves(own):
        own_x = lax.ppermute(own, "tp", ACROSS_X)
        return own_x, lax.ppermute(own, "tp", ACROSS_CORE)

    keep_0, near_0 = sums(0, placed[3])
    turn, far_0 = across(keep_0, near_0, keep_0)
    keep_1, near_1 = sums(1, turn)
    own_0 = hidden_quarter(keep_0, near_0, far_0, keep_1)
    x_0, core_0 = halves(own_0)
    both_0 = lax.ppermute(x_0, "tp", ACROSS_CORE)
    turn, far_1 = across(keep_1, near_1, own_0)
    hidden_0 = {0: own_0, 1: core_0, 2: x_0, 3: both_0}
    (carry,) = down(where, hidden_0, tables, down_weight, 0, group, None, turn)
    own_1 = hidden_quarter(keep_1, near_1, far_1, carry)
    x_1, core_1 = halves(own_1)
    (part,) = down(
        where, {0: own_1, 1: core_1}, tables, down_weight, 1, group, None, own_1, is_part=True
    )
    (x_1,) = hold((x_1,), (part,))
    both_1 = lax.ppermute(x_1, "tp", ACROSS_CORE)
    own, other, far_in, far_out = down(
        where, {2: x_1, 3: both_1}, tables, down_weight, 1, group, carry, part, part
    )

    def plus(a, b):
        return (a.astype(F32) + b.astype(F32)).astype(BF16)

    out_inner = hop(far_out, INWARD)
    far_out, far_in = plus_then(far_out, out_inner, far_in)
    out_mid = hop(far_out, MIDDLE)
    in_inner = hop(far_in, INWARD)
    last = hop(plus(other, out_mid), PAIR)
    in_mid = hop(plus(far_in, in_inner), MIDDLE)
    return (own.astype(F32) + in_mid.astype(F32) + last.astype(F32)).astype(BF16)


def local_general(tokens, expert_ids, gate_weights, gu_weight, down_weight):
    tok_rows, local_width = tokens.shape
    table = route(expert_ids, gate_weights)
    slots = jnp.arange(CAP, dtype=jnp.int32).astype(F32)
    matches = table[:EXPERTS, None, :] == slots[None, :, None]
    dispatch_table = matches.astype(BF16).reshape(EXPERTS * CAP, tok_rows)
    outgoing = jnp.dot(dispatch_table, tokens, preferred_element_type=F32)
    outgoing = outgoing.astype(BF16).reshape(EXPERTS, CAP, local_width)
    received = lax.all_to_all(outgoing, "ep", split_axis=0, concat_axis=1, tiled=True)
    terms = jnp.einsum("efgd,esd->fegs", gu_weight, received, preferred_element_type=F32)
    totals = lax.psum(terms.astype(BF16), "tp").astype(F32)
    hidden = (jax.nn.silu(totals[:, :, 0]) * totals[:, :, 1]).astype(BF16)
    expert_out = jnp.einsum("fes,efd->esd", hidden, down_weight, preferred_element_type=F32)
    returned = lax.all_to_all(
        expert_out.astype(BF16), "ep", split_axis=1, concat_axis=0, tiled=True
    )
    combine_table = jnp.where(matches, table[EXPERTS:, None, :], 0.0).astype(BF16)
    mixed = lax.dot_general(
        combine_table.reshape(EXPERTS * CAP, tok_rows),
        returned.reshape(EXPERTS * CAP, local_width),
        TN,
        preferred_element_type=F32,
    )
    return mixed.astype(BF16)


def solution(mesh):
    placed = (
        P(("grp", "ep"), "tp"),
        P(("grp", "ep"), None),
        P(("grp", "ep"), None),
        P("ep", None, None, "tp"),
        P("ep", None, "tp"),
    )
    square = mesh.shape["ep"] == 4 and mesh.shape["tp"] == 4
    return jax.shard_map(
        local_square if square else local_general,
        mesh=mesh,
        in_specs=placed,
        out_specs=P(("grp", "ep"), "tp"),
        check_vma=False,
    )
```

```python
import functools

import jax
import jax.numpy as jnp
from jax import lax
from jax.experimental import pallas as pl
from jax.experimental.pallas import tpu as pltpu
from jax.sharding import PartitionSpec as P

EXPERTS = 32
TOPK = 6
CAP = 48
LANES = 128
BF16, F32 = jnp.bfloat16, jnp.float32
NT = (((1,), (1,)), ((), ()))
TN = (((0,), (0,)), ((), ()))
NN = (((1,), (0,)), ((), ()))

PAIR = [(0, 1), (1, 0), (2, 3), (3, 2)]
MIDDLE = [(1, 2), (2, 1)]
OUTWARD = [(1, 0), (2, 3)]
INWARD = [(0, 1), (3, 2)]
ACROSS_X = [(0, 2), (1, 3), (2, 0), (3, 1)]
ACROSS_CORE = [(0, 1), (1, 0), (2, 3), (3, 2)]


QUICK = pl.CostEstimate(flops=1024, bytes_accessed=1024, transcendentals=0)


SLOW = pl.CostEstimate(flops=20_000_000_000, bytes_accessed=1024, transcendentals=0)


def params(mib):
    return pltpu.CompilerParams(vmem_limit_bytes=mib << 20)


def route_kernel(ids_ref, gates_ref, out_ref):
    count = ids_ref.shape[1]
    expert = lax.broadcasted_iota(jnp.int32, (EXPERTS, count), 0)
    weight = jnp.zeros((EXPERTS, count), F32)
    chosen = jnp.zeros((EXPERTS, count), F32)
    for k in range(TOPK):
        hit = ids_ref[k : k + 1, :] == expert
        chosen = jnp.where(hit, 1.0, chosen)
        weight = jnp.where(hit, gates_ref[k : k + 1, :], weight)
    first = lax.broadcasted_iota(jnp.int32, (count, count), 0)
    second = lax.broadcasted_iota(jnp.int32, (count, count), 1)
    before = jnp.where(first < second, 1.0, 0.0).astype(BF16)
    position = lax.dot_general(chosen.astype(BF16), before, NN, preferred_element_type=F32)
    out_ref[:EXPERTS, :] = jnp.where(chosen > 0.0, position, -1.0)
    out_ref[EXPERTS:, :] = weight


def route(expert_ids, gate_weights):
    return pl.pallas_call(
        route_kernel,
        out_shape=jax.ShapeDtypeStruct((2 * EXPERTS, expert_ids.shape[0]), F32),
        name="route",
    )(expert_ids.T, gate_weights.T.astype(F32))


EXTRA = 16


def pack_kernel(tokens_ref, ids_ref, gates_ref, out_ref, sem):
    count, width = tokens_ref.shape
    lanes = count + -count % LANES
    copy = pltpu.make_async_copy(tokens_ref, out_ref.at[pl.ds(0, count)], sem)
    copy.start()
    out_ref[count:, :] = jnp.zeros((EXTRA, width), BF16)
    none = jnp.zeros((EXTRA - TOPK, count), F32)
    ids = jnp.concatenate([ids_ref[...].astype(F32), none], axis=0)
    gates = jnp.concatenate([gates_ref[...].astype(F32), none], axis=0)
    out_ref[count:, :count] = ids.astype(BF16)
    out_ref[count:, lanes : lanes + count] = gates.astype(BF16)
    copy.wait()


def pack(tokens, expert_ids, gate_weights):
    count, width = tokens.shape
    whole = pl.BlockSpec(memory_space=pltpu.VMEM)
    return pl.pallas_call(
        pack_kernel,
        out_shape=jax.ShapeDtypeStruct((count + EXTRA, width), BF16),
        in_specs=[pl.BlockSpec(memory_space=pl.ANY), whole, whole],
        out_specs=whole,
        scratch_shapes=[pltpu.SemaphoreType.DMA(())],
        compiler_params=params(8),
        cost_estimate=QUICK,
        name="pack",
    )(tokens, expert_ids.T, gate_weights.T)


def place_kernel(experts, where_ref, *refs):
    *message_refs, out_ref, table_ref = refs
    count = table_ref.shape[1]
    lanes = count + -count % LANES
    message = message_refs[0][...]
    for more in message_refs[1:]:
        message = message + more[...]
    ids = message[count:, :count].astype(F32)
    gates = message[count:, lanes : lanes + count].astype(F32)
    expert = lax.broadcasted_iota(jnp.int32, (experts, count), 0) + where_ref[0]
    expert = expert.astype(F32)
    weight = jnp.zeros((experts, count), F32)
    chosen = jnp.zeros((experts, count), F32)
    for k in range(TOPK):
        hit = ids[k : k + 1, :] == expert
        chosen = jnp.where(hit, 1.0, chosen)
        weight = jnp.where(hit, gates[k : k + 1, :], weight)
    first = lax.broadcasted_iota(jnp.int32, (count, count), 0)
    second = lax.broadcasted_iota(jnp.int32, (count, count), 1)
    before = jnp.where(first < second, 1.0, 0.0).astype(BF16)
    position = lax.dot_general(chosen.astype(BF16), before, NN, preferred_element_type=F32)
    position = jnp.where(chosen > 0.0, position, -1.0)
    table_ref[:experts, :] = position
    table_ref[experts:, :] = weight
    slot_of = lax.broadcasted_iota(jnp.int32, (CAP, count), 0).astype(F32)
    table = [jnp.where(position[e : e + 1, :] == slot_of, 1.0, 0.0) for e in range(experts)]
    table = jnp.concatenate(table, axis=0).astype(BF16)
    rows = lax.dot_general(table, message[:count], NN, preferred_element_type=F32).astype(BF16)
    for e in range(experts):
        out_ref[e] = rows[e * CAP : (e + 1) * CAP]


def place(where, messages, experts):
    whole = pl.BlockSpec(memory_space=pltpu.VMEM)
    length, width = messages[0].shape
    return pl.pallas_call(
        functools.partial(place_kernel, experts),
        out_shape=(
            jax.ShapeDtypeStruct((experts, CAP, width), BF16),
            jax.ShapeDtypeStruct((2 * experts, length - EXTRA), F32),
        ),
        in_specs=[pl.BlockSpec(memory_space=pltpu.SMEM)] + [whole] * len(messages),
        out_specs=(whole, whole),
        compiler_params=params(12),
        cost_estimate=QUICK,
        name="place",
    )(where, *messages)


def gate_up_kernel(n_blocks, where_ref, *refs):
    row_refs = refs[:n_blocks]
    w_ref, _, send_ref, keep_ref, rows_ref, carry = refs[n_blocks:]
    step = pl.program_id(0)
    rows = n_blocks * CAP
    spare = 2 * LANES - rows
    x, core = where_ref[1], where_ref[2]
    quarter = w_ref.shape[1] // 4

    @pl.when(step == 0)
    def _():
        rows_ref[...] = jnp.zeros_like(rows_ref)

    def product(parity):
        for i in range(n_blocks):
            at = parity * spare + i * CAP
            rows_ref[parity, at : at + CAP, :] = row_refs[i][0]
        w = w_ref[0].reshape(8 * quarter, w_ref.shape[3])
        return lax.dot_general(w, rows_ref[parity], NT, preferred_element_type=F32)

    def store(tile, lane):
        tile = tile.astype(BF16)
        for q in range(4):
            piece = tile[2 * q * quarter : 2 * (q + 1) * quarter]
            at = jnp.where(x == q // 2, 1, 0)

            @pl.when(core == q % 2)
            def _():
                keep_ref[at, :, lane : lane + LANES] = piece

            @pl.when(core != q % 2)
            def _():
                send_ref[at, :, lane : lane + LANES] = piece

    @pl.when(lax.rem(step, 2) == 0)
    def _():
        out = product(0)
        store(out[:, :LANES], 0)
        carry[...] = out[:, LANES:]

    @pl.when(lax.rem(step, 2) == 1)
    def _():
        out = product(1)
        store(carry[...] + out[:, :LANES], LANES)
        store(out[:, LANES:], 2 * LANES)


def gate_up(where, placed, gu_weight, chunk, group, after):
    _, units, _, width = gu_weight.shape
    n_blocks = len(placed)
    lanes = 2 * n_blocks * CAP
    half = jax.ShapeDtypeStruct((2, units // 2, group // 2 * lanes), BF16)
    pair = pl.BlockSpec((2, units // 2, lanes), lambda i: (0, 0, i // 2))
    return pl.pallas_call(
        functools.partial(gate_up_kernel, n_blocks),
        grid=(group,),
        out_shape=(half, half),
        in_specs=[pl.BlockSpec(memory_space=pltpu.SMEM)]
        + [pl.BlockSpec((1, CAP, width), lambda i: (chunk * group + i, 0, 0))] * n_blocks
        + [pl.BlockSpec((1, units, 2, width), lambda i: (chunk * group + i, 0, 0, 0))]
        + [pl.BlockSpec(memory_space=pl.ANY)],
        out_specs=(pair, pair),
        scratch_shapes=[
            pltpu.VMEM((2, 2 * LANES, width), BF16),
            pltpu.VMEM((2 * units, LANES), F32),
        ],
        compiler_params=params(28),
        cost_estimate=QUICK,
        name="gate_up",
    )(where, *placed, gu_weight, after)


def hidden_kernel(keep_ref, near_ref, far_ref, _, out_ref, sums):
    units = out_ref.shape[1]
    for n in range(sums.shape[0]):
        lanes = slice(n * LANES, (n + 1) * LANES)
        total = keep_ref[0, :, lanes].astype(F32) + near_ref[0, :, lanes].astype(F32)
        sums[n] = total + far_ref[:, lanes].astype(F32)
        gate = sums[n, pl.ds(0, units, stride=2), :]
        up = sums[n, pl.ds(1, units, stride=2), :]
        out_ref[lanes, :] = (gate / (1.0 + jnp.exp(-gate)) * up).T.astype(BF16)


def hidden_quarter(keep, near, far, after):
    _, doubled, columns = keep.shape
    mine = pl.BlockSpec((1, doubled, columns), lambda i: (1, 0, 0))
    return pl.pallas_call(
        hidden_kernel,
        grid=(1,),
        out_shape=jax.ShapeDtypeStruct((columns, doubled // 2), BF16),
        in_specs=[
            mine,
            mine,
            pl.BlockSpec((doubled, columns), lambda i: (0, 0)),
            pl.BlockSpec(memory_space=pl.ANY),
        ],
        out_specs=pl.BlockSpec((columns, doubled // 2), lambda i: (0, 0)),
        scratch_shapes=[pltpu.VMEM((columns // LANES, doubled, LANES), F32)],
        compiler_params=params(10),
        cost_estimate=SLOW,
        name="hidden",
    )(keep, near, far, after)


def add_kernel(keep_ref, near_ref, _, out_ref):
    out_ref[...] = (keep_ref[0].astype(F32) + near_ref[0].astype(F32)).astype(BF16)


def chip_sum(keep, near, after):
    _, doubled, columns = keep.shape
    other = pl.BlockSpec((1, doubled, columns), lambda i: (0, 0, 0))
    return pl.pallas_call(
        add_kernel,
        grid=(1,),
        out_shape=jax.ShapeDtypeStruct((doubled, columns), BF16),
        in_specs=[other, other, pl.BlockSpec(memory_space=pl.ANY)],
        out_specs=pl.BlockSpec((doubled, columns), lambda i: (0, 0)),
        compiler_params=params(8),
        cost_estimate=QUICK,
        name="chip_sum",
    )(keep, near, after)


def down_kernel(group, n_blocks, chunk, has_carry, where_ref, *refs):
    hidden_refs, refs = refs[:4], refs[4:]
    route_refs, refs = refs[:n_blocks], refs[n_blocks:]
    w_hbm, refs = refs[0], refs[2:]
    carry_ref, refs = (refs[0], refs[1:]) if has_carry else (None, refs)
    out_refs, (held, w_buf, sems) = refs[:-3], refs[-3:]
    rows = n_blocks * CAP
    quarter = w_hbm.shape[1] // 4
    count = route_refs[0].shape[1]
    local = w_hbm.shape[0]
    x, core = where_ref[1], where_ref[2]
    order = [(x, core), (1 - x, core), (x, 1 - core), (1 - x, 1 - core)]

    def fetch(e):
        copies = []
        for j in range(4):
            f0 = pl.multiple_of((order[j][0] * 2 + order[j][1]) * quarter, quarter)
            copies.append(
                pltpu.make_async_copy(
                    w_hbm.at[chunk * group + e, pl.ds(f0, quarter)],
                    w_buf.at[e, pl.ds(j * quarter, quarter)],
                    sems.at[e, j],
                )
            )
        return copies

    def start(e):
        for copy in fetch(e):
            copy.start()

    start(0)
    start(1)
    for e in range(group):
        for copy in fetch(e):
            copy.wait()
        if e + 2 < group:
            start(e + 2)
        units = jnp.concatenate([h[e * rows : (e + 1) * rows, :] for h in hidden_refs], axis=1)
        out = lax.dot_general(units, w_buf[e], NN, preferred_element_type=F32).astype(BF16)
        for i in range(n_blocks):
            held[i, e * CAP : (e + 1) * CAP, :] = out[i * CAP : (i + 1) * CAP]
    slot_of = lax.broadcasted_iota(jnp.int32, (CAP, count), 0).astype(F32)
    for i in range(n_blocks):
        table = [
            jnp.where(
                route_refs[i][chunk * group + e : chunk * group + e + 1, :] == slot_of,
                route_refs[i][local + chunk * group + e : local + chunk * group + e + 1, :],
                0.0,
            )
            for e in range(group)
        ]
        table = jnp.concatenate(table, axis=0).astype(BF16)
        total = lax.dot_general(table, held[i], TN, preferred_element_type=F32)
        if has_carry:
            out_refs[i][...] = (total + carry_ref[i]).astype(BF16)
        else:
            out_refs[0][i] = total


def down(where, hidden, routes, down_weight, chunk, group, carry, after):
    n_blocks = len(routes)
    units = hidden[0].shape[1]
    count = routes[0].shape[1]
    width = down_weight.shape[2]
    whole = pl.BlockSpec(memory_space=pltpu.VMEM)
    carried = [] if carry is None else [carry]
    if carry is None:
        out_shape = (jax.ShapeDtypeStruct((n_blocks, count, width), F32),)
    else:
        out_shape = tuple(jax.ShapeDtypeStruct((count, width), BF16) for _ in routes)
    return pl.pallas_call(
        functools.partial(down_kernel, group, n_blocks, chunk, carry is not None),
        out_shape=out_shape,
        in_specs=[pl.BlockSpec(memory_space=pltpu.SMEM)]
        + [whole] * (4 + n_blocks)
        + [pl.BlockSpec(memory_space=pl.ANY)] * 2
        + [whole] * len(carried),
        out_specs=tuple(whole for _ in out_shape),
        scratch_shapes=[
            pltpu.VMEM((n_blocks, group * CAP, width), BF16),
            pltpu.VMEM((group, 4 * units, width), BF16),
            pltpu.SemaphoreType.DMA((group, 4)),
        ],
        compiler_params=params(28),
        cost_estimate=QUICK,
        name="down",
    )(where, *hidden, *routes, down_weight, after, *carried)


def plus_kernel(a_ref, b_ref, _, out_ref, __):
    out_ref[...] = (a_ref[...].astype(F32) + b_ref[...].astype(F32)).astype(BF16)


def plus_then(a, b, other):
    whole = pl.BlockSpec(memory_space=pltpu.VMEM)
    free = pl.BlockSpec(memory_space=pl.ANY)
    return pl.pallas_call(
        plus_kernel,
        out_shape=(jax.ShapeDtypeStruct(a.shape, a.dtype), jax.ShapeDtypeStruct(a.shape, a.dtype)),
        in_specs=[whole, whole, free],
        out_specs=(whole, free),
        input_output_aliases={2: 1},
        compiler_params=params(4),
        cost_estimate=QUICK,
        name="plus",
    )(a, b, other)


def local_square(tokens, expert_ids, gate_weights, gu_weight, down_weight):
    z, t = lax.axis_index("ep"), lax.axis_index("tp")
    x, core = t // 2, t % 2
    local = gu_weight.shape[0]
    group = local // 2
    where = jnp.stack([z * local, x, core]).astype(jnp.int32)

    def hop(array, pairs):
        return lax.ppermute(array, "ep", pairs)

    message = pack(tokens, expert_ids, gate_weights)
    neighbour = hop(message, PAIR)
    middle_1 = hop(message, MIDDLE)
    middle_2 = hop(neighbour, MIDDLE)
    end_1 = hop(middle_1, OUTWARD)
    end_2 = hop(middle_2, OUTWARD)
    blocks = [(message,), (neighbour,), (middle_1, end_1), (middle_2, end_2)]
    placed, tables = zip(*(place(where, b, local) for b in blocks))

    def sums(n, after):
        send, keep = gate_up(where, placed, gu_weight, n, group, after)
        return keep, lax.ppermute(send, "tp", ACROSS_CORE)

    def across(keep, near, after):
        total = chip_sum(keep, near, after)
        return total, lax.ppermute(total, "tp", ACROSS_X)

    def gathered(own):
        own_x = lax.ppermute(own, "tp", ACROSS_X)
        own_core = lax.ppermute(own, "tp", ACROSS_CORE)
        return own, own_x, own_core, lax.ppermute(own_x, "tp", ACROSS_CORE)

    keep_0, near_0 = sums(0, placed[3])
    turn, far_0 = across(keep_0, near_0, keep_0)
    keep_1, near_1 = sums(1, turn)
    own_0 = hidden_quarter(keep_0, near_0, far_0, keep_1)
    hidden_0 = gathered(own_0)
    turn, far_1 = across(keep_1, near_1, own_0)
    (carry,) = down(where, hidden_0, tables, down_weight, 0, group, None, turn)
    own_1 = hidden_quarter(keep_1, near_1, far_1, carry)
    hidden_1 = gathered(own_1)
    own, other, far_in, far_out = down(
        where, hidden_1, tables, down_weight, 1, group, carry, own_1
    )

    def plus(a, b):
        return (a.astype(F32) + b.astype(F32)).astype(BF16)

    out_inner = hop(far_out, INWARD)
    far_out, far_in = plus_then(far_out, out_inner, far_in)
    out_mid = hop(far_out, MIDDLE)
    in_inner = hop(far_in, INWARD)
    last = hop(plus(other, out_mid), PAIR)
    in_mid = hop(plus(far_in, in_inner), MIDDLE)
    return (own.astype(F32) + in_mid.astype(F32) + last.astype(F32)).astype(BF16)


def local_general(tokens, expert_ids, gate_weights, gu_weight, down_weight):
    tok_rows, local_width = tokens.shape
    table = route(expert_ids, gate_weights)
    slots = jnp.arange(CAP, dtype=jnp.int32).astype(F32)
    matches = table[:EXPERTS, None, :] == slots[None, :, None]
    dispatch_table = matches.astype(BF16).reshape(EXPERTS * CAP, tok_rows)
    outgoing = jnp.dot(dispatch_table, tokens, preferred_element_type=F32)
    outgoing = outgoing.astype(BF16).reshape(EXPERTS, CAP, local_width)
    received = lax.all_to_all(outgoing, "ep", split_axis=0, concat_axis=1, tiled=True)
    terms = jnp.einsum("efgd,esd->fegs", gu_weight, received, preferred_element_type=F32)
    totals = lax.psum(terms.astype(BF16), "tp").astype(F32)
    hidden = (jax.nn.silu(totals[:, :, 0]) * totals[:, :, 1]).astype(BF16)
    expert_out = jnp.einsum("fes,efd->esd", hidden, down_weight, preferred_element_type=F32)
    returned = lax.all_to_all(
        expert_out.astype(BF16), "ep", split_axis=1, concat_axis=0, tiled=True
    )
    combine_table = jnp.where(matches, table[EXPERTS:, None, :], 0.0).astype(BF16)
    mixed = lax.dot_general(
        combine_table.reshape(EXPERTS * CAP, tok_rows),
        returned.reshape(EXPERTS * CAP, local_width),
        TN,
        preferred_element_type=F32,
    )
    return mixed.astype(BF16)


def solution(mesh):
    placed = (
        P(("grp", "ep"), "tp"),
        P(("grp", "ep"), None),
        P(("grp", "ep"), None),
        P("ep", None, None, "tp"),
        P("ep", None, "tp"),
    )
    square = mesh.shape["ep"] == 4 and mesh.shape["tp"] == 4
    return jax.shard_map(
        local_square if square else local_general,
        mesh=mesh,
        in_specs=placed,
        out_specs=P(("grp", "ep"), "tp"),
        check_vma=False,
    )
```

```python
import functools

import jax
import jax.numpy as jnp
from jax import lax
from jax.experimental import pallas as pl
from jax.experimental.pallas import tpu as pltpu
from jax.sharding import PartitionSpec as P

EXPERTS = 32
TOPK = 6
CAP = 48
LANES = 128
BF16, F32 = jnp.bfloat16, jnp.float32
NT = (((1,), (1,)), ((), ()))
TN = (((0,), (0,)), ((), ()))
NN = (((1,), (0,)), ((), ()))

PAIR = [(0, 1), (1, 0), (2, 3), (3, 2)]
MIDDLE = [(1, 2), (2, 1)]
OUTWARD = [(1, 0), (2, 3)]
INWARD = [(0, 1), (3, 2)]
ACROSS_X = [(0, 2), (1, 3), (2, 0), (3, 1)]
ACROSS_CORE = [(0, 1), (1, 0), (2, 3), (3, 2)]


QUICK = pl.CostEstimate(flops=1024, bytes_accessed=1024, transcendentals=0)


SLOW = pl.CostEstimate(flops=20_000_000_000, bytes_accessed=1024, transcendentals=0)


def params(mib):
    return pltpu.CompilerParams(vmem_limit_bytes=mib << 20)


def route_kernel(ids_ref, gates_ref, out_ref):
    count = ids_ref.shape[1]
    expert = lax.broadcasted_iota(jnp.int32, (EXPERTS, count), 0)
    weight = jnp.zeros((EXPERTS, count), F32)
    chosen = jnp.zeros((EXPERTS, count), F32)
    for k in range(TOPK):
        hit = ids_ref[k : k + 1, :] == expert
        chosen = jnp.where(hit, 1.0, chosen)
        weight = jnp.where(hit, gates_ref[k : k + 1, :], weight)
    first = lax.broadcasted_iota(jnp.int32, (count, count), 0)
    second = lax.broadcasted_iota(jnp.int32, (count, count), 1)
    before = jnp.where(first < second, 1.0, 0.0).astype(BF16)
    position = lax.dot_general(chosen.astype(BF16), before, NN, preferred_element_type=F32)
    out_ref[:EXPERTS, :] = jnp.where(chosen > 0.0, position, -1.0)
    out_ref[EXPERTS:, :] = weight


def route(expert_ids, gate_weights):
    return pl.pallas_call(
        route_kernel,
        out_shape=jax.ShapeDtypeStruct((2 * EXPERTS, expert_ids.shape[0]), F32),
        name="route",
    )(expert_ids.T, gate_weights.T.astype(F32))


EXTRA = 16


def pack_kernel(tokens_ref, extra_ref, out_ref):
    count, lanes = tokens_ref.shape[0], extra_ref.shape[1]
    out_ref[:count, :] = tokens_ref[...]
    out_ref[count:, lanes:] = jnp.zeros((EXTRA, out_ref.shape[1] - lanes), BF16)
    out_ref[count:, :lanes] = extra_ref[...]


def pack(tokens, expert_ids, gate_weights):
    count, width = tokens.shape
    spare = -count % LANES
    extra = [
        jnp.pad(a.T.astype(BF16), ((0, EXTRA - TOPK), (0, spare)))
        for a in (expert_ids, gate_weights)
    ]
    return pl.pallas_call(
        pack_kernel,
        out_shape=jax.ShapeDtypeStruct((count + EXTRA, width), BF16),
        compiler_params=params(8),
        cost_estimate=QUICK,
        name="pack",
    )(tokens, jnp.concatenate(extra, axis=1))


def place_kernel(experts, where_ref, *refs):
    *message_refs, out_ref, table_ref = refs
    count = table_ref.shape[1]
    lanes = count + -count % LANES
    message = message_refs[0][...]
    for more in message_refs[1:]:
        message = message + more[...]
    ids = message[count:, :count].astype(F32)
    gates = message[count:, lanes : lanes + count].astype(F32)
    expert = lax.broadcasted_iota(jnp.int32, (experts, count), 0) + where_ref[0]
    expert = expert.astype(F32)
    weight = jnp.zeros((experts, count), F32)
    chosen = jnp.zeros((experts, count), F32)
    for k in range(TOPK):
        hit = ids[k : k + 1, :] == expert
        chosen = jnp.where(hit, 1.0, chosen)
        weight = jnp.where(hit, gates[k : k + 1, :], weight)
    first = lax.broadcasted_iota(jnp.int32, (count, count), 0)
    second = lax.broadcasted_iota(jnp.int32, (count, count), 1)
    before = jnp.where(first < second, 1.0, 0.0).astype(BF16)
    position = lax.dot_general(chosen.astype(BF16), before, NN, preferred_element_type=F32)
    position = jnp.where(chosen > 0.0, position, -1.0)
    table_ref[:experts, :] = position
    table_ref[experts:, :] = weight
    slot_of = lax.broadcasted_iota(jnp.int32, (CAP, count), 0).astype(F32)
    table = [jnp.where(position[e : e + 1, :] == slot_of, 1.0, 0.0) for e in range(experts)]
    table = jnp.concatenate(table, axis=0).astype(BF16)
    rows = lax.dot_general(table, message[:count], NN, preferred_element_type=F32).astype(BF16)
    for e in range(experts):
        out_ref[e] = rows[e * CAP : (e + 1) * CAP]


def place(where, messages, experts):
    whole = pl.BlockSpec(memory_space=pltpu.VMEM)
    length, width = messages[0].shape
    return pl.pallas_call(
        functools.partial(place_kernel, experts),
        out_shape=(
            jax.ShapeDtypeStruct((experts, CAP, width), BF16),
            jax.ShapeDtypeStruct((2 * experts, length - EXTRA), F32),
        ),
        in_specs=[pl.BlockSpec(memory_space=pltpu.SMEM)] + [whole] * len(messages),
        out_specs=(whole, whole),
        compiler_params=params(12),
        cost_estimate=QUICK,
        name="place",
    )(where, *messages)


def gate_up_kernel(n_blocks, where_ref, *refs):
    row_refs = refs[:n_blocks]
    w_ref, _, send_ref, keep_ref, rows_ref, carry = refs[n_blocks:]
    step = pl.program_id(0)
    rows = n_blocks * CAP
    spare = 2 * LANES - rows
    x, core = where_ref[1], where_ref[2]
    quarter = w_ref.shape[1] // 4

    @pl.when(step == 0)
    def _():
        rows_ref[...] = jnp.zeros_like(rows_ref)

    def product(parity):
        for i in range(n_blocks):
            at = parity * spare + i * CAP
            rows_ref[parity, at : at + CAP, :] = row_refs[i][0]
        w = w_ref[0].reshape(8 * quarter, w_ref.shape[3])
        return lax.dot_general(w, rows_ref[parity], NT, preferred_element_type=F32)

    def store(tile, lane):
        tile = tile.astype(BF16)
        for q in range(4):
            piece = tile[2 * q * quarter : 2 * (q + 1) * quarter]
            at = jnp.where(x == q // 2, 1, 0)

            @pl.when(core == q % 2)
            def _():
                keep_ref[at, :, lane : lane + LANES] = piece

            @pl.when(core != q % 2)
            def _():
                send_ref[at, :, lane : lane + LANES] = piece

    @pl.when(lax.rem(step, 2) == 0)
    def _():
        out = product(0)
        store(out[:, :LANES], 0)
        carry[...] = out[:, LANES:]

    @pl.when(lax.rem(step, 2) == 1)
    def _():
        out = product(1)
        store(carry[...] + out[:, :LANES], LANES)
        store(out[:, LANES:], 2 * LANES)


def gate_up(where, placed, gu_weight, chunk, group, after):
    _, units, _, width = gu_weight.shape
    n_blocks = len(placed)
    lanes = 2 * n_blocks * CAP
    half = jax.ShapeDtypeStruct((2, units // 2, group // 2 * lanes), BF16)
    pair = pl.BlockSpec((2, units // 2, lanes), lambda i: (0, 0, i // 2))
    return pl.pallas_call(
        functools.partial(gate_up_kernel, n_blocks),
        grid=(group,),
        out_shape=(half, half),
        in_specs=[pl.BlockSpec(memory_space=pltpu.SMEM)]
        + [pl.BlockSpec((1, CAP, width), lambda i: (chunk * group + i, 0, 0))] * n_blocks
        + [pl.BlockSpec((1, units, 2, width), lambda i: (chunk * group + i, 0, 0, 0))]
        + [pl.BlockSpec(memory_space=pl.ANY)],
        out_specs=(pair, pair),
        scratch_shapes=[
            pltpu.VMEM((2, 2 * LANES, width), BF16),
            pltpu.VMEM((2 * units, LANES), F32),
        ],
        compiler_params=params(28),
        cost_estimate=QUICK,
        name="gate_up",
    )(where, *placed, gu_weight, after)


def hidden_kernel(keep_ref, near_ref, far_ref, _, out_ref, sums):
    units = out_ref.shape[1]
    for n in range(sums.shape[0]):
        lanes = slice(n * LANES, (n + 1) * LANES)
        total = keep_ref[0, :, lanes].astype(F32) + near_ref[0, :, lanes].astype(F32)
        sums[n] = total + far_ref[:, lanes].astype(F32)
        gate = sums[n, pl.ds(0, units, stride=2), :]
        up = sums[n, pl.ds(1, units, stride=2), :]
        out_ref[lanes, :] = (gate / (1.0 + jnp.exp(-gate)) * up).T.astype(BF16)


def hidden_quarter(keep, near, far, after):
    _, doubled, columns = keep.shape
    mine = pl.BlockSpec((1, doubled, columns), lambda i: (1, 0, 0))
    return pl.pallas_call(
        hidden_kernel,
        grid=(1,),
        out_shape=jax.ShapeDtypeStruct((columns, doubled // 2), BF16),
        in_specs=[
            mine,
            mine,
            pl.BlockSpec((doubled, columns), lambda i: (0, 0)),
            pl.BlockSpec(memory_space=pl.ANY),
        ],
        out_specs=pl.BlockSpec((columns, doubled // 2), lambda i: (0, 0)),
        scratch_shapes=[pltpu.VMEM((columns // LANES, doubled, LANES), F32)],
        compiler_params=params(10),
        cost_estimate=SLOW,
        name="hidden",
    )(keep, near, far, after)


def add_kernel(keep_ref, near_ref, _, out_ref):
    out_ref[...] = (keep_ref[0].astype(F32) + near_ref[0].astype(F32)).astype(BF16)


def chip_sum(keep, near, after):
    _, doubled, columns = keep.shape
    other = pl.BlockSpec((1, doubled, columns), lambda i: (0, 0, 0))
    return pl.pallas_call(
        add_kernel,
        grid=(1,),
        out_shape=jax.ShapeDtypeStruct((doubled, columns), BF16),
        in_specs=[other, other, pl.BlockSpec(memory_space=pl.ANY)],
        out_specs=pl.BlockSpec((doubled, columns), lambda i: (0, 0)),
        compiler_params=params(8),
        cost_estimate=QUICK,
        name="chip_sum",
    )(keep, near, after)


def down_kernel(group, n_blocks, chunk, has_carry, where_ref, *refs):
    hidden_refs, refs = refs[:4], refs[4:]
    route_refs, refs = refs[:n_blocks], refs[n_blocks:]
    w_hbm, refs = refs[0], refs[2:]
    carry_ref, refs = (refs[0], refs[1:]) if has_carry else (None, refs)
    out_refs, (held, w_buf, sems) = refs[:-3], refs[-3:]
    rows = n_blocks * CAP
    quarter = w_hbm.shape[1] // 4
    count = route_refs[0].shape[1]
    local = w_hbm.shape[0]
    x, core = where_ref[1], where_ref[2]
    order = [(x, core), (1 - x, core), (x, 1 - core), (1 - x, 1 - core)]

    def fetch(e):
        copies = []
        for j in range(4):
            f0 = pl.multiple_of((order[j][0] * 2 + order[j][1]) * quarter, quarter)
            copies.append(
                pltpu.make_async_copy(
                    w_hbm.at[chunk * group + e, pl.ds(f0, quarter)],
                    w_buf.at[e, pl.ds(j * quarter, quarter)],
                    sems.at[e, j],
                )
            )
        return copies

    def start(e):
        for copy in fetch(e):
            copy.start()

    start(0)
    start(1)
    for e in range(group):
        for copy in fetch(e):
            copy.wait()
        if e + 2 < group:
            start(e + 2)
        units = jnp.concatenate([h[e * rows : (e + 1) * rows, :] for h in hidden_refs], axis=1)
        out = lax.dot_general(units, w_buf[e], NN, preferred_element_type=F32).astype(BF16)
        for i in range(n_blocks):
            held[i, e * CAP : (e + 1) * CAP, :] = out[i * CAP : (i + 1) * CAP]
    slot_of = lax.broadcasted_iota(jnp.int32, (CAP, count), 0).astype(F32)
    for i in range(n_blocks):
        table = [
            jnp.where(
                route_refs[i][chunk * group + e : chunk * group + e + 1, :] == slot_of,
                route_refs[i][local + chunk * group + e : local + chunk * group + e + 1, :],
                0.0,
            )
            for e in range(group)
        ]
        table = jnp.concatenate(table, axis=0).astype(BF16)
        total = lax.dot_general(table, held[i], TN, preferred_element_type=F32)
        if has_carry:
            out_refs[i][...] = (total + carry_ref[i]).astype(BF16)
        else:
            out_refs[0][i] = total


def down(where, hidden, routes, down_weight, chunk, group, carry, after):
    n_blocks = len(routes)
    units = hidden[0].shape[1]
    count = routes[0].shape[1]
    width = down_weight.shape[2]
    whole = pl.BlockSpec(memory_space=pltpu.VMEM)
    carried = [] if carry is None else [carry]
    if carry is None:
        out_shape = (jax.ShapeDtypeStruct((n_blocks, count, width), F32),)
    else:
        out_shape = tuple(jax.ShapeDtypeStruct((count, width), BF16) for _ in routes)
    return pl.pallas_call(
        functools.partial(down_kernel, group, n_blocks, chunk, carry is not None),
        out_shape=out_shape,
        in_specs=[pl.BlockSpec(memory_space=pltpu.SMEM)]
        + [whole] * (4 + n_blocks)
        + [pl.BlockSpec(memory_space=pl.ANY)] * 2
        + [whole] * len(carried),
        out_specs=tuple(whole for _ in out_shape),
        scratch_shapes=[
            pltpu.VMEM((n_blocks, group * CAP, width), BF16),
            pltpu.VMEM((group, 4 * units, width), BF16),
            pltpu.SemaphoreType.DMA((group, 4)),
        ],
        compiler_params=params(28),
        cost_estimate=QUICK,
        name="down",
    )(where, *hidden, *routes, down_weight, after, *carried)


def local_square(tokens, expert_ids, gate_weights, gu_weight, down_weight):
    z, t = lax.axis_index("ep"), lax.axis_index("tp")
    x, core = t // 2, t % 2
    local = gu_weight.shape[0]
    group = local // 2
    where = jnp.stack([z * local, x, core]).astype(jnp.int32)

    def hop(array, pairs):
        return lax.ppermute(array, "ep", pairs)

    message = pack(tokens, expert_ids, gate_weights)
    neighbour = hop(message, PAIR)
    middle_1 = hop(message, MIDDLE)
    middle_2 = hop(neighbour, MIDDLE)
    end_1 = hop(middle_1, OUTWARD)
    end_2 = hop(middle_2, OUTWARD)
    blocks = [(message,), (neighbour,), (middle_1, end_1), (middle_2, end_2)]
    placed, tables = zip(*(place(where, b, local) for b in blocks))

    def sums(n, after):
        send, keep = gate_up(where, placed, gu_weight, n, group, after)
        return keep, lax.ppermute(send, "tp", ACROSS_CORE)

    def across(keep, near, after):
        total = chip_sum(keep, near, after)
        return total, lax.ppermute(total, "tp", ACROSS_X)

    def gathered(own):
        own_x = lax.ppermute(own, "tp", ACROSS_X)
        own_core = lax.ppermute(own, "tp", ACROSS_CORE)
        return own, own_x, own_core, lax.ppermute(own_x, "tp", ACROSS_CORE)

    keep_0, near_0 = sums(0, placed[3])
    turn, far_0 = across(keep_0, near_0, keep_0)
    keep_1, near_1 = sums(1, turn)
    own_0 = hidden_quarter(keep_0, near_0, far_0, keep_1)
    hidden_0 = gathered(own_0)
    turn, far_1 = across(keep_1, near_1, own_0)
    (carry,) = down(where, hidden_0, tables, down_weight, 0, group, None, turn)
    own_1 = hidden_quarter(keep_1, near_1, far_1, carry)
    hidden_1 = gathered(own_1)
    own, other, far_in, far_out = down(
        where, hidden_1, tables, down_weight, 1, group, carry, own_1
    )

    def plus(a, b):
        return (a.astype(F32) + b.astype(F32)).astype(BF16)

    out_inner = hop(far_out, INWARD)
    in_inner = hop(far_in, INWARD)
    out_mid = hop(plus(far_out, out_inner), MIDDLE)
    last = hop(plus(other, out_mid), PAIR)
    in_mid = hop(plus(far_in, in_inner), MIDDLE)
    return (own.astype(F32) + in_mid.astype(F32) + last.astype(F32)).astype(BF16)


def local_general(tokens, expert_ids, gate_weights, gu_weight, down_weight):
    tok_rows, local_width = tokens.shape
    table = route(expert_ids, gate_weights)
    slots = jnp.arange(CAP, dtype=jnp.int32).astype(F32)
    matches = table[:EXPERTS, None, :] == slots[None, :, None]
    dispatch_table = matches.astype(BF16).reshape(EXPERTS * CAP, tok_rows)
    outgoing = jnp.dot(dispatch_table, tokens, preferred_element_type=F32)
    outgoing = outgoing.astype(BF16).reshape(EXPERTS, CAP, local_width)
    received = lax.all_to_all(outgoing, "ep", split_axis=0, concat_axis=1, tiled=True)
    terms = jnp.einsum("efgd,esd->fegs", gu_weight, received, preferred_element_type=F32)
    totals = lax.psum(terms.astype(BF16), "tp").astype(F32)
    hidden = (jax.nn.silu(totals[:, :, 0]) * totals[:, :, 1]).astype(BF16)
    expert_out = jnp.einsum("fes,efd->esd", hidden, down_weight, preferred_element_type=F32)
    returned = lax.all_to_all(
        expert_out.astype(BF16), "ep", split_axis=1, concat_axis=0, tiled=True
    )
    combine_table = jnp.where(matches, table[EXPERTS:, None, :], 0.0).astype(BF16)
    mixed = lax.dot_general(
        combine_table.reshape(EXPERTS * CAP, tok_rows),
        returned.reshape(EXPERTS * CAP, local_width),
        TN,
        preferred_element_type=F32,
    )
    return mixed.astype(BF16)


def solution(mesh):
    placed = (
        P(("grp", "ep"), "tp"),
        P(("grp", "ep"), None),
        P(("grp", "ep"), None),
        P("ep", None, None, "tp"),
        P("ep", None, "tp"),
    )
    square = mesh.shape["ep"] == 4 and mesh.shape["tp"] == 4
    return jax.shard_map(
        local_square if square else local_general,
        mesh=mesh,
        in_specs=placed,
        out_specs=P(("grp", "ep"), "tp"),
        check_vma=False,
    )
```

```python
import functools

import jax
import jax.numpy as jnp
from jax import lax
from jax.experimental import pallas as pl
from jax.experimental.pallas import tpu as pltpu
from jax.sharding import PartitionSpec as P

EXPERTS = 32
TOPK = 6
CAP = 48
LANES = 128
BF16, F32 = jnp.bfloat16, jnp.float32
NT = (((1,), (1,)), ((), ()))
TN = (((0,), (0,)), ((), ()))
NN = (((1,), (0,)), ((), ()))

PAIR = [(0, 1), (1, 0), (2, 3), (3, 2)]
MIDDLE = [(1, 2), (2, 1)]
OUTWARD = [(1, 0), (2, 3)]
INWARD = [(0, 1), (3, 2)]
ACROSS_X = [(0, 2), (1, 3), (2, 0), (3, 1)]
ACROSS_CORE = [(0, 1), (1, 0), (2, 3), (3, 2)]


QUICK = pl.CostEstimate(flops=1024, bytes_accessed=1024, transcendentals=0)


SLOW = pl.CostEstimate(flops=20_000_000_000, bytes_accessed=1024, transcendentals=0)


def params(mib):
    return pltpu.CompilerParams(vmem_limit_bytes=mib << 20)


def route_kernel(ids_ref, gates_ref, out_ref):
    count = ids_ref.shape[1]
    expert = lax.broadcasted_iota(jnp.int32, (EXPERTS, count), 0)
    weight = jnp.zeros((EXPERTS, count), F32)
    chosen = jnp.zeros((EXPERTS, count), F32)
    for k in range(TOPK):
        hit = ids_ref[k : k + 1, :] == expert
        chosen = jnp.where(hit, 1.0, chosen)
        weight = jnp.where(hit, gates_ref[k : k + 1, :], weight)
    first = lax.broadcasted_iota(jnp.int32, (count, count), 0)
    second = lax.broadcasted_iota(jnp.int32, (count, count), 1)
    before = jnp.where(first < second, 1.0, 0.0).astype(BF16)
    position = lax.dot_general(chosen.astype(BF16), before, NN, preferred_element_type=F32)
    out_ref[:EXPERTS, :] = jnp.where(chosen > 0.0, position, -1.0)
    out_ref[EXPERTS:, :] = weight


def route(expert_ids, gate_weights):
    return pl.pallas_call(
        route_kernel,
        out_shape=jax.ShapeDtypeStruct((2 * EXPERTS, expert_ids.shape[0]), F32),
        name="route",
    )(expert_ids.T, gate_weights.T.astype(F32))


EXTRA = 16


def pack_kernel(tokens_ref, ids_ref, gates_ref, out_ref, sem):
    count, width = tokens_ref.shape
    lanes = count + -count % LANES
    copy = pltpu.make_async_copy(tokens_ref, out_ref.at[pl.ds(0, count)], sem)
    copy.start()
    out_ref[count:, :] = jnp.zeros((EXTRA, width), BF16)
    none = jnp.zeros((EXTRA - TOPK, count), F32)
    ids = jnp.concatenate([ids_ref[...].astype(F32), none], axis=0)
    gates = jnp.concatenate([gates_ref[...].astype(F32), none], axis=0)
    out_ref[count:, :count] = ids.astype(BF16)
    out_ref[count:, lanes : lanes + count] = gates.astype(BF16)
    copy.wait()


def pack(tokens, expert_ids, gate_weights):
    count, width = tokens.shape
    whole = pl.BlockSpec(memory_space=pltpu.VMEM)
    return pl.pallas_call(
        pack_kernel,
        out_shape=jax.ShapeDtypeStruct((count + EXTRA, width), BF16),
        in_specs=[pl.BlockSpec(memory_space=pl.ANY), whole, whole],
        out_specs=whole,
        scratch_shapes=[pltpu.SemaphoreType.DMA(())],
        compiler_params=params(8),
        cost_estimate=QUICK,
        name="pack",
    )(tokens, expert_ids.T, gate_weights.T)


def place_kernel(experts, where_ref, *refs):
    *message_refs, out_ref, table_ref = refs
    count = table_ref.shape[1]
    lanes = count + -count % LANES
    message = message_refs[0][...]
    for more in message_refs[1:]:
        message = message + more[...]
    ids = message[count:, :count].astype(F32)
    gates = message[count:, lanes : lanes + count].astype(F32)
    expert = lax.broadcasted_iota(jnp.int32, (experts, count), 0) + where_ref[0]
    expert = expert.astype(F32)
    weight = jnp.zeros((experts, count), F32)
    chosen = jnp.zeros((experts, count), F32)
    for k in range(TOPK):
        hit = ids[k : k + 1, :] == expert
        chosen = jnp.where(hit, 1.0, chosen)
        weight = jnp.where(hit, gates[k : k + 1, :], weight)
    first = lax.broadcasted_iota(jnp.int32, (count, count), 0)
    second = lax.broadcasted_iota(jnp.int32, (count, count), 1)
    before = jnp.where(first < second, 1.0, 0.0).astype(BF16)
    position = lax.dot_general(chosen.astype(BF16), before, NN, preferred_element_type=F32)
    position = jnp.where(chosen > 0.0, position, -1.0)
    table_ref[:experts, :] = position
    table_ref[experts:, :] = weight
    slot_of = lax.broadcasted_iota(jnp.int32, (CAP, count), 0).astype(F32)
    table = [jnp.where(position[e : e + 1, :] == slot_of, 1.0, 0.0) for e in range(experts)]
    table = jnp.concatenate(table, axis=0).astype(BF16)
    rows = lax.dot_general(table, message[:count], NN, preferred_element_type=F32).astype(BF16)
    for e in range(experts):
        out_ref[e] = rows[e * CAP : (e + 1) * CAP]


def place(where, messages, experts):
    whole = pl.BlockSpec(memory_space=pltpu.VMEM)
    length, width = messages[0].shape
    return pl.pallas_call(
        functools.partial(place_kernel, experts),
        out_shape=(
            jax.ShapeDtypeStruct((experts, CAP, width), BF16),
            jax.ShapeDtypeStruct((2 * experts, length - EXTRA), F32),
        ),
        in_specs=[pl.BlockSpec(memory_space=pltpu.SMEM)] + [whole] * len(messages),
        out_specs=(whole, whole),
        compiler_params=params(12),
        cost_estimate=QUICK,
        name="place",
    )(where, *messages)


def gate_up_kernel(n_blocks, where_ref, *refs):
    row_refs = refs[:n_blocks]
    w_ref, _, send_ref, keep_ref, rows_ref, carry = refs[n_blocks:]
    step = pl.program_id(0)
    rows = n_blocks * CAP
    spare = 2 * LANES - rows
    x, core = where_ref[1], where_ref[2]
    quarter = w_ref.shape[1] // 4

    @pl.when(step == 0)
    def _():
        rows_ref[...] = jnp.zeros_like(rows_ref)

    def product(parity):
        for i in range(n_blocks):
            at = parity * spare + i * CAP
            rows_ref[parity, at : at + CAP, :] = row_refs[i][0]
        w = w_ref[0].reshape(8 * quarter, w_ref.shape[3])
        return lax.dot_general(w, rows_ref[parity], NT, preferred_element_type=F32)

    def store(tile, lane):
        tile = tile.astype(BF16)
        for q in range(4):
            piece = tile[2 * q * quarter : 2 * (q + 1) * quarter]
            at = jnp.where(x == q // 2, 1, 0)

            @pl.when(core == q % 2)
            def _():
                keep_ref[at, :, lane : lane + LANES] = piece

            @pl.when(core != q % 2)
            def _():
                send_ref[at, :, lane : lane + LANES] = piece

    @pl.when(lax.rem(step, 2) == 0)
    def _():
        out = product(0)
        store(out[:, :LANES], 0)
        carry[...] = out[:, LANES:]

    @pl.when(lax.rem(step, 2) == 1)
    def _():
        out = product(1)
        store(carry[...] + out[:, :LANES], LANES)
        store(out[:, LANES:], 2 * LANES)


def gate_up(where, placed, gu_weight, chunk, group, after):
    _, units, _, width = gu_weight.shape
    n_blocks = len(placed)
    lanes = 2 * n_blocks * CAP
    half = jax.ShapeDtypeStruct((2, units // 2, group // 2 * lanes), BF16)
    pair = pl.BlockSpec((2, units // 2, lanes), lambda i: (0, 0, i // 2))
    return pl.pallas_call(
        functools.partial(gate_up_kernel, n_blocks),
        grid=(group,),
        out_shape=(half, half),
        in_specs=[pl.BlockSpec(memory_space=pltpu.SMEM)]
        + [pl.BlockSpec((1, CAP, width), lambda i: (chunk * group + i, 0, 0))] * n_blocks
        + [pl.BlockSpec((1, units, 2, width), lambda i: (chunk * group + i, 0, 0, 0))]
        + [pl.BlockSpec(memory_space=pl.ANY)],
        out_specs=(pair, pair),
        scratch_shapes=[
            pltpu.VMEM((2, 2 * LANES, width), BF16),
            pltpu.VMEM((2 * units, LANES), F32),
        ],
        compiler_params=params(28),
        cost_estimate=QUICK,
        name="gate_up",
    )(where, *placed, gu_weight, after)


def hidden_kernel(keep_ref, near_ref, far_ref, _, out_ref, sums):
    units = out_ref.shape[1]
    for n in range(sums.shape[0]):
        lanes = slice(n * LANES, (n + 1) * LANES)
        total = keep_ref[0, :, lanes].astype(F32) + near_ref[0, :, lanes].astype(F32)
        sums[n] = total + far_ref[:, lanes].astype(F32)
        gate = sums[n, pl.ds(0, units, stride=2), :]
        up = sums[n, pl.ds(1, units, stride=2), :]
        out_ref[lanes, :] = (gate / (1.0 + jnp.exp(-gate)) * up).T.astype(BF16)


def hidden_quarter(keep, near, far, after):
    _, doubled, columns = keep.shape
    mine = pl.BlockSpec((1, doubled, columns), lambda i: (1, 0, 0))
    return pl.pallas_call(
        hidden_kernel,
        grid=(1,),
        out_shape=jax.ShapeDtypeStruct((columns, doubled // 2), BF16),
        in_specs=[
            mine,
            mine,
            pl.BlockSpec((doubled, columns), lambda i: (0, 0)),
            pl.BlockSpec(memory_space=pl.ANY),
        ],
        out_specs=pl.BlockSpec((columns, doubled // 2), lambda i: (0, 0)),
        scratch_shapes=[pltpu.VMEM((columns // LANES, doubled, LANES), F32)],
        compiler_params=params(10),
        cost_estimate=SLOW,
        name="hidden",
    )(keep, near, far, after)


def add_kernel(keep_ref, near_ref, _, out_ref):
    out_ref[...] = (keep_ref[0].astype(F32) + near_ref[0].astype(F32)).astype(BF16)


def chip_sum(keep, near, after):
    _, doubled, columns = keep.shape
    other = pl.BlockSpec((1, doubled, columns), lambda i: (0, 0, 0))
    return pl.pallas_call(
        add_kernel,
        grid=(1,),
        out_shape=jax.ShapeDtypeStruct((doubled, columns), BF16),
        in_specs=[other, other, pl.BlockSpec(memory_space=pl.ANY)],
        out_specs=pl.BlockSpec((doubled, columns), lambda i: (0, 0)),
        compiler_params=params(8),
        cost_estimate=QUICK,
        name="chip_sum",
    )(keep, near, after)


def down_kernel(group, n_blocks, chunk, has_carry, where_ref, *refs):
    hidden_refs, refs = refs[:4], refs[4:]
    route_refs, refs = refs[:n_blocks], refs[n_blocks:]
    w_hbm, refs = refs[0], refs[2:]
    carry_ref, refs = (refs[0], refs[1:]) if has_carry else (None, refs)
    out_refs, (held, w_buf, sems) = refs[:-3], refs[-3:]
    rows = n_blocks * CAP
    quarter = w_hbm.shape[1] // 4
    count = route_refs[0].shape[1]
    local = w_hbm.shape[0]
    x, core = where_ref[1], where_ref[2]
    order = [(x, core), (1 - x, core), (x, 1 - core), (1 - x, 1 - core)]

    def fetch(e):
        copies = []
        for j in range(4):
            f0 = pl.multiple_of((order[j][0] * 2 + order[j][1]) * quarter, quarter)
            copies.append(
                pltpu.make_async_copy(
                    w_hbm.at[chunk * group + e, pl.ds(f0, quarter)],
                    w_buf.at[e, pl.ds(j * quarter, quarter)],
                    sems.at[e, j],
                )
            )
        return copies

    def start(e):
        for copy in fetch(e):
            copy.start()

    start(0)
    start(1)
    for e in range(group):
        for copy in fetch(e):
            copy.wait()
        if e + 2 < group:
            start(e + 2)
        units = jnp.concatenate([h[e * rows : (e + 1) * rows, :] for h in hidden_refs], axis=1)
        out = lax.dot_general(units, w_buf[e], NN, preferred_element_type=F32).astype(BF16)
        for i in range(n_blocks):
            held[i, e * CAP : (e + 1) * CAP, :] = out[i * CAP : (i + 1) * CAP]
    slot_of = lax.broadcasted_iota(jnp.int32, (CAP, count), 0).astype(F32)
    for i in range(n_blocks):
        table = [
            jnp.where(
                route_refs[i][chunk * group + e : chunk * group + e + 1, :] == slot_of,
                route_refs[i][local + chunk * group + e : local + chunk * group + e + 1, :],
                0.0,
            )
            for e in range(group)
        ]
        table = jnp.concatenate(table, axis=0).astype(BF16)
        total = lax.dot_general(table, held[i], TN, preferred_element_type=F32)
        if has_carry:
            out_refs[i][...] = (total + carry_ref[i]).astype(BF16)
        else:
            out_refs[0][i] = total


def down(where, hidden, routes, down_weight, chunk, group, carry, after):
    n_blocks = len(routes)
    units = hidden[0].shape[1]
    count = routes[0].shape[1]
    width = down_weight.shape[2]
    whole = pl.BlockSpec(memory_space=pltpu.VMEM)
    carried = [] if carry is None else [carry]
    if carry is None:
        out_shape = (jax.ShapeDtypeStruct((n_blocks, count, width), F32),)
    else:
        out_shape = tuple(jax.ShapeDtypeStruct((count, width), BF16) for _ in routes)
    return pl.pallas_call(
        functools.partial(down_kernel, group, n_blocks, chunk, carry is not None),
        out_shape=out_shape,
        in_specs=[pl.BlockSpec(memory_space=pltpu.SMEM)]
        + [whole] * (4 + n_blocks)
        + [pl.BlockSpec(memory_space=pl.ANY)] * 2
        + [whole] * len(carried),
        out_specs=tuple(whole for _ in out_shape),
        scratch_shapes=[
            pltpu.VMEM((n_blocks, group * CAP, width), BF16),
            pltpu.VMEM((group, 4 * units, width), BF16),
            pltpu.SemaphoreType.DMA((group, 4)),
        ],
        compiler_params=params(28),
        cost_estimate=QUICK,
        name="down",
    )(where, *hidden, *routes, down_weight, after, *carried)


def local_square(tokens, expert_ids, gate_weights, gu_weight, down_weight):
    z, t = lax.axis_index("ep"), lax.axis_index("tp")
    x, core = t // 2, t % 2
    local = gu_weight.shape[0]
    group = local // 2
    where = jnp.stack([z * local, x, core]).astype(jnp.int32)

    def hop(array, pairs):
        return lax.ppermute(array, "ep", pairs)

    message = pack(tokens, expert_ids, gate_weights)
    neighbour = hop(message, PAIR)
    middle_1 = hop(message, MIDDLE)
    middle_2 = hop(neighbour, MIDDLE)
    end_1 = hop(middle_1, OUTWARD)
    end_2 = hop(middle_2, OUTWARD)
    blocks = [(message,), (neighbour,), (middle_1, end_1), (middle_2, end_2)]
    placed, tables = zip(*(place(where, b, local) for b in blocks))

    def sums(n, after):
        send, keep = gate_up(where, placed, gu_weight, n, group, after)
        return keep, lax.ppermute(send, "tp", ACROSS_CORE)

    def across(keep, near, after):
        total = chip_sum(keep, near, after)
        return total, lax.ppermute(total, "tp", ACROSS_X)

    def gathered(own):
        own_x = lax.ppermute(own, "tp", ACROSS_X)
        own_core = lax.ppermute(own, "tp", ACROSS_CORE)
        return own, own_x, own_core, lax.ppermute(own_x, "tp", ACROSS_CORE)

    keep_0, near_0 = sums(0, placed[3])
    turn, far_0 = across(keep_0, near_0, keep_0)
    keep_1, near_1 = sums(1, turn)
    own_0 = hidden_quarter(keep_0, near_0, far_0, keep_1)
    hidden_0 = gathered(own_0)
    turn, far_1 = across(keep_1, near_1, own_0)
    (carry,) = down(where, hidden_0, tables, down_weight, 0, group, None, turn)
    own_1 = hidden_quarter(keep_1, near_1, far_1, carry)
    hidden_1 = gathered(own_1)
    own, other, far_in, far_out = down(
        where, hidden_1, tables, down_weight, 1, group, carry, own_1
    )

    def plus(a, b):
        return (a.astype(F32) + b.astype(F32)).astype(BF16)

    out_inner = hop(far_out, INWARD)
    in_inner = hop(far_in, INWARD)
    out_mid = hop(plus(far_out, out_inner), MIDDLE)
    last = hop(plus(other, out_mid), PAIR)
    in_mid = hop(plus(far_in, in_inner), MIDDLE)
    return (own.astype(F32) + in_mid.astype(F32) + last.astype(F32)).astype(BF16)


def local_general(tokens, expert_ids, gate_weights, gu_weight, down_weight):
    tok_rows, local_width = tokens.shape
    table = route(expert_ids, gate_weights)
    slots = jnp.arange(CAP, dtype=jnp.int32).astype(F32)
    matches = table[:EXPERTS, None, :] == slots[None, :, None]
    dispatch_table = matches.astype(BF16).reshape(EXPERTS * CAP, tok_rows)
    outgoing = jnp.dot(dispatch_table, tokens, preferred_element_type=F32)
    outgoing = outgoing.astype(BF16).reshape(EXPERTS, CAP, local_width)
    received = lax.all_to_all(outgoing, "ep", split_axis=0, concat_axis=1, tiled=True)
    terms = jnp.einsum("efgd,esd->fegs", gu_weight, received, preferred_element_type=F32)
    totals = lax.psum(terms.astype(BF16), "tp").astype(F32)
    hidden = (jax.nn.silu(totals[:, :, 0]) * totals[:, :, 1]).astype(BF16)
    expert_out = jnp.einsum("fes,efd->esd", hidden, down_weight, preferred_element_type=F32)
    returned = lax.all_to_all(
        expert_out.astype(BF16), "ep", split_axis=1, concat_axis=0, tiled=True
    )
    combine_table = jnp.where(matches, table[EXPERTS:, None, :], 0.0).astype(BF16)
    mixed = lax.dot_general(
        combine_table.reshape(EXPERTS * CAP, tok_rows),
        returned.reshape(EXPERTS * CAP, local_width),
        TN,
        preferred_element_type=F32,
    )
    return mixed.astype(BF16)


def solution(mesh):
    placed = (
        P(("grp", "ep"), "tp"),
        P(("grp", "ep"), None),
        P(("grp", "ep"), None),
        P("ep", None, None, "tp"),
        P("ep", None, "tp"),
    )
    square = mesh.shape["ep"] == 4 and mesh.shape["tp"] == 4
    return jax.shard_map(
        local_square if square else local_general,
        mesh=mesh,
        in_specs=placed,
        out_specs=P(("grp", "ep"), "tp"),
        check_vma=False,
    )
```
